32 devices in a mesh: seq: 8 (over y, x, core), head: 4 (over z).
Axes of the slice: x: 2, y: 2, z: 4, core: 2. Of those that a mesh axis runs over, the one named last changes fastest.
Arguments:
- block_input: bfloat16 [32768, 768], P(('seq', 'head')), may hold values from -6 to 6
- out_cotangent: bfloat16 [32768, 768], P(('seq', 'head')), may hold values from -6 to 6
- segment_ids: int32 [32768], replicated, may hold values from 0 to 4, as said below
- in_weight: float32 [768, 3352], P(('seq', 'head')), may hold values from -0.21875 to 0.21875
- out_weight: float32 [1536, 768], P(('seq', 'head')), may hold values from -0.15625 to 0.15625
- vector_params: float32 [11336], replicated, may hold values from -13 to 2
- in_first: float32 [768, 3352], P(('seq', 'head')), may hold values from -54.3058 to 54.3058
- in_second: float32 [768, 3352], P(('seq', 'head')), may hold values from 294.912 to 2162.688
- out_first: float32 [1536, 768], P(('seq', 'head')), may hold values from -108.6116 to 108.6116
- out_second: float32 [1536, 768], P(('seq', 'head')), may hold values from 1212.416 to 8519.68
- vector_first: float32 [11336], replicated, may hold values from -54.3058 to 54.3058
- vector_second: float32 [11336], replicated, may hold values from 294.912 to 2162.688
Outputs:
- block_output: bfloat16 [32768, 768], P(('seq', 'head'))
- input_grad: bfloat16 [32768, 768], P(('seq', 'head'))
- in_first_new: float32 [768, 3352], P(('seq', 'head'))
- in_second_new: float32 [768, 3352], P(('seq', 'head'))
- in_weight_new: float32 [768, 3352], P(('seq', 'head'))
- out_first_new: float32 [1536, 768], P(('seq', 'head'))
- out_second_new: float32 [1536, 768], P(('seq', 'head'))
- out_weight_new: float32 [1536, 768], P(('seq', 'head'))
- vector_first_new: float32 [11336], replicated
- vector_second_new: float32 [11336], replicated
- vector_new: float32 [11336], replicated
The draws below stay inside these ranges and needn't reach their ends.
Inputs may be any that keep to these rules, and one draw needn't show every extreme that they name: `segment_ids`: never falls along the tokens; starts at 0 and ends at 4; one document begins within the first 4096 tokens and ends within the last 4096.
All inputs are finite; a program needn't handle non-finite values.
Results may differ from the reference program's by a relative error of at most 0.011.
Values may be sent and summed in bfloat16 or wider, within the bound.
No kernel may reach another device: no remote copies, remote signals or barrier semaphores. Data moves between devices by JAX's collectives and lax.ppermute only.
A program may use at most 256 MiB of HBM per device.

```python
import math
import jax
import jax.numpy as jnp
from jax import lax

WIDTH = 768
INNER = 1536
HEADS = 24
HEAD_SIZE = 64
STATE = 128
CONV_WIDTH = 4
STRETCH = 256
STEP = 10
DEVICE_TOKENS = 1024
TOKENS = 32768
CONV_CHANNELS = 1792
PROJECTED = 3352
VECTOR_SIZE = 11336
N_HEAD = 4


def draw_segment_ids(key, part):
    key = jax.random.fold_in(key, 11)
    keys = jax.random.split(key, 4)
    group = DEVICE_TOKENS * N_HEAD
    first = jax.random.randint(keys[0], (), 2, group)
    final = jax.random.randint(keys[1], (), TOKENS - group + 1, TOKENS - 1)
    early = jax.random.randint(keys[2], (), 1, first)
    later = jax.random.randint(keys[3], (), final + 1, TOKENS)
    places = jnp.arange(TOKENS, dtype=jnp.int32)
    counted = (places >= early).astype(jnp.int32) + (places >= first).astype(jnp.int32)
    counted = counted + (places >= final).astype(jnp.int32) + (places >= later).astype(jnp.int32)
    return counted.astype(jnp.int32)


def draw_vector_params(key, part):
    key = jax.random.fold_in(key, 5)
    keys = jax.random.split(key, 9)
    gains = 1.0 + 0.15 * jax.random.truncated_normal(keys[0], -2.0, 2.0, (WIDTH + INNER,), jnp.float32)
    conv_taps = 0.5 * jax.random.truncated_normal(keys[1], -3.0, 3.0, (CONV_WIDTH * CONV_CHANNELS,), jnp.float32)
    slow_share = 0.5
    conv_bias = 0.2 * jax.random.truncated_normal(keys[2], -3.0, 3.0, (CONV_CHANNELS,), jnp.float32)
    slower = jax.random.uniform(keys[3], (HEADS,), jnp.float32) < slow_share
    slow_scale = jnp.exp(jax.random.uniform(keys[4], (HEADS,), jnp.float32, math.log(3.0), math.log(30.0)))
    slow_keep = jnp.exp(jax.random.uniform(keys[5], (HEADS,), jnp.float32, math.log(0.3), math.log(2.0)))
    fast_bias = jax.random.uniform(keys[6], (HEADS,), jnp.float32, -3.0, -1.0)
    fast_span = jax.random.uniform(keys[7], (HEADS,), jnp.float32, 20.0, 60.0)
    step_bias = jnp.where(slower, jnp.log(slow_scale / TOKENS) - 0.5, fast_bias)
    log_rate = jnp.where(slower, jnp.log(slow_keep) - jnp.log(slow_scale), -fast_bias - 0.5 - jnp.log(fast_span))
    skip_gain = jax.random.uniform(keys[8], (HEADS,), jnp.float32, 0.5, 1.5)
    return jnp.concatenate([gains, conv_taps, conv_bias, step_bias, log_rate, skip_gain]).astype(jnp.float32)


def block_scale(key, dims, cuts, least, largest):
    loudness = 1.0
    for dim, parts in cuts:
        steps = jax.random.uniform(jax.random.fold_in(jax.random.fold_in(key, 6), dim), (parts,), jnp.float32, least / len(cuts), largest / len(cuts))
        loudness = loudness * jnp.repeat(jnp.exp(steps), dims[dim] // parts).reshape((-1,) + (1,) * (len(dims) - 1 - dim))
    return loudness


def noise(own_key, dims, scale, most, cuts=(), held_as=jnp.bfloat16):
    values = jax.random.normal(own_key, dims, jnp.float32) * scale
    if len(cuts) > 0:
        values = block_scale(own_key, dims, cuts, -0.22, 0.18) * values
    return jnp.clip(values, min=-most, max=most).astype(held_as)


def setup_inputs(seed: int = 0) -> dict:
    key_of = jax.random.split(jax.random.key(seed), 13)
    return {
        "block_input": noise(key_of[0], (TOKENS, WIDTH), 1.0, 6.0, ((0, 32),)),
        "out_cotangent": noise(key_of[1], (TOKENS, WIDTH), 1.0, 6.0, ((0, 32),)),
        "segment_ids": draw_segment_ids(jax.random.fold_in(key_of[12], 71), 0),
        "in_weight": noise(key_of[3], (WIDTH, PROJECTED), WIDTH ** -0.5, 0.21875, ((0, 32),), jnp.float32),
        "out_weight": noise(key_of[4], (INNER, WIDTH), INNER ** -0.5, 0.15625, ((0, 32),), jnp.float32),
        "vector_params": draw_vector_params(jax.random.fold_in(key_of[12], 71), 0),
        "in_first": noise(key_of[6], (WIDTH, PROJECTED), (0.055 * TOKENS ** 0.5), 54.3058, ((0, 32),), jnp.float32),
        "in_second": jnp.clip(jnp.exp(math.log(2162.688) - 1.9924302 * jax.random.uniform(key_of[7], (WIDTH, PROJECTED), jnp.float32) ** block_scale(key_of[7], (WIDTH, PROJECTED), ((0, 32),), -0.2, 0.2)), 294.912, 2162.688),
        "out_first": noise(key_of[8], (INNER, WIDTH), (0.11 * TOKENS ** 0.5), 108.6116, ((0, 32),), jnp.float32),
        "out_second": jnp.clip(jnp.exp(math.log(8519.68) - 1.9497637 * jax.random.uniform(key_of[9], (INNER, WIDTH), jnp.float32) ** block_scale(key_of[9], (INNER, WIDTH), ((0, 32),), -0.2, 0.2)), 1212.416, 8519.68),
        "vector_first": noise(key_of[10], (VECTOR_SIZE,), (0.055 * TOKENS ** 0.5), 54.3058, (), jnp.float32),
        "vector_second": jnp.clip(jnp.exp(jax.random.uniform(key_of[11], (VECTOR_SIZE,), jnp.float32, math.log(294.912), math.log(2162.688))), 294.912, 2162.688),
    }


EPS = 1e-05
BETA_ONE = 0.9
BETA_TWO = 0.95
ADAM_EPS = 1e-08
WEIGHT_DECAY = 0.1
RATE_MATRIX = 0.05
RATE_VECTOR = 0.3
HIGHEST = lax.Precision.HIGHEST

@jax.custom_vjp
def low(v):
    return lax.optimization_barrier(v.astype(jnp.bfloat16)).astype(jnp.float32)

@jax.custom_vjp
def low_back(v):
    return v

def low_keep(v):
    return (low(v), None)

def low_pass(kept, grad):
    return (grad,)

def back_keep(v):
    return (v, None)

def back_low(kept, grad):
    return (low(grad),)
low.defvjp(low_keep, low_pass)
low_back.defvjp(back_keep, back_low)

def split_vector(vector):
    cursor = 0
    pieces = []
    for length in (WIDTH, INNER, CONV_WIDTH * CONV_CHANNELS, CONV_CHANNELS, HEADS, HEADS, HEADS):
        pieces.append(vector[cursor:cursor + length])
        cursor = cursor + length
    norm_gain, gated_gain, conv_flat, conv_bias, step_bias, log_rate, skip_gain = pieces
    return (norm_gain, gated_gain, conv_flat.reshape(CONV_WIDTH, CONV_CHANNELS), conv_bias, step_bias, log_rate, skip_gain)

def stretch_step(state, pieces):
    values, writes, reads, delta, decay, segments, before = pieces
    cumul = jnp.cumsum(decay, axis=0)
    causal = jnp.tril(jnp.ones((STRETCH, STRETCH), dtype=jnp.bool_))
    inside = (causal & (segments[:, None] == segments[None, :]))[:, :, None]
    spread = cumul[:, None, :] - cumul[None, :, :]
    lower = jnp.where(inside, jnp.exp(jnp.where(inside, spread, 0.0)), 0.0)
    scores = low_back(jnp.einsum('in,jn->ij', reads, writes, precision=HIGHEST))
    weights = low_back(low(scores[:, :, None] * lower * delta[None, :, :]))
    diagonal = jnp.einsum('ijh,jhp->ihp', weights, values, precision=HIGHEST)
    enter = jnp.exp(cumul) * (segments == before).astype(jnp.float32)[:, None]
    entry = jnp.einsum('in,hpn->ihp', reads, state, precision=HIGHEST)
    end_weight = jnp.exp(cumul[-1:] - cumul) * (segments == segments[-1]).astype(jnp.float32)[:, None] * delta
    carry = jnp.exp(cumul[-1]) * (segments[-1] == before).astype(jnp.float32)
    fresh = jnp.einsum('jhp,jn->hpn', values * end_weight[:, :, None], writes, precision=HIGHEST)
    return (carry[:, None, None] * state + fresh, diagonal + entry * enter[:, :, None])

def forward(inputs, in_weight, out_weight, vector, segment_ids):
    norm_gain, gated_gain, conv_taps, conv_bias, step_bias, log_rate, skip_gain = split_vector(vector)
    in_scale = lax.rsqrt(lax.optimization_barrier(jnp.mean(inputs * inputs, axis=-1, keepdims=True)) + EPS)
    normed = low(inputs * in_scale * norm_gain)
    projected = jnp.dot(normed, low(in_weight), precision=HIGHEST)
    gate = low_back(projected[:, :INNER])
    mixed_in = low_back(low(projected[:, INNER:INNER + CONV_CHANNELS]))
    delta_raw = low_back(low(projected[:, INNER + CONV_CHANNELS:]))
    padded = jnp.concatenate([jnp.zeros((CONV_WIDTH - 1, CONV_CHANNELS), jnp.float32), mixed_in], axis=0)
    seg_padded = jnp.concatenate([jnp.full((CONV_WIDTH - 1,), -1, jnp.int32), segment_ids.astype(jnp.int32)])
    conv_sum = jnp.broadcast_to(conv_bias, (TOKENS, CONV_CHANNELS))
    for offset in range(CONV_WIDTH):
        same = (seg_padded[offset:offset + TOKENS] == segment_ids).astype(jnp.float32)
        conv_sum = conv_sum + conv_taps[offset] * padded[offset:offset + TOKENS] * same[:, None]
    convolved = jax.nn.silu(conv_sum)
    values = low(convolved[:, :INNER]).reshape(TOKENS, HEADS, HEAD_SIZE)
    writes = low(convolved[:, INNER:INNER + STATE])
    reads = low(convolved[:, INNER + STATE:])
    delta = jax.nn.softplus(delta_raw + step_bias)
    decay = delta * -jnp.exp(log_rate)
    blocks = TOKENS // STRETCH
    befores = seg_padded[CONV_WIDTH - 2:CONV_WIDTH - 2 + TOKENS].reshape(blocks, STRETCH)[:, 0]
    pieces = (values.reshape(blocks, STRETCH, HEADS, HEAD_SIZE), writes.reshape(blocks, STRETCH, STATE), reads.reshape(blocks, STRETCH, STATE), delta.reshape(blocks, STRETCH, HEADS), decay.reshape(blocks, STRETCH, HEADS), segment_ids.reshape(blocks, STRETCH), befores)
    start = jnp.zeros((HEADS, HEAD_SIZE, STATE), jnp.float32)
    final_state, stretch_out = lax.scan(jax.checkpoint(stretch_step), start, pieces)
    outputs = stretch_out.reshape(TOKENS, HEADS, HEAD_SIZE) + skip_gain[:, None] * values
    mixed = low_back(low(outputs.reshape(TOKENS, INNER)))
    gated = mixed * jax.nn.silu(gate)
    gated_scale = lax.rsqrt(lax.optimization_barrier(jnp.mean(gated * gated, axis=-1, keepdims=True)) + EPS)
    gated_normed = low(gated * gated_scale * gated_gain)
    return inputs + jnp.dot(gated_normed, low(out_weight), precision=HIGHEST)

def adamw(weight, first, second, grad, rate, decay):
    first_new = BETA_ONE * first + (1.0 - BETA_ONE) * grad
    second_new = BETA_TWO * second + (1.0 - BETA_TWO) * grad * grad
    corrected_first = first_new / (1.0 - BETA_ONE ** STEP)
    corrected_second = second_new / (1.0 - BETA_TWO ** STEP)
    weight_new = weight - rate * (corrected_first / (jnp.sqrt(corrected_second) + ADAM_EPS) + decay * weight)
    return (first_new, second_new, weight_new)

def reference(block_input, out_cotangent, segment_ids, in_weight, out_weight, vector_params, in_first, in_second, out_first, out_second, vector_first, vector_second):
    inputs = block_input.astype(jnp.float32)

    def closed(inputs_now, in_now, out_now, vector_now):
        return forward(inputs_now, in_now, out_now, vector_now, segment_ids)
    result, pullback = jax.vjp(closed, inputs, in_weight, out_weight, vector_params)
    input_grad, in_grad, out_grad, vector_grad = pullback(out_cotangent.astype(jnp.float32))
    in_first_new, in_second_new, in_weight_new = adamw(in_weight, in_first, in_second, in_grad, RATE_MATRIX, WEIGHT_DECAY)
    out_first_new, out_second_new, out_weight_new = adamw(out_weight, out_first, out_second, out_grad, RATE_MATRIX, WEIGHT_DECAY)
    vector_first_new, vector_second_new, vector_new = adamw(vector_params, vector_first, vector_second, vector_grad, RATE_VECTOR, 0.0)
    return (result.astype(jnp.bfloat16), input_grad.astype(jnp.bfloat16), in_first_new, in_second_new, in_weight_new, out_first_new, out_second_new, out_weight_new, vector_first_new, vector_second_new, vector_new)
```

```python
import functools

import jax
import jax.numpy as jnp
from jax import lax
from jax.experimental import pallas as pl
from jax.experimental.pallas import tpu as pltpu
from jax.sharding import PartitionSpec as P

WIDTH = 768
INNER = 1536
HEADS = 24
HEAD_SIZE = 64
STATE = 128
CONV_WIDTH = 4
STRETCH = 256
STEP = 10
CONV_CHANNELS = 1792
LANES = 128
PAIRS = HEADS // 2
MIXED = CONV_CHANNELS + LANES
HALO = 16
CHUNK = 16
HALF = STRETCH // 2
TILE = 256

EPS = 1e-05
BETA_ONE = 0.9
BETA_TWO = 0.95
ADAM_EPS = 1e-08
WEIGHT_DECAY = 0.1
RATE_MATRIX = 0.05
RATE_VECTOR = 0.3
HIGHEST = lax.Precision.HIGHEST
f32 = jnp.float32
bf16 = jnp.bfloat16
EVERY = ("seq", "head")
VMEM = 56 * 1024 * 1024


def passed_along(value, axis, steps):
    count = lax.axis_size(axis)
    leading, last = (max(0, -steps), min(count, count - steps))
    return lax.ppermute(value, axis, [(source, source + steps) for source in range(leading, last)])


def split_vector(vector):
    cursor = 0
    pieces = []
    for length in (WIDTH, INNER, CONV_WIDTH * CONV_CHANNELS, CONV_CHANNELS, HEADS, HEADS, HEADS):
        pieces.append(vector[cursor : cursor + length])
        cursor = cursor + length
    norm_gain, gated_gain, conv_flat, conv_bias, step_bias, log_rate, skip_gain = pieces
    return (
        norm_gain,
        gated_gain,
        conv_flat.reshape(CONV_WIDTH, CONV_CHANNELS),
        conv_bias,
        step_bias,
        log_rate,
        skip_gain,
    )


def adamw(weight, first, second, grad, rate, decay):
    first_new = BETA_ONE * first + (1.0 - BETA_ONE) * grad
    second_new = BETA_TWO * second + (1.0 - BETA_TWO) * grad * grad
    corrected_first = first_new / (1.0 - BETA_ONE**STEP)
    corrected_second = second_new / (1.0 - BETA_TWO**STEP)
    weight_new = weight - rate * (
        corrected_first / (jnp.sqrt(corrected_second) + ADAM_EPS) + decay * weight
    )
    return (first_new, second_new, weight_new)


def mm(left, right, dims=((1,), (0,)), precision=None):
    return lax.dot_general(left, right, (dims, ((), ())), preferred_element_type=f32, precision=precision)


NT = ((1,), (1,))
TN = ((0,), (0,))


def spec(block, index):
    return pl.BlockSpec(block, index)


def whole(*shape):
    return pl.BlockSpec(shape, lambda *ids: (0,) * len(shape))


def call(body, grid, ins, outs, out_shapes, scratch, cost):
    return pl.pallas_call(
        body,
        grid=grid,
        in_specs=ins,
        out_specs=outs,
        out_shape=[jax.ShapeDtypeStruct(shape, kind) for shape, kind in out_shapes],
        scratch_shapes=scratch,
        compiler_params=pltpu.CompilerParams(vmem_limit_bytes=VMEM),
        cost_estimate=pl.CostEstimate(flops=int(cost[0]), bytes_accessed=int(cost[1]), transcendentals=0),
    )


def spread_heads(per_head):
    rows = per_head.shape[0]
    low = lax.broadcasted_iota(jnp.int32, (rows, LANES), 1) < HEAD_SIZE
    tiles = []
    for j in range(PAIRS):
        one = jnp.broadcast_to(per_head[:, 2 * j : 2 * j + 1], (rows, LANES))
        two = jnp.broadcast_to(per_head[:, 2 * j + 1 : 2 * j + 2], (rows, LANES))
        tiles.append(jnp.where(low, one, two))
    return jnp.concatenate(tiles, axis=1)


def chunks(count, size, body):
    def step(i, _):
        body(pl.ds(pl.multiple_of(i * size, size), size))
        return 0

    lax.fori_loop(0, count // size, step, 0)


def sigmoid(v):
    return 1.0 / (1.0 + jnp.exp(-v))


def softplus(v):
    small = jnp.exp(-jnp.abs(v))
    series = small * (1.0 - small * (0.5 - small * (1.0 / 3.0 - small * 0.25)))
    return jnp.maximum(v, 0.0) + jnp.where(small < 0.01, series, jnp.log(1.0 + small))


def conv_rows(held, masks, taps, rows):
    total = taps[CONV_WIDTH : CONV_WIDTH + 1, :] + taps[3:4, :] * held[pl.ds(HALO + rows, STRETCH), :]
    for k in range(1, CONV_WIDTH):
        shifted = held[pl.ds(HALO + rows - k, STRETCH), :]
        total = total + taps[3 - k : 4 - k, :] * (shifted * masks[rows : rows + STRETCH, k - 1 : k])
    return total


def conv_forward(normed, weight, masks, taps, out, mixed, held):
    low = mm(normed[...], weight[...]).astype(bf16)
    mixed[...] = low
    held[...] = low.astype(f32)
    for rows in range(0, out.shape[0], STRETCH):
        total = conv_rows(held, masks, taps[...], rows)
        out[rows : rows + STRETCH, :] = (total * sigmoid(total)).astype(bf16)


def local_states(
    values, both, raw, masks, bias, rate,
    scaled, cumul_out, delta_out, cumul_rows, start, factors, device_state, device_decay,
    state, reach, weighted,
):
    c = pl.program_id(0)

    @pl.when(c == 0)
    def _():
        state[...] = jnp.zeros_like(state)
        reach[...] = jnp.ones_like(reach)

    delta = softplus(raw[...].astype(f32) + bias[...])
    row = lax.broadcasted_iota(jnp.int32, (STRETCH, STRETCH), 0)
    col = lax.broadcasted_iota(jnp.int32, (STRETCH, STRETCH), 1)
    cumul = mm((row >= col).astype(f32), delta * rate[...], precision=HIGHEST)
    last = cumul[STRETCH - 1 : STRETCH, :]
    end_weight = jnp.exp(last - cumul) * masks[:, 3:4] * delta
    carry = jnp.exp(last) * masks[STRETCH - 1 : STRETCH, 4:5]
    cumul_out[...] = cumul
    delta_out[...] = delta
    cumul_rows[0] = cumul.T[: cumul_rows.shape[1], :]
    low = lax.broadcasted_iota(jnp.int32, (STRETCH, LANES), 1) < HEAD_SIZE
    for j in range(PAIRS):
        cols = slice(j * LANES, (j + 1) * LANES)
        v = values[:, cols].astype(f32)
        ahead = [jnp.broadcast_to(delta[:, h : h + 1], (STRETCH, LANES)) for h in (2 * j, 2 * j + 1)]
        scaled[:, cols] = (v * jnp.where(low, *ahead)).astype(bf16)
        ahead = [jnp.broadcast_to(end_weight[:, h : h + 1], (STRETCH, LANES)) for h in (2 * j, 2 * j + 1)]
        weighted[:, cols] = (v * jnp.where(low, *ahead)).astype(bf16)
    local = mm(both[:, :STATE], weighted[...], TN)
    carry_wide = spread_heads(carry)
    start[0] = state[...]
    factors[0] = jnp.concatenate(
        [carry_wide, spread_heads(reach[0:1, :]), jnp.zeros((6, INNER), f32)], axis=0
    )
    state[...] = state[...] * carry_wide + local
    reach[...] = reach[...] * carry

    @pl.when(c == pl.num_programs(0) - 1)
    def _():
        for j in range(PAIRS):
            device_state[j] = state[:, j * LANES : (j + 1) * LANES].astype(bf16)
        device_decay[...] = reach[...]


def spread_columns(cumul, columns):
    for h in range(HEADS):
        columns[h] = jnp.broadcast_to(cumul[:, h : h + 1], (STRETCH, LANES))


def diagonal(scaled, both, cumul, cumul_rows, masks, segments, out, columns, scores):
    spread_columns(cumul, columns)
    row = lax.broadcasted_iota(jnp.int32, (STRETCH, STRETCH), 0)
    col = lax.broadcasted_iota(jnp.int32, (STRETCH, STRETCH), 1)
    inside = (row >= col) & (masks[:, 5:6] == segments[0])
    scores[...] = jnp.where(inside, mm(both[:, STATE:], both[:, :STATE], NT), 0.0)
    low = lax.broadcasted_iota(jnp.int32, (HALF, LANES), 1) < HEAD_SIZE

    def pair(j, _):
        cols = pl.ds(pl.multiple_of(j * LANES, LANES), LANES)
        v = scaled[:, cols]
        tops, bottoms = [], []
        for q in range(2):
            h = 2 * j + q
            line = cumul_rows[0, pl.ds(h, 1), :]
            upper = columns[h, :HALF, :]
            lower = columns[h, HALF:, :]
            top = jnp.exp(jnp.minimum(upper - line[:, :HALF], 0.0)) * scores[:HALF, :HALF]
            left = jnp.exp(jnp.minimum(lower - line[:, :HALF], 0.0)) * scores[HALF:, :HALF]
            right = jnp.exp(jnp.minimum(lower - line[:, HALF:], 0.0)) * scores[HALF:, HALF:]
            tops.append(mm(top.astype(bf16), v[:HALF]))
            bottoms.append(mm(jnp.concatenate([left.astype(bf16), right.astype(bf16)], axis=1), v))
        out[:HALF, cols] = jnp.where(low, *tops)
        out[HALF:, cols] = jnp.where(low, *bottoms)
        return 0

    lax.fori_loop(0, PAIRS, pair, 0)


def diagonal_back(
    scaled, both, cumul, cumul_rows, masks, segments, out_grad, sums, both_grad, columns, scores, total
):
    spread_columns(cumul, columns)
    row = lax.broadcasted_iota(jnp.int32, (STRETCH, STRETCH), 0)
    col = lax.broadcasted_iota(jnp.int32, (STRETCH, STRETCH), 1)
    inside = (row <= col) & (masks[:, 5:6] == segments[0])
    scores[...] = jnp.where(inside, mm(both[:, :STATE], both[:, STATE:], NT), 0.0)
    total[...] = jnp.zeros_like(total)
    low = lax.broadcasted_iota(jnp.int32, (HALF, LANES), 1) < HEAD_SIZE
    first = lax.broadcasted_iota(jnp.int32, (STRETCH, LANES), 1) < HEAD_SIZE

    def pair(j, _):
        cols = pl.ds(pl.multiple_of(j * LANES, LANES), LANES)
        v = scaled[:, cols]
        g = out_grad[:, cols]
        tops, bottoms = [], []
        for q in range(2):
            h = 2 * j + q
            line = cumul_rows[0, pl.ds(h, 1), :]
            upper = columns[h, :HALF, :]
            lower = columns[h, HALF:, :]
            own = jnp.where(first == (q == 0), g.astype(f32), 0.0).astype(bf16)
            left = jnp.exp(jnp.minimum(line[:, :HALF] - upper, 0.0))
            right = jnp.exp(jnp.minimum(line[:, HALF:] - upper, 0.0))
            corner = jnp.exp(jnp.minimum(line[:, HALF:] - lower, 0.0))
            tops.append(
                mm(
                    jnp.concatenate(
                        [(left * scores[:HALF, :HALF]).astype(bf16), (right * scores[:HALF, HALF:]).astype(bf16)],
                        axis=1,
                    ),
                    g,
                )
            )
            bottoms.append(mm((corner * scores[HALF:, HALF:]).astype(bf16), g[HALF:]))
            top_grad = mm(v[:HALF], own, NT)
            total[:HALF, :HALF] += left * top_grad[:, :HALF]
            total[:HALF, HALF:] += right * top_grad[:, HALF:]
            total[HALF:, HALF:] += corner * mm(v[HALF:], own[HALF:], NT)
        sums[:HALF, cols] = jnp.where(low, *tops)
        sums[HALF:, cols] = jnp.where(low, *bottoms)
        return 0

    lax.fori_loop(0, PAIRS, pair, 0)
    scores_grad = jnp.where(inside, total[...], 0.0).astype(bf16)
    both_grad[:, :STATE] = mm(scores_grad, both[:, STATE:])
    both_grad[:, STATE:] = mm(scores_grad, both[:, :STATE], TN)


def prefix(parts, decays, second, out, reverse):
    count = parts.shape[0]
    rows = out.shape[1]

    def step(i, state):
        k = count - 1 - i if reverse else i
        out[pl.ds(k, 1)] = state.astype(bf16)[None]
        two = decays[pl.ds(k, 1)][0]
        decay = jnp.where(second[...] > 0.0, two[1:2, :], two[0:1, :])
        return decay * state + parts[pl.ds(k, 1), :rows, :][0].astype(f32)

    lax.fori_loop(0, count, step, jnp.zeros((rows, LANES), f32))


def head_sums(high, low, heads):
    return mm(high[...], heads[...]) + mm(low[...], heads[...])


def put_split(value, high, low, rows):
    top = value.astype(bf16)
    high[rows, :] = top
    low[rows, :] = (value - top.astype(f32)).astype(bf16)


def middle(
    diag, values, both, cumul, masks, start, factors, prior, gate, inputs, cotangent, weight, gain, skip, heads,
    block_output, gated_low, gate_grad, mixed_grad, row_sums, reads_grad, after_local, full_out, sums, start_grad,
    after_decay, entry, normed_grad, enter, entry_low, high, low, state_grad, tail_decay,
):
    i = pl.program_id(0)

    @pl.when(i == 0)
    def _():
        state_grad[...] = jnp.zeros_like(state_grad)
        tail_decay[...] = jnp.ones_like(tail_decay)
        sums[...] = jnp.zeros_like(sums)

    reads = both[:, STATE:]
    for j in range(PAIRS):
        cols = slice(j * LANES, (j + 1) * LANES)
        full_out[0, :, cols] = (
            start[0, :, cols] + factors[0, 1:2, cols] * prior[j].astype(f32)
        ).astype(bf16)
    full = full_out[0]
    entry[...] = mm(reads, full)
    normed_grad[...] = mm(cotangent[...], weight[...], NT)
    enter_coef = jnp.exp(cumul[...]) * masks[:, 4:5]
    first = lax.broadcasted_iota(jnp.int32, (STRETCH, LANES), 1) < HEAD_SIZE
    for j in range(PAIRS):
        two = [jnp.broadcast_to(enter_coef[:, h : h + 1], (STRETCH, LANES)) for h in (2 * j, 2 * j + 1)]
        enter[:, j * LANES : (j + 1) * LANES] = jnp.where(first, *two)

    def rows_step(rows):
        coef = enter[rows, :]
        v = values[rows, :].astype(f32)
        mixed_sum = diag[rows, :] + entry[rows, :] * coef
        mixed = (mixed_sum + skip[...] * v).astype(bf16).astype(f32)
        z = gate[rows, :]
        sig = sigmoid(z)
        act = z * sig
        gated = mixed * act
        scale = lax.rsqrt(jnp.mean(gated * gated, axis=1, keepdims=True) + EPS)
        unit = gated * scale
        gated_low[rows, :] = (unit * gain[...]).astype(bf16)
        back = normed_grad[rows, :]
        scaled = back * gain[...]
        inner = jnp.mean(scaled * unit, axis=1, keepdims=True)
        gated_grad = scale * (scaled - unit * inner)
        gate_grad[rows, :] = (gated_grad * mixed * (sig + act * (1.0 - sig))).astype(bf16)
        low_grad = (gated_grad * act).astype(bf16)
        mixed_grad[rows, :] = low_grad
        grad = low_grad.astype(f32)
        entry_low[rows, :] = (grad * coef).astype(bf16)
        put_split(grad * mixed_sum, high, low, rows)
        sums[0:1, :] += jnp.sum(back * unit, axis=0, keepdims=True)
        sums[1:2, :] += jnp.sum(grad * v, axis=0, keepdims=True)

    chunks(STRETCH, CHUNK, rows_step)
    block_output[...] = (inputs[...].astype(f32) + mm(gated_low[...], weight[...])).astype(bf16)
    row_sums[...] = head_sums(high, low, heads)
    reads_grad[...] = mm(entry_low[...], full, NT)
    after_local[0] = state_grad[...]
    after_decay[0] = jnp.broadcast_to(tail_decay[0:1, :], after_decay.shape[1:])
    state_grad[...] = state_grad[...] * factors[0, 0:1, :] + mm(reads, entry_low[...], TN)
    tail_decay[...] = tail_decay[...] * factors[0, 0:1, :]

    @pl.when(i == pl.num_programs(0) - 1)
    def _():
        for j in range(PAIRS):
            start_grad[j] = state_grad[:, j * LANES : (j + 1) * LANES].astype(bf16)


def late(
    values, both, cumul, delta, raw, masks, bias, rate, factors, full, after_local, after_decay, after,
    diag_sums, scaled, out_grad, row_sums, reads_grad, both_grad, skip, heads,
    conv_grad, raw_grad, sums,
    after_low, spread_grad, factor, wide, weighted, high_a, low_a, high_b, low_b, high_c, low_c,
):
    @pl.when(pl.program_id(0) == 0)
    def _():
        sums[...] = jnp.zeros_like(sums)

    carry_rows = []
    for j in range(PAIRS):
        cols = slice(j * LANES, (j + 1) * LANES)
        here = after_local[0, :, cols] + after_decay[0, 0:1, cols] * after[j].astype(f32)
        after_low[:, cols] = here.astype(bf16)
        carry_rows.append(
            jnp.sum(here * full[0, :, cols].astype(f32), axis=0, keepdims=True) * factors[0, 0:1, cols]
        )
    carry_row = jnp.broadcast_to(jnp.concatenate(carry_rows, axis=1), (8, INNER))
    carry_high = carry_row.astype(bf16)
    carry_low = (carry_row - carry_high.astype(f32)).astype(bf16)
    carry_grad = (mm(carry_high, heads[...]) + mm(carry_low, heads[...]))[0:1, :]
    spread_grad[...] = mm(both[:, :STATE], after_low[...])
    step = delta[...]
    total = cumul[...]
    end_factor = jnp.exp(total[STRETCH - 1 : STRETCH, :] - total) * masks[:, 3:4]
    first = lax.broadcasted_iota(jnp.int32, (STRETCH, LANES), 1) < HEAD_SIZE
    for j in range(PAIRS):
        cols = slice(j * LANES, (j + 1) * LANES)
        two = [jnp.broadcast_to(end_factor[:, h : h + 1], (STRETCH, LANES)) for h in (2 * j, 2 * j + 1)]
        factor[:, cols] = jnp.where(first, *two)
        two = [jnp.broadcast_to(step[:, h : h + 1], (STRETCH, LANES)) for h in (2 * j, 2 * j + 1)]
        wide[:, cols] = jnp.where(first, *two)

    def rows_step(rows):
        v = values[rows, :].astype(f32)
        ends = factor[rows, :]
        step_wide = wide[rows, :]
        inner = diag_sums[rows, :]
        outer = spread_grad[rows, :] * ends
        conv_grad[rows, :INNER] = (
            step_wide * (inner + outer) + skip[...] * out_grad[rows, :].astype(f32)
        ).astype(bf16)
        weighted[rows, :] = (v * ends * step_wide).astype(bf16)
        put_split(v * inner, high_a, low_a, rows)
        put_split(v * outer, high_b, low_b, rows)
        put_split(scaled[rows, :].astype(f32) * inner, high_c, low_c, rows)

    chunks(STRETCH, CHUNK, rows_step)
    conv_grad[:, INNER : INNER + STATE] = (
        both_grad[:, :STATE] + mm(weighted[...], after_low[...], NT)
    ).astype(bf16)
    conv_grad[:, INNER + STATE :] = (both_grad[:, STATE:] + reads_grad[...]).astype(bf16)
    outer_sum = head_sums(high_b, low_b, heads)
    step_grad = head_sums(high_a, low_a, heads) + outer_sum
    end_spread = outer_sum * step
    last_grad = jnp.sum(end_spread, axis=0, keepdims=True) + carry_grad
    cumul_grad = row_sums[...] - head_sums(high_c, low_c, heads) - end_spread
    row = lax.broadcasted_iota(jnp.int32, (STRETCH, STRETCH), 0)
    col = lax.broadcasted_iota(jnp.int32, (STRETCH, STRETCH), 1)
    decay_grad = mm((row <= col).astype(f32), cumul_grad, precision=HIGHEST) + last_grad
    step_grad = step_grad + decay_grad * rate[...]
    pre_grad = step_grad * sigmoid(raw[...].astype(f32) + bias[...])
    raw_grad[...] = pre_grad.astype(bf16)
    sums[0:1, :] += jnp.sum(decay_grad * step, axis=0, keepdims=True)
    sums[1:2, :] += jnp.sum(pre_grad, axis=0, keepdims=True)


def conv_back(mixed, grad, masks, taps, out, rim, tail, tap_grads, held, kept):
    rows_all = grad.shape[0]
    held[...] = mixed[...].astype(f32)
    weights = taps[...]
    kept[pl.ds(rows_all, 8), :] = jnp.zeros((8, TILE), f32)
    taken = [jnp.zeros((1, TILE), f32) for _ in range(CONV_WIDTH + 1)]
    for rows in range(0, rows_all, STRETCH):
        total = conv_rows(held, masks, weights, rows)
        sig = sigmoid(total)
        here = grad[rows : rows + STRETCH, :].astype(f32) * (sig * (1.0 + total * (1.0 - sig)))
        kept[pl.ds(rows, STRETCH), :] = here
        taken[4] = taken[4] + jnp.sum(here, axis=0, keepdims=True)
        taken[3] = taken[3] + jnp.sum(here * held[pl.ds(HALO + rows, STRETCH), :], axis=0, keepdims=True)
        for k in range(1, CONV_WIDTH):
            shifted = held[pl.ds(HALO + rows - k, STRETCH), :] * masks[rows : rows + STRETCH, k - 1 : k]
            taken[3 - k] = taken[3 - k] + jnp.sum(here * shifted, axis=0, keepdims=True)
    tap_grads[...] = jnp.concatenate(taken + [jnp.zeros((3, TILE), f32)], axis=0)
    for rows in range(0, rows_all, STRETCH):
        value = weights[3:4, :] * kept[pl.ds(rows, STRETCH), :]
        for k in range(1, CONV_WIDTH):
            ahead = kept[pl.ds(rows + k, STRETCH), :]
            value = value + weights[3 - k : 4 - k, :] * (ahead * masks[rows : rows + STRETCH, 8 + k - 1 : 8 + k])
        out[rows : rows + STRETCH, :] = value.astype(bf16)
        if rows + STRETCH == rows_all:
            tail[...] = value[STRETCH - HALO :, :]
    top = kept[0:8, :]
    marks = masks[0:8, :]
    lines = []
    for m in range(1, CONV_WIDTH):
        line = jnp.zeros((1, TILE), f32)
        for k in range(m, CONV_WIDTH):
            line = line + weights[3 - k : 4 - k, :] * (top[k - m : k - m + 1, :] * marks[k - m : k - m + 1, k - 1 : k])
        lines.append(line)
    rim[...] = jnp.concatenate([jnp.zeros((5, TILE), f32), lines[2], lines[1], lines[0]], axis=0)


def per_device(
    block_input,
    out_cotangent,
    segment_ids,
    in_weight,
    out_weight,
    vector_params,
    in_first,
    in_second,
    out_first,
    out_second,
    vector_first,
    vector_second,
):
    count = lax.axis_size("seq") * lax.axis_size("head")
    device_index = lax.axis_index(EVERY)
    rows = block_input.shape[0]
    stretches = rows // STRETCH
    own_rows = in_weight.shape[0]
    norm_gain, gated_gain, conv_taps, conv_bias, step_bias, log_rate, skip_gain = split_vector(vector_params)

    mixer_own = jnp.pad(in_weight[:, INNER:].astype(bf16), ((0, 0), (0, LANES - HEADS)))
    mixer_group = lax.all_gather(mixer_own, "head", axis=0, tiled=True)
    mixer_weight = lax.all_gather(mixer_group, "seq", axis=0, tiled=True)
    halo = passed_along(block_input[rows - HALO :], EVERY, 1)
    gate_weight = lax.all_gather(in_weight[:, :INNER].astype(bf16), EVERY, axis=0, tiled=True)
    out_full = lax.all_gather(out_weight.astype(bf16), EVERY, axis=0, tiled=True)

    def unit_rows(block):
        wide = block.astype(f32)
        scale = lax.rsqrt(jnp.mean(wide * wide, axis=-1, keepdims=True) + EPS)
        return wide, scale

    inputs, in_scale = unit_rows(block_input)
    normed = (inputs * in_scale * norm_gain).astype(bf16)
    halo_wide, halo_scale = unit_rows(halo)
    extended = jnp.concatenate([(halo_wide * halo_scale * norm_gain).astype(bf16), normed], axis=0)

    padded = jnp.concatenate(
        [jnp.full((3,), -1, jnp.int32), segment_ids, jnp.full((3,), -1, jnp.int32)]
    )
    window = lax.dynamic_slice_in_dim(padded, device_index * rows, rows + 6)
    own = window[3 : 3 + rows]
    blocks = own.reshape(stretches, STRETCH)
    before = window[2 : 2 + rows].reshape(stretches, STRETCH)[:, :1]
    columns = [(window[3 - k : 3 - k + rows] == own) for k in (1, 2, 3)]
    columns.append((blocks == blocks[:, -1:]).reshape(rows))
    columns.append((blocks == before).reshape(rows))
    columns.append(own)
    columns += [jnp.zeros((rows,), f32)] * 2
    columns += [(window[3 + k : 3 + k + rows] == own) for k in (1, 2, 3)]
    columns += [jnp.zeros((rows,), f32)] * 5
    masks = jnp.stack([column.astype(f32) for column in columns], axis=1)
    marks = masks.shape[1]
    segments = blocks.astype(f32).reshape(stretches, 1, STRETCH)

    taps = jnp.concatenate([conv_taps, conv_bias[None], jnp.zeros((3, CONV_CHANNELS), f32)], axis=0)

    def head_row(vector):
        return jnp.pad(vector, (0, LANES - HEADS)).reshape(1, LANES)

    bias_row = head_row(step_bias)
    rate_row = head_row(-jnp.exp(log_rate))
    skip_row = jnp.repeat(skip_gain, HEAD_SIZE).reshape(1, INNER)
    gain_row = gated_gain.reshape(1, INNER)
    head_of = (
        lax.broadcasted_iota(jnp.int32, (INNER, LANES), 0) // HEAD_SIZE
        == lax.broadcasted_iota(jnp.int32, (INNER, LANES), 1)
    ).astype(bf16)

    convolved, mixed_low = call(
        conv_forward,
        (CONV_CHANNELS // TILE,),
        [
            whole(rows + HALO, WIDTH),
            spec((WIDTH, TILE), lambda i: (0, i)),
            whole(rows, marks),
            spec((8, TILE), lambda i: (0, i)),
        ],
        [spec((rows, TILE), lambda i: (0, i)), spec((rows + HALO, TILE), lambda i: (0, i))],
        [((rows, CONV_CHANNELS), bf16), ((rows + HALO, CONV_CHANNELS), bf16)],
        [pltpu.VMEM((rows + HALO, TILE), f32)],
        (2 * rows * WIDTH * CONV_CHANNELS, 12e6),
    )(extended, mixer_weight, masks, taps)
    raw = jnp.dot(normed, mixer_weight[:, CONV_CHANNELS:], preferred_element_type=f32).astype(bf16)

    by_block = lambda *tail: spec((STRETCH,) + tail, lambda c: (c,) + (0,) * len(tail))
    both_spec = spec((STRETCH, 2 * STATE), lambda c: (c, INNER // (2 * STATE)))
    values_spec = spec((STRETCH, INNER), lambda c: (c, 0))
    per_block = lambda *tail: spec((1,) + tail, lambda c: (c,) + (0,) * len(tail))

    scaled, cumul, delta, cumul_rows, start, factors, device_state, device_decay = call(
        local_states,
        (stretches,),
        [values_spec, both_spec, by_block(LANES), by_block(marks), whole(1, LANES), whole(1, LANES)],
        [
            by_block(INNER),
            by_block(LANES),
            by_block(LANES),
            per_block(32, STRETCH),
            per_block(STATE, INNER),
            per_block(8, INNER),
            whole(PAIRS, STATE, LANES),
            whole(8, LANES),
        ],
        [
            ((rows, INNER), bf16),
            ((rows, LANES), f32),
            ((rows, LANES), f32),
            ((stretches, 32, STRETCH), f32),
            ((stretches, STATE, INNER), f32),
            ((stretches, 8, INNER), f32),
            ((PAIRS, STATE, LANES), bf16),
            ((8, LANES), f32),
        ],
        [pltpu.VMEM((STATE, INNER), f32), pltpu.VMEM((8, LANES), f32), pltpu.VMEM((STRETCH, INNER), bf16)],
        (2 * rows * STATE * INNER, 12e6),
    )(convolved, convolved, raw, masks, bias_row, rate_row)

    share = PAIRS * STATE // count
    decay_high = device_decay[0].astype(bf16)
    decay_low = (device_decay[0] - decay_high.astype(f32)).astype(bf16)
    decay_rows = jnp.broadcast_to(jnp.stack([decay_high, decay_low])[None], (count, 2, LANES))
    sent = jnp.concatenate([device_state.reshape(count, share, LANES), decay_rows], axis=1)

    def exchange(value):
        return lax.all_to_all(value, EVERY, split_axis=0, concat_axis=0, tiled=True)

    def scan_parts(parts, reverse):
        return pl.pallas_call(
            functools.partial(prefix, reverse=reverse),
            out_shape=jax.ShapeDtypeStruct((count, share, LANES), bf16),
            compiler_params=pltpu.CompilerParams(vmem_limit_bytes=VMEM),
        )(parts, pair_decays, second)

    arrived = exchange(sent)
    all_decays = arrived[:, share, :HEADS].astype(f32) + arrived[:, share + 1, :HEADS].astype(f32)
    wide_decays = jnp.repeat(all_decays, HEAD_SIZE, axis=1).reshape(count, PAIRS, LANES)
    wide_decays = jnp.pad(wide_decays, ((0, 0), (0, 1), (0, 0)))
    first_pair = device_index * share // STATE
    pair_decays = lax.dynamic_slice_in_dim(wide_decays, first_pair, 2, axis=1)
    places = device_index * share + lax.broadcasted_iota(jnp.int32, (share, LANES), 0)
    second = (places >= (first_pair + 1) * STATE).astype(f32)
    prior = exchange(scan_parts(arrived, False)).reshape(PAIRS, STATE, LANES)

    diag = call(
        diagonal,
        (stretches,),
        [
            by_block(INNER),
            both_spec,
            by_block(LANES),
            per_block(32, STRETCH),
            by_block(marks),
            per_block(1, STRETCH),
        ],
        [by_block(INNER)],
        [((rows, INNER), f32)],
        [pltpu.VMEM((HEADS, STRETCH, LANES), f32), pltpu.VMEM((STRETCH, STRETCH), f32)],
        (40e9, 12e6),
    )(scaled, convolved, cumul, cumul_rows, masks, segments)[0]
    gate = jnp.dot(normed, gate_weight, preferred_element_type=f32)

    back = stretches - 1
    by_block_r = lambda *tail: spec((STRETCH,) + tail, lambda c: (back - c,) + (0,) * len(tail))
    per_block_r = lambda *tail: spec((1,) + tail, lambda c: (back - c,) + (0,) * len(tail))
    wide_scratch = lambda kind: pltpu.VMEM((STRETCH, INNER), kind)
    (
        block_output,
        gated_low,
        gate_grad,
        mixed_grad,
        row_sums,
        reads_grad,
        after_local,
        full,
        middle_sums,
        start_grad,
        after_decay,
    ) = call(
        middle,
        (stretches,),
        [
            by_block_r(INNER),
            spec((STRETCH, INNER), lambda c: (back - c, 0)),
            spec((STRETCH, 2 * STATE), lambda c: (back - c, INNER // (2 * STATE))),
            by_block_r(LANES),
            by_block_r(marks),
            per_block_r(STATE, INNER),
            per_block_r(8, INNER),
            whole(PAIRS, STATE, LANES),
            by_block_r(INNER),
            by_block_r(WIDTH),
            by_block_r(WIDTH),
            whole(INNER, WIDTH),
            whole(1, INNER),
            whole(1, INNER),
            whole(INNER, LANES),
        ],
        [
            by_block_r(WIDTH),
            by_block_r(INNER),
            by_block_r(INNER),
            by_block_r(INNER),
            by_block_r(LANES),
            by_block_r(STATE),
            per_block_r(STATE, INNER),
            per_block_r(STATE, INNER),
            whole(8, INNER),
            whole(PAIRS, STATE, LANES),
            per_block_r(8, INNER),
        ],
        [
            ((rows, WIDTH), bf16),
            ((rows, INNER), bf16),
            ((rows, INNER), bf16),
            ((rows, INNER), bf16),
            ((rows, LANES), f32),
            ((rows, STATE), f32),
            ((stretches, STATE, INNER), f32),
            ((stretches, STATE, INNER), bf16),
            ((8, INNER), f32),
            ((PAIRS, STATE, LANES), bf16),
            ((stretches, 8, INNER), f32),
        ],
        [
            wide_scratch(f32),
            wide_scratch(f32),
            wide_scratch(f32),
            wide_scratch(bf16),
            wide_scratch(bf16),
            wide_scratch(bf16),
            pltpu.VMEM((STATE, INNER), f32),
            pltpu.VMEM((8, INNER), f32),
        ],
        (20e9, 40e6),
    )(
        diag, convolved, convolved, cumul, masks, start, factors, prior, gate, block_input, out_cotangent,
        out_full, gain_row, skip_row, head_of,
    )

    sent_back = exchange(start_grad.reshape(count, share, LANES))
    after = exchange(scan_parts(sent_back, True)).reshape(PAIRS, STATE, LANES)

    def scattered(value):
        part = lax.psum_scatter(value, "seq", scatter_dimension=0, tiled=True)
        return lax.optimization_barrier(lax.psum_scatter(part, "head", scatter_dimension=0, tiled=True)).astype(f32)

    out_grad = scattered(mm(gated_low, out_cotangent, TN).astype(bf16))
    gate_weight_grad = scattered(mm(normed, gate_grad, TN).astype(bf16))

    diag_sums, both_grad = call(
        diagonal_back,
        (stretches,),
        [
            by_block(INNER),
            both_spec,
            by_block(LANES),
            per_block(32, STRETCH),
            by_block(marks),
            per_block(1, STRETCH),
            by_block(INNER),
        ],
        [by_block(INNER), by_block(2 * STATE)],
        [((rows, INNER), f32), ((rows, 2 * STATE), f32)],
        [
            pltpu.VMEM((HEADS, STRETCH, LANES), f32),
            pltpu.VMEM((STRETCH, STRETCH), f32),
            pltpu.VMEM((STRETCH, STRETCH), f32),
        ],
        (50e9, 16e6),
    )(scaled, convolved, cumul, cumul_rows, masks, segments, mixed_grad)

    conv_out_grad, raw_grad, late_sums = call(
        late,
        (stretches,),
        [
            values_spec,
            both_spec,
            by_block(LANES),
            by_block(LANES),
            by_block(LANES),
            by_block(marks),
            whole(1, LANES),
            whole(1, LANES),
            per_block(8, INNER),
            per_block(STATE, INNER),
            per_block(STATE, INNER),
            per_block(8, INNER),
            whole(PAIRS, STATE, LANES),
            by_block(INNER),
            by_block(INNER),
            by_block(INNER),
            by_block(LANES),
            by_block(STATE),
            by_block(2 * STATE),
            whole(1, INNER),
            whole(INNER, LANES),
        ],
        [by_block(CONV_CHANNELS), by_block(LANES), whole(8, LANES)],
        [((rows, CONV_CHANNELS), bf16), ((rows, LANES), bf16), ((8, LANES), f32)],
        [
            pltpu.VMEM((STATE, INNER), bf16),
            wide_scratch(f32),
            wide_scratch(f32),
            wide_scratch(f32),
        ]
        + [wide_scratch(bf16)] * 7,
        (10e9, 24e6),
    )(
        convolved, convolved, cumul, delta, raw, masks, bias_row, rate_row, factors, full, after_local, after_decay,
        after, diag_sums, scaled, mixed_grad, row_sums, reads_grad, both_grad, skip_row, head_of,
    )

    mixed_in_grad, rim, tail, tap_grads = call(
        conv_back,
        (CONV_CHANNELS // TILE,),
        [
            spec((rows + HALO, TILE), lambda i: (0, i)),
            spec((rows, TILE), lambda i: (0, i)),
            whole(rows, marks),
            spec((8, TILE), lambda i: (0, i)),
        ],
        [
            spec((rows, TILE), lambda i: (0, i)),
            spec((8, TILE), lambda i: (0, i)),
            spec((HALO, TILE), lambda i: (0, i)),
            spec((8, TILE), lambda i: (0, i)),
        ],
        [
            ((rows, CONV_CHANNELS), bf16),
            ((8, CONV_CHANNELS), f32),
            ((HALO, CONV_CHANNELS), f32),
            ((8, CONV_CHANNELS), f32),
        ],
        [pltpu.VMEM((rows + HALO, TILE), f32), pltpu.VMEM((rows + 8, TILE), f32)],
        (10e9, 12e6),
    )(mixed_low, conv_out_grad, masks, taps)

    from_next = passed_along(rim, EVERY, -1)
    gate_part = mm(gate_grad, gate_weight, NT)
    fixed = jnp.concatenate([tail[: HALO - 8], tail[HALO - 8 :] + from_next], axis=0).astype(bf16)
    mixer_grad = jnp.concatenate(
        [jnp.concatenate([mixed_in_grad[: rows - HALO], fixed], axis=0), raw_grad], axis=1
    )
    mixer_weight_grad = scattered(mm(normed, mixer_grad, TN).astype(bf16))
    normed_in_grad = gate_part + mm(mixer_grad, mixer_weight, NT)
    norm_gain_grad = jnp.sum(normed_in_grad * inputs * in_scale, axis=0)
    scaled_in = normed_in_grad * norm_gain
    input_grad = (
        out_cotangent.astype(f32)
        + in_scale * scaled_in
        - inputs * in_scale**3 * jnp.mean(scaled_in * inputs, axis=-1, keepdims=True)
    )

    vector_local = jnp.concatenate(
        [
            norm_gain_grad,
            middle_sums[0],
            tap_grads[: CONV_WIDTH + 1].reshape(-1),
            late_sums[1, :HEADS],
            late_sums[0, :HEADS] * rate_row[0, :HEADS],
            jnp.sum(middle_sums[1].reshape(HEADS, HEAD_SIZE), axis=1),
        ]
    )
    size = vector_local.shape[0]
    piece = -(-size // count)
    parts = exchange(jnp.pad(vector_local, (0, piece * count - size)).reshape(count, piece))
    total = jnp.broadcast_to(jnp.sum(parts, axis=0, keepdims=True), (count, piece))
    vector_grad = exchange(total).reshape(-1)[:size]

    in_grad = jnp.concatenate([gate_weight_grad, mixer_weight_grad[:, : CONV_CHANNELS + HEADS]], axis=1)
    in_first_new, in_second_new, in_weight_new = adamw(
        in_weight, in_first, in_second, in_grad, RATE_MATRIX, WEIGHT_DECAY
    )
    out_first_new, out_second_new, out_weight_new = adamw(
        out_weight, out_first, out_second, out_grad, RATE_MATRIX, WEIGHT_DECAY
    )
    vector_first_new, vector_second_new, vector_new = adamw(
        vector_params, vector_first, vector_second, vector_grad, RATE_VECTOR, 0.0
    )
    return (
        block_output,
        input_grad.astype(bf16),
        in_first_new,
        in_second_new,
        in_weight_new,
        out_first_new,
        out_second_new,
        out_weight_new,
        vector_first_new,
        vector_second_new,
        vector_new,
    )


def solution(mesh):
    split = P(EVERY, None)
    in_specs = (split, split, P(), split, split, P(), split, split, split, split, P(), P())
    out_specs = (split,) * 8 + (P(),) * 3
    return jax.shard_map(
        per_device, mesh=mesh, in_specs=in_specs, out_specs=out_specs, check_vma=False
    )
```

```python
import functools

import jax
import jax.numpy as jnp
from jax import lax
from jax.experimental import pallas as pl
from jax.experimental.pallas import tpu as pltpu
from jax.sharding import PartitionSpec as P

WIDTH = 768
INNER = 1536
HEADS = 24
HEAD_SIZE = 64
STATE = 128
CONV_WIDTH = 4
STRETCH = 256
STEP = 10
CONV_CHANNELS = 1792
LANES = 128
PAIRS = HEADS // 2
MIXED = CONV_CHANNELS + LANES
HALO = 16
CHUNK = 32
PART = 64
LOG2E = 1.4426950408889634
HALF = STRETCH // 2
TILE = 256

EPS = 1e-05
BETA_ONE = 0.9
BETA_TWO = 0.95
ADAM_EPS = 1e-08
WEIGHT_DECAY = 0.1
RATE_MATRIX = 0.05
RATE_VECTOR = 0.3
HIGHEST = lax.Precision.HIGHEST
f32 = jnp.float32
bf16 = jnp.bfloat16
EVERY = ("seq", "head")
VMEM = 56 * 1024 * 1024


def passed_along(value, axis, steps):
    count = lax.axis_size(axis)
    leading, last = (max(0, -steps), min(count, count - steps))
    return lax.ppermute(value, axis, [(source, source + steps) for source in range(leading, last)])


def split_vector(vector):
    cursor = 0
    pieces = []
    for length in (WIDTH, INNER, CONV_WIDTH * CONV_CHANNELS, CONV_CHANNELS, HEADS, HEADS, HEADS):
        pieces.append(vector[cursor : cursor + length])
        cursor = cursor + length
    norm_gain, gated_gain, conv_flat, conv_bias, step_bias, log_rate, skip_gain = pieces
    return (
        norm_gain,
        gated_gain,
        conv_flat.reshape(CONV_WIDTH, CONV_CHANNELS),
        conv_bias,
        step_bias,
        log_rate,
        skip_gain,
    )


def adamw(weight, first, second, grad, rate, decay):
    first_new = BETA_ONE * first + (1.0 - BETA_ONE) * grad
    second_new = BETA_TWO * second + (1.0 - BETA_TWO) * grad * grad
    corrected_first = first_new / (1.0 - BETA_ONE**STEP)
    corrected_second = second_new / (1.0 - BETA_TWO**STEP)
    weight_new = weight - rate * (
        corrected_first / (jnp.sqrt(corrected_second) + ADAM_EPS) + decay * weight
    )
    return (first_new, second_new, weight_new)


def mm(left, right, dims=((1,), (0,)), precision=None):
    return lax.dot_general(left, right, (dims, ((), ())), preferred_element_type=f32, precision=precision)


NT = ((1,), (1,))
TN = ((0,), (0,))


def spec(block, index):
    return pl.BlockSpec(block, index)


def whole(*shape):
    return pl.BlockSpec(shape, lambda *ids: (0,) * len(shape))


def call(body, grid, ins, outs, out_shapes, scratch, micros):
    return pl.pallas_call(
        body,
        grid=grid,
        in_specs=ins,
        out_specs=outs,
        out_shape=[jax.ShapeDtypeStruct(shape, kind) for shape, kind in out_shapes],
        scratch_shapes=scratch,
        compiler_params=pltpu.CompilerParams(vmem_limit_bytes=VMEM),
        cost_estimate=pl.CostEstimate(flops=0, bytes_accessed=int(micros * 3.4e6), transcendentals=0),
    )


def in_two(value):
    top = value.astype(bf16)
    return top, (value - top.astype(f32)).astype(bf16)


def spread_heads(per_head, spreader):
    return mm(jnp.concatenate(in_two(per_head), axis=1), spreader)


def eights(value):
    return jnp.sum(value.reshape(value.shape[0] // 8, 8, value.shape[1]), axis=0)


def tiles(width):
    return [slice(j * LANES, (j + 1) * LANES) for j in range(width // LANES)]


def chunks(count, size, body):
    def step(i, _):
        body(pl.ds(pl.multiple_of(i * size, size), size))
        return 0

    lax.fori_loop(0, count // size, step, 0)


def sigmoid(v):
    return 0.5 * jnp.tanh(0.5 * v) + 0.5


def softplus(v):
    small = jnp.exp(-jnp.abs(v))
    series = small * (1.0 - small * (0.5 - small * (1.0 / 3.0 - small * 0.25)))
    return jnp.maximum(v, 0.0) + jnp.where(small < 0.01, series, jnp.log(1.0 + small))


def spread_masks(masks, same):
    @pl.when(pl.program_id(0) == 0)
    def _():
        for k in range(1, CONV_WIDTH):
            same[k - 1] = jnp.broadcast_to(masks[:, k - 1 : k], same.shape[1:])


def conv_part(held, same, taps, rows, cols):
    taken = [held[pl.ds(HALO + rows - k, PART), cols] for k in range(CONV_WIDTH)]
    total = taps[CONV_WIDTH : CONV_WIDTH + 1, cols] + taps[3:4, cols] * taken[0]
    for k in range(1, CONV_WIDTH):
        total = total + taps[3 - k : 4 - k, cols] * (taken[k] * same[k - 1, rows : rows + PART, :])
    return total, taken


def conv_forward(normed, weight, masks, taps, out, mixed, held, same):
    spread_masks(masks, same)
    low = mm(normed[...], weight[...]).astype(bf16)
    mixed[...] = low
    held[...] = low.astype(f32)
    for rows in range(0, out.shape[0], PART):
        for cols in tiles(TILE):
            total, _ = conv_part(held, same, taps, rows, cols)
            out[rows : rows + PART, cols] = (total * sigmoid(total)).astype(bf16)


def local_states(
    values, both, raw, masks, bias, rate, spreader,
    scaled, cumul_out, delta_out, cumul_rows, start, factors, device_state, device_decay,
    state, reach, weighted, steps, ends,
):
    c = pl.program_id(0)

    @pl.when(c == 0)
    def _():
        state[...] = jnp.zeros_like(state)
        reach[...] = jnp.ones_like(reach)

    delta = softplus(raw[...].astype(f32) + bias[...])
    row = lax.broadcasted_iota(jnp.int32, (STRETCH, STRETCH), 0)
    col = lax.broadcasted_iota(jnp.int32, (STRETCH, STRETCH), 1)
    cumul = mm((row >= col).astype(f32), delta * rate[...], precision=HIGHEST)
    last = cumul[STRETCH - 1 : STRETCH, :]
    carry = jnp.exp(last) * masks[STRETCH - 1 : STRETCH, 4:5]
    cumul_out[...] = cumul
    delta_out[...] = delta
    cumul_rows[0] = cumul.T[: cumul_rows.shape[1], :] * LOG2E
    steps[...] = spread_heads(delta, spreader[...])
    ends[...] = spread_heads(jnp.exp(last - cumul) * masks[:, 3:4] * delta, spreader[...])
    for cols in tiles(INNER):
        v = values[:, cols].astype(f32)
        scaled[:, cols] = (v * steps[:, cols]).astype(bf16)
        weighted[:, cols] = (v * ends[:, cols]).astype(bf16)
    start[0] = state[...]
    line = lax.broadcasted_iota(jnp.int32, (8, LANES), 0)
    wide = spread_heads(jnp.where(line == 0, carry, reach[...]), spreader[...])
    factors[0] = wide
    state[...] = state[...] * wide[0:1, :] + mm(both[:, :STATE], weighted[...], TN)
    reach[...] = reach[...] * carry

    @pl.when(c == pl.num_programs(0) - 1)
    def _():
        for j, cols in enumerate(tiles(INNER)):
            device_state[j] = state[:, cols].astype(bf16)
        device_decay[...] = reach[...]


def spread_columns(cumul, columns):
    for h in range(HEADS):
        columns[h] = jnp.broadcast_to(cumul[:, h : h + 1] * LOG2E, (STRETCH, LANES))


def diagonal(scaled, both, cumul, cumul_rows, masks, segments, out, columns, scores):
    spread_columns(cumul, columns)
    row = lax.broadcasted_iota(jnp.int32, (STRETCH, STRETCH), 0)
    col = lax.broadcasted_iota(jnp.int32, (STRETCH, STRETCH), 1)
    inside = (row >= col) & (masks[:, 5:6] == segments[0])
    scores[...] = jnp.where(inside, mm(both[:, STATE:], both[:, :STATE], NT), 0.0)
    low = lax.broadcasted_iota(jnp.int32, (HALF, LANES), 1) < HEAD_SIZE

    def pair(j, _):
        cols = pl.ds(pl.multiple_of(j * LANES, LANES), LANES)
        v = scaled[:, cols]
        tops, bottoms = [], []
        for q in range(2):
            h = 2 * j + q
            line = cumul_rows[0, pl.ds(h, 1), :]
            upper = columns[h, :HALF, :]
            lower = columns[h, HALF:, :]
            top = jnp.exp2(jnp.minimum(upper - line[:, :HALF], 0.0)) * scores[:HALF, :HALF]
            left = jnp.exp2(jnp.minimum(lower - line[:, :HALF], 0.0)) * scores[HALF:, :HALF]
            right = jnp.exp2(jnp.minimum(lower - line[:, HALF:], 0.0)) * scores[HALF:, HALF:]
            tops.append(mm(top.astype(bf16), v[:HALF]))
            bottoms.append(mm(jnp.concatenate([left.astype(bf16), right.astype(bf16)], axis=1), v))
        out[:HALF, cols] = jnp.where(low, *tops)
        out[HALF:, cols] = jnp.where(low, *bottoms)
        return 0

    lax.fori_loop(0, PAIRS, pair, 0)


def diagonal_back(
    scaled, both, cumul, cumul_rows, masks, segments, out_grad, sums, both_grad, columns, scores, total
):
    spread_columns(cumul, columns)
    row = lax.broadcasted_iota(jnp.int32, (STRETCH, STRETCH), 0)
    col = lax.broadcasted_iota(jnp.int32, (STRETCH, STRETCH), 1)
    inside = (row <= col) & (masks[:, 5:6] == segments[0])
    scores[...] = jnp.where(inside, mm(both[:, :STATE], both[:, STATE:], NT), 0.0)
    total[...] = jnp.zeros_like(total)
    low = lax.broadcasted_iota(jnp.int32, (HALF, LANES), 1) < HEAD_SIZE
    first = lax.broadcasted_iota(jnp.int32, (STRETCH, LANES), 1) < HEAD_SIZE

    def pair(j, _):
        cols = pl.ds(pl.multiple_of(j * LANES, LANES), LANES)
        v = scaled[:, cols]
        g = out_grad[:, cols]
        tops, bottoms = [], []
        for q in range(2):
            h = 2 * j + q
            line = cumul_rows[0, pl.ds(h, 1), :]
            upper = columns[h, :HALF, :]
            lower = columns[h, HALF:, :]
            own = jnp.where(first == (q == 0), g.astype(f32), 0.0).astype(bf16)
            left = jnp.exp2(jnp.minimum(line[:, :HALF] - upper, 0.0))
            right = jnp.exp2(jnp.minimum(line[:, HALF:] - upper, 0.0))
            corner = jnp.exp2(jnp.minimum(line[:, HALF:] - lower, 0.0))
            tops.append(
                mm(
                    jnp.concatenate(
                        [(left * scores[:HALF, :HALF]).astype(bf16), (right * scores[:HALF, HALF:]).astype(bf16)],
                        axis=1,
                    ),
                    g,
                )
            )
            bottoms.append(mm((corner * scores[HALF:, HALF:]).astype(bf16), g[HALF:]))
            top_grad = mm(v[:HALF], own, NT)
            total[:HALF, :HALF] += left * top_grad[:, :HALF]
            total[:HALF, HALF:] += right * top_grad[:, HALF:]
            total[HALF:, HALF:] += corner * mm(v[HALF:], own[HALF:], NT)
        sums[:HALF, cols] = jnp.where(low, *tops)
        sums[HALF:, cols] = jnp.where(low, *bottoms)
        return 0

    lax.fori_loop(0, PAIRS, pair, 0)
    scores_grad = jnp.where(inside, total[...], 0.0).astype(bf16)
    both_grad[:, :STATE] = mm(scores_grad, both[:, STATE:])
    both_grad[:, STATE:] = mm(scores_grad, both[:, :STATE], TN)


def prefix(parts, decays, second, out, reverse):
    count = parts.shape[0]
    rows = out.shape[1]

    def step(i, state):
        k = count - 1 - i if reverse else i
        out[pl.ds(k, 1)] = state.astype(bf16)[None]
        two = decays[pl.ds(k, 1)][0]
        decay = jnp.where(second[...] > 0.0, two[1:2, :], two[0:1, :])
        return decay * state + parts[pl.ds(k, 1), :rows, :][0].astype(f32)

    lax.fori_loop(0, count, step, jnp.zeros((rows, LANES), f32))


def head_sums(products, heads):
    return sum(mm(product[...], heads[...]) for product in products)


def middle(
    diag, values, both, cumul, masks, start, factors, prior, gate, normed_grad, inputs, weight, gain, skip, heads,
    spreader,
    block_output, gated_low, gate_grad, mixed_grad, row_sums, reads_grad, after_local, full_out, sums, start_grad,
    after_decay, entry, enter, gated_all, sig_all, mixed_all, entry_low, high, low, state_grad, tail_decay,
):
    i = pl.program_id(0)

    @pl.when(i == 0)
    def _():
        state_grad[...] = jnp.zeros_like(state_grad)
        tail_decay[...] = jnp.ones_like(tail_decay)
        sums[...] = jnp.zeros_like(sums)

    reads = both[:, STATE:]
    for j, cols in enumerate(tiles(INNER)):
        full_out[0, :, cols] = (start[0, :, cols] + factors[0, 1:2, cols] * prior[j].astype(f32)).astype(bf16)
    entry[...] = mm(reads, full_out[0])
    enter[...] = spread_heads(jnp.exp(cumul[...]) * masks[:, 4:5], spreader[...])

    def rows_step(rows):
        square = jnp.zeros((CHUNK, LANES), f32)
        cross = jnp.zeros((CHUNK, LANES), f32)
        for cols in tiles(INNER):
            mixed_sum = diag[rows, cols] + entry[rows, cols] * enter[rows, cols]
            mixed = (mixed_sum + skip[:, cols] * values[rows, cols].astype(f32)).astype(bf16)
            z = gate[rows, cols]
            sig = sigmoid(z)
            gated = mixed.astype(f32) * (z * sig)
            square = square + gated * gated
            cross = cross + (normed_grad[rows, cols] * gain[:, cols]) * gated
            entry[rows, cols] = mixed_sum
            gated_all[rows, cols] = gated
            sig_all[rows, cols] = sig
            mixed_all[rows, cols] = mixed
        scale = lax.rsqrt(jnp.sum(square, axis=1, keepdims=True) * (1.0 / INNER) + EPS)
        pull = jnp.sum(cross, axis=1, keepdims=True) * (1.0 / INNER) * (scale * scale * scale)
        scale = jnp.broadcast_to(scale, (CHUNK, LANES))
        pull = jnp.broadcast_to(pull, (CHUNK, LANES))
        for cols in tiles(INNER):
            gated = gated_all[rows, cols]
            sig = sig_all[rows, cols]
            back = normed_grad[rows, cols]
            unit = gated * scale
            gated_low[rows, cols] = (unit * gain[:, cols]).astype(bf16)
            gated_grad = scale * (back * gain[:, cols]) - gated * pull
            act = gate[rows, cols] * sig
            slope = sig + act * (1.0 - sig)
            gate_grad[rows, cols] = (gated_grad * mixed_all[rows, cols].astype(f32) * slope).astype(bf16)
            low_grad = (gated_grad * act).astype(bf16)
            mixed_grad[rows, cols] = low_grad
            grad = low_grad.astype(f32)
            entry_low[rows, cols] = (grad * enter[rows, cols]).astype(bf16)
            high[rows, cols], low[rows, cols] = in_two(grad * entry[rows, cols])
            sums[0:8, cols] += eights(back * unit)
            sums[8:16, cols] += eights(grad * values[rows, cols].astype(f32))

    chunks(STRETCH, CHUNK, rows_step)
    block_output[...] = (inputs[...].astype(f32) + mm(gated_low[...], weight[...])).astype(bf16)
    row_sums[...] = head_sums((high, low), heads)
    reads_grad[...] = mm(entry_low[...], full_out[0], NT)
    after_local[0] = state_grad[...]
    after_decay[0] = tail_decay[...]
    state_grad[...] = state_grad[...] * factors[0, 0:1, :] + mm(reads, entry_low[...], TN)
    tail_decay[...] = tail_decay[...] * factors[0, 0:1, :]

    @pl.when(i == pl.num_programs(0) - 1)
    def _():
        for j, cols in enumerate(tiles(INNER)):
            start_grad[j] = state_grad[:, cols].astype(bf16)


def late(
    values, both, cumul, delta, raw, masks, bias, rate, factors, full, after_local, after_decay, after,
    diag_sums, scaled, out_grad, row_sums, reads_grad, both_grad, skip, heads, spreader,
    conv_grad, raw_grad, sums,
    after_low, spread_grad, factor, wide, weighted, joint, outer_low, high, low,
):
    @pl.when(pl.program_id(0) == 0)
    def _():
        sums[...] = jnp.zeros_like(sums)

    carry_rows = []
    for j, cols in enumerate(tiles(INNER)):
        here = after_local[0, :, cols] + after_decay[0, 0:1, cols] * after[j].astype(f32)
        after_low[:, cols] = here.astype(bf16)
        carry_rows.append(eights(here * full[0, :, cols].astype(f32)) * factors[0, 0:1, cols])
    carry_grad = sum(mm(part, heads[...]) for part in in_two(jnp.concatenate(carry_rows, axis=1)))
    spread_grad[...] = mm(both[:, :STATE], after_low[...])
    step = delta[...]
    total = cumul[...]
    end_factor = jnp.exp(total[STRETCH - 1 : STRETCH, :] - total) * masks[:, 3:4]
    factor[...] = spread_heads(end_factor, spreader[...])
    wide[...] = spread_heads(step, spreader[...])

    def rows_step(rows):
        for cols in tiles(INNER):
            v = values[rows, cols].astype(f32)
            ends = factor[rows, cols]
            step_wide = wide[rows, cols]
            inner = diag_sums[rows, cols]
            outer = spread_grad[rows, cols] * ends
            both_sums = inner + outer
            conv_grad[rows, cols] = (
                step_wide * both_sums + skip[:, cols] * out_grad[rows, cols].astype(f32)
            ).astype(bf16)
            weighted[rows, cols] = (v * (ends * step_wide)).astype(bf16)
            joint[rows, cols] = (v * both_sums).astype(bf16)
            outer_low[rows, cols] = (v * outer).astype(bf16)
            high[rows, cols], low[rows, cols] = in_two(scaled[rows, cols].astype(f32) * inner)

    chunks(STRETCH, CHUNK, rows_step)
    conv_grad[:, INNER : INNER + STATE] = (
        both_grad[:, :STATE] + mm(weighted[...], after_low[...], NT)
    ).astype(bf16)
    conv_grad[:, INNER + STATE :] = (both_grad[:, STATE:] + reads_grad[...]).astype(bf16)
    end_spread = head_sums((outer_low,), heads) * step
    last_grad = jnp.sum(end_spread, axis=0, keepdims=True) + jnp.sum(carry_grad, axis=0, keepdims=True)
    cumul_grad = row_sums[...] - head_sums((high, low), heads) - end_spread
    row = lax.broadcasted_iota(jnp.int32, (STRETCH, STRETCH), 0)
    col = lax.broadcasted_iota(jnp.int32, (STRETCH, STRETCH), 1)
    decay_grad = mm((row <= col).astype(f32), cumul_grad, precision=HIGHEST) + last_grad
    step_grad = head_sums((joint,), heads) + decay_grad * rate[...]
    pre_grad = step_grad * sigmoid(raw[...].astype(f32) + bias[...])
    raw_grad[...] = pre_grad.astype(bf16)
    sums[0:1, :] += jnp.sum(decay_grad * step, axis=0, keepdims=True)
    sums[1:2, :] += jnp.sum(pre_grad, axis=0, keepdims=True)


def conv_back(mixed, grad, masks, taps, out, rim, tail, tap_grads, held, same, kept):
    rows_all = grad.shape[0]
    spread_masks(masks, same)
    held[...] = mixed[...].astype(f32)
    kept[:, pl.ds(rows_all, 8), :] = jnp.zeros((CONV_WIDTH, 8, TILE), f32)
    for cols in tiles(TILE):
        found = [jnp.zeros((8, LANES), f32) for _ in range(CONV_WIDTH + 1)]
        for rows in range(0, rows_all, PART):
            total, taken = conv_part(held, same, taps, rows, cols)
            sig = sigmoid(total)
            here = grad[rows : rows + PART, cols].astype(f32) * (sig * (1.0 + total * (1.0 - sig)))
            found[CONV_WIDTH] = found[CONV_WIDTH] + eights(here)
            for k in range(CONV_WIDTH):
                masked = here if k == 0 else here * same[k - 1, rows : rows + PART, :]
                kept[k, pl.ds(rows, PART), cols] = masked
                found[3 - k] = found[3 - k] + eights(masked * taken[k])
        lines = [jnp.sum(line, axis=0, keepdims=True) for line in found]
        tap_grads[:, cols] = jnp.concatenate(lines + [jnp.zeros((3, LANES), f32)], axis=0)
        for rows in range(0, rows_all, PART):
            value = taps[3:4, cols] * kept[0, pl.ds(rows, PART), cols]
            for k in range(1, CONV_WIDTH):
                value = value + taps[3 - k : 4 - k, cols] * kept[k, pl.ds(rows + k, PART), cols]
            out[rows : rows + PART, cols] = value.astype(bf16)
            if rows + PART == rows_all:
                tail[:, cols] = value[PART - HALO :, :]
        lines = [jnp.zeros((5, LANES), f32)]
        for m in (3, 2, 1):
            line = jnp.zeros((1, LANES), f32)
            for k in range(m, CONV_WIDTH):
                line = line + taps[3 - k : 4 - k, cols] * kept[k, k - m : k - m + 1, cols]
            lines.append(line)
        rim[:, cols] = jnp.concatenate(lines, axis=0)


def per_device(
    block_input,
    out_cotangent,
    segment_ids,
    in_weight,
    out_weight,
    vector_params,
    in_first,
    in_second,
    out_first,
    out_second,
    vector_first,
    vector_second,
):
    count = lax.axis_size("seq") * lax.axis_size("head")
    device_index = lax.axis_index(EVERY)
    rows = block_input.shape[0]
    stretches = rows // STRETCH
    own_rows = in_weight.shape[0]
    norm_gain, gated_gain, conv_taps, conv_bias, step_bias, log_rate, skip_gain = split_vector(vector_params)

    mixer_own = jnp.pad(in_weight[:, INNER:].astype(bf16), ((0, 0), (0, LANES - HEADS)))
    mixer_group = lax.all_gather(mixer_own, "head", axis=0, tiled=True)
    rest_own = jnp.concatenate([in_weight[:, :WIDTH], in_weight[:, WIDTH:INNER], out_weight], axis=0).astype(bf16)
    rest_own, mixer_group = lax.optimization_barrier((rest_own, mixer_group))
    mixer_weight = lax.all_gather(mixer_group, "seq", axis=0, tiled=True)
    rest_group = lax.all_gather(rest_own, "head", axis=0, tiled=True)
    rest_group, mixer_weight = lax.optimization_barrier((rest_group, mixer_weight))
    rest = lax.all_gather(rest_group, "seq", axis=0, tiled=True).reshape(count, -1, WIDTH)
    gate_weight = jnp.concatenate(
        [rest[:, :own_rows].reshape(WIDTH, WIDTH), rest[:, own_rows : 2 * own_rows].reshape(WIDTH, WIDTH)], axis=1
    )
    out_full = rest[:, 2 * own_rows :].reshape(INNER, WIDTH)
    halo = passed_along(block_input[rows - HALO :], EVERY, 1)

    def unit_rows(block):
        wide = block.astype(f32)
        scale = lax.rsqrt(jnp.mean(wide * wide, axis=-1, keepdims=True) + EPS)
        return wide, scale

    inputs, in_scale = unit_rows(block_input)
    normed = (inputs * in_scale * norm_gain).astype(bf16)
    halo_wide, halo_scale = unit_rows(halo)
    extended = jnp.concatenate([(halo_wide * halo_scale * norm_gain).astype(bf16), normed], axis=0)

    padded = jnp.concatenate(
        [jnp.full((3,), -1, jnp.int32), segment_ids, jnp.full((3,), -1, jnp.int32)]
    )
    window = lax.dynamic_slice_in_dim(padded, device_index * rows, rows + 6)
    own = window[3 : 3 + rows]
    blocks = own.reshape(stretches, STRETCH)
    before = window[2 : 2 + rows].reshape(stretches, STRETCH)[:, :1]
    columns = [(window[3 - k : 3 - k + rows] == own) for k in (1, 2, 3)]
    columns.append((blocks == blocks[:, -1:]).reshape(rows))
    columns.append((blocks == before).reshape(rows))
    columns.append(own)
    columns += [jnp.zeros((rows,), f32)] * 2
    masks = jnp.stack([column.astype(f32) for column in columns], axis=1)
    marks = masks.shape[1]
    segments = blocks.astype(f32).reshape(stretches, 1, STRETCH)

    taps = jnp.concatenate([conv_taps, conv_bias[None], jnp.zeros((3, CONV_CHANNELS), f32)], axis=0)

    def head_row(vector):
        return jnp.pad(vector, (0, LANES - HEADS)).reshape(1, LANES)

    bias_row = head_row(step_bias)
    rate_row = head_row(-jnp.exp(log_rate))
    skip_row = jnp.repeat(skip_gain, HEAD_SIZE).reshape(1, INNER)
    gain_row = gated_gain.reshape(1, INNER)
    head_of = (
        lax.broadcasted_iota(jnp.int32, (INNER, LANES), 0) // HEAD_SIZE
        == lax.broadcasted_iota(jnp.int32, (INNER, LANES), 1)
    ).astype(bf16)
    spreader = jnp.concatenate([head_of.T, head_of.T], axis=0)

    convolved, mixed_low = call(
        conv_forward,
        (CONV_CHANNELS // TILE,),
        [
            whole(rows + HALO, WIDTH),
            spec((WIDTH, TILE), lambda i: (0, i)),
            whole(rows, marks),
            spec((8, TILE), lambda i: (0, i)),
        ],
        [spec((rows, TILE), lambda i: (0, i)), spec((rows + HALO, TILE), lambda i: (0, i))],
        [((rows, CONV_CHANNELS), bf16), ((rows + HALO, CONV_CHANNELS), bf16)],
        [pltpu.VMEM((rows + HALO, TILE), f32), pltpu.VMEM((3, rows, LANES), f32)],
        11,
    )(extended, mixer_weight, masks, taps)
    raw = jnp.dot(normed, mixer_weight[:, CONV_CHANNELS:], preferred_element_type=f32).astype(bf16)

    by_block = lambda *tail: spec((STRETCH,) + tail, lambda c: (c,) + (0,) * len(tail))
    both_spec = spec((STRETCH, 2 * STATE), lambda c: (c, INNER // (2 * STATE)))
    values_spec = spec((STRETCH, INNER), lambda c: (c, 0))
    per_block = lambda *tail: spec((1,) + tail, lambda c: (c,) + (0,) * len(tail))

    scaled, cumul, delta, cumul_rows, start, factors, device_state, device_decay = call(
        local_states,
        (stretches,),
        [values_spec, both_spec, by_block(LANES), by_block(marks), whole(1, LANES), whole(1, LANES), whole(2 * LANES, INNER)],
        [
            by_block(INNER),
            by_block(LANES),
            by_block(LANES),
            per_block(32, STRETCH),
            per_block(STATE, INNER),
            per_block(8, INNER),
            whole(PAIRS, STATE, LANES),
            whole(8, LANES),
        ],
        [
            ((rows, INNER), bf16),
            ((rows, LANES), f32),
            ((rows, LANES), f32),
            ((stretches, 32, STRETCH), f32),
            ((stretches, STATE, INNER), f32),
            ((stretches, 8, INNER), f32),
            ((PAIRS, STATE, LANES), bf16),
            ((8, LANES), f32),
        ],
        [
            pltpu.VMEM((STATE, INNER), f32),
            pltpu.VMEM((8, LANES), f32),
            pltpu.VMEM((STRETCH, INNER), bf16),
            pltpu.VMEM((STRETCH, INNER), f32),
            pltpu.VMEM((STRETCH, INNER), f32),
        ],
        10,
    )(convolved, convolved, raw, masks, bias_row, rate_row, spreader)

    share = PAIRS * STATE // count
    decay_high = device_decay[0].astype(bf16)
    decay_low = (device_decay[0] - decay_high.astype(f32)).astype(bf16)
    decay_rows = jnp.broadcast_to(jnp.stack([decay_high, decay_low])[None], (count, 2, LANES))
    sent = jnp.concatenate([device_state.reshape(count, share, LANES), decay_rows], axis=1)

    def exchange(value):
        return lax.all_to_all(value, EVERY, split_axis=0, concat_axis=0, tiled=True)

    def scan_parts(parts, reverse):
        return pl.pallas_call(
            functools.partial(prefix, reverse=reverse),
            out_shape=jax.ShapeDtypeStruct((count, share, LANES), bf16),
            compiler_params=pltpu.CompilerParams(vmem_limit_bytes=VMEM),
        )(parts, pair_decays, second)

    arrived = exchange(sent)
    all_decays = arrived[:, share, :HEADS].astype(f32) + arrived[:, share + 1, :HEADS].astype(f32)
    wide_decays = jnp.repeat(all_decays, HEAD_SIZE, axis=1).reshape(count, PAIRS, LANES)
    wide_decays = jnp.pad(wide_decays, ((0, 0), (0, 1), (0, 0)))
    first_pair = device_index * share // STATE
    pair_decays = lax.dynamic_slice_in_dim(wide_decays, first_pair, 2, axis=1)
    places = device_index * share + lax.broadcasted_iota(jnp.int32, (share, LANES), 0)
    second = (places >= (first_pair + 1) * STATE).astype(f32)
    prior = exchange(scan_parts(arrived, False)).reshape(PAIRS, STATE, LANES)

    diag = call(
        diagonal,
        (stretches,),
        [
            by_block(INNER),
            both_spec,
            by_block(LANES),
            per_block(32, STRETCH),
            by_block(marks),
            per_block(1, STRETCH),
        ],
        [by_block(INNER)],
        [((rows, INNER), f32)],
        [pltpu.VMEM((HEADS, STRETCH, LANES), f32), pltpu.VMEM((STRETCH, STRETCH), f32)],
        16,
    )(scaled, convolved, cumul, cumul_rows, masks, segments)[0]
    gate = jnp.dot(normed, gate_weight, preferred_element_type=f32)
    normed_grad = mm(out_cotangent, out_full, NT)

    back = stretches - 1
    by_block_r = lambda *tail: spec((STRETCH,) + tail, lambda c: (back - c,) + (0,) * len(tail))
    per_block_r = lambda *tail: spec((1,) + tail, lambda c: (back - c,) + (0,) * len(tail))
    wide_scratch = lambda kind: pltpu.VMEM((STRETCH, INNER), kind)
    (
        block_output,
        gated_low,
        gate_grad,
        mixed_grad,
        row_sums,
        reads_grad,
        after_local,
        full,
        middle_sums,
        start_grad,
        after_decay,
    ) = call(
        middle,
        (stretches,),
        [
            by_block_r(INNER),
            spec((STRETCH, INNER), lambda c: (back - c, 0)),
            spec((STRETCH, 2 * STATE), lambda c: (back - c, INNER // (2 * STATE))),
            by_block_r(LANES),
            by_block_r(marks),
            per_block_r(STATE, INNER),
            per_block_r(8, INNER),
            whole(PAIRS, STATE, LANES),
            by_block_r(INNER),
            by_block_r(INNER),
            by_block_r(WIDTH),
            whole(INNER, WIDTH),
            whole(1, INNER),
            whole(1, INNER),
            whole(INNER, LANES),
            whole(2 * LANES, INNER),
        ],
        [
            by_block_r(WIDTH),
            by_block_r(INNER),
            by_block_r(INNER),
            by_block_r(INNER),
            by_block_r(LANES),
            by_block_r(STATE),
            per_block_r(STATE, INNER),
            per_block_r(STATE, INNER),
            whole(16, INNER),
            whole(PAIRS, STATE, LANES),
            per_block_r(8, INNER),
        ],
        [
            ((rows, WIDTH), bf16),
            ((rows, INNER), bf16),
            ((rows, INNER), bf16),
            ((rows, INNER), bf16),
            ((rows, LANES), f32),
            ((rows, STATE), f32),
            ((stretches, STATE, INNER), f32),
            ((stretches, STATE, INNER), bf16),
            ((16, INNER), f32),
            ((PAIRS, STATE, LANES), bf16),
            ((stretches, 8, INNER), f32),
        ],
        [
            wide_scratch(f32),
            wide_scratch(f32),
            wide_scratch(f32),
            wide_scratch(f32),
            wide_scratch(bf16),
            wide_scratch(bf16),
            wide_scratch(bf16),
            wide_scratch(bf16),
            pltpu.VMEM((STATE, INNER), f32),
            pltpu.VMEM((8, INNER), f32),
        ],
        25,
    )(
        diag, convolved, convolved, cumul, masks, start, factors, prior, gate, normed_grad, block_input,
        out_full, gain_row, skip_row, head_of, spreader,
    )

    sent_back = exchange(start_grad.reshape(count, share, LANES))
    after = exchange(scan_parts(sent_back, True)).reshape(PAIRS, STATE, LANES)

    def scattered(value):
        part = lax.psum_scatter(value, "seq", scatter_dimension=0, tiled=True)
        return lax.optimization_barrier(lax.psum_scatter(part, "head", scatter_dimension=0, tiled=True)).astype(f32)

    def scattered_by_parts(value):
        members, width = lax.axis_size("seq"), value.shape[1]
        chips = members // 2
        core = lax.rem(lax.axis_index("seq"), 2)
        parts = value.reshape(chips, 2, -1, width)
        kept = lax.dynamic_index_in_dim(parts, core, 1, keepdims=False)
        given = lax.dynamic_index_in_dim(parts, 1 - core, 1, keepdims=False)
        taken = lax.ppermute(given, "seq", [(k, k + 1 - 2 * (k % 2)) for k in range(members)])
        pair = (kept.astype(f32) + taken.astype(f32)).astype(bf16)
        groups = [list(range(k, members, 2)) for k in range(2)]
        spread = lax.all_to_all(pair, "seq", split_axis=0, concat_axis=0, tiled=True, axis_index_groups=groups)
        line = jnp.sum(spread.astype(f32), axis=0).astype(bf16).reshape(lax.axis_size("head"), -1, width)
        spread = lax.all_to_all(line, "head", split_axis=0, concat_axis=0, tiled=True)
        return jnp.sum(spread.astype(f32), axis=0)

    gate_term = mm(normed, gate_grad, TN).astype(bf16)
    out_term = mm(gated_low, out_cotangent, TN).astype(bf16)
    rest_grad = scattered(
        jnp.concatenate(
            [
                gate_term[:, :WIDTH].reshape(count, -1, WIDTH),
                gate_term[:, WIDTH:].reshape(count, -1, WIDTH),
                out_term.reshape(count, -1, WIDTH),
            ],
            axis=1,
        ).reshape(-1, WIDTH)
    )
    gate_weight_grad = jnp.concatenate([rest_grad[:own_rows], rest_grad[own_rows : 2 * own_rows]], axis=1)
    out_grad = rest_grad[2 * own_rows :]

    diag_sums, both_grad = call(
        diagonal_back,
        (stretches,),
        [
            by_block(INNER),
            both_spec,
            by_block(LANES),
            per_block(32, STRETCH),
            by_block(marks),
            per_block(1, STRETCH),
            by_block(INNER),
        ],
        [by_block(INNER), by_block(2 * STATE)],
        [((rows, INNER), f32), ((rows, 2 * STATE), f32)],
        [
            pltpu.VMEM((HEADS, STRETCH, LANES), f32),
            pltpu.VMEM((STRETCH, STRETCH), f32),
            pltpu.VMEM((STRETCH, STRETCH), f32),
        ],
        20,
    )(scaled, convolved, cumul, cumul_rows, masks, segments, mixed_grad)

    conv_out_grad, raw_grad, late_sums = call(
        late,
        (stretches,),
        [
            values_spec,
            both_spec,
            by_block(LANES),
            by_block(LANES),
            by_block(LANES),
            by_block(marks),
            whole(1, LANES),
            whole(1, LANES),
            per_block(8, INNER),
            per_block(STATE, INNER),
            per_block(STATE, INNER),
            per_block(8, INNER),
            whole(PAIRS, STATE, LANES),
            by_block(INNER),
            by_block(INNER),
            by_block(INNER),
            by_block(LANES),
            by_block(STATE),
            by_block(2 * STATE),
            whole(1, INNER),
            whole(INNER, LANES),
            whole(2 * LANES, INNER),
        ],
        [by_block(CONV_CHANNELS), by_block(LANES), whole(8, LANES)],
        [((rows, CONV_CHANNELS), bf16), ((rows, LANES), bf16), ((8, LANES), f32)],
        [
            pltpu.VMEM((STATE, INNER), bf16),
            wide_scratch(f32),
            wide_scratch(f32),
            wide_scratch(f32),
        ]
        + [wide_scratch(bf16)] * 5,
        18,
    )(
        convolved, convolved, cumul, delta, raw, masks, bias_row, rate_row, factors, full, after_local, after_decay,
        after, diag_sums, scaled, mixed_grad, row_sums, reads_grad, both_grad, skip_row, head_of, spreader,
    )

    mixed_in_grad, rim, tail, tap_grads = call(
        conv_back,
        (CONV_CHANNELS // TILE,),
        [
            spec((rows + HALO, TILE), lambda i: (0, i)),
            spec((rows, TILE), lambda i: (0, i)),
            whole(rows, marks),
            spec((8, TILE), lambda i: (0, i)),
        ],
        [
            spec((rows, TILE), lambda i: (0, i)),
            spec((8, TILE), lambda i: (0, i)),
            spec((HALO, TILE), lambda i: (0, i)),
            spec((8, TILE), lambda i: (0, i)),
        ],
        [
            ((rows, CONV_CHANNELS), bf16),
            ((8, CONV_CHANNELS), f32),
            ((HALO, CONV_CHANNELS), f32),
            ((8, CONV_CHANNELS), f32),
        ],
        [
            pltpu.VMEM((rows + HALO, TILE), f32),
            pltpu.VMEM((3, rows, LANES), f32),
            pltpu.VMEM((CONV_WIDTH, rows + 8, TILE), f32),
        ],
        15,
    )(mixed_low, conv_out_grad, masks, taps)

    from_next = passed_along(rim, EVERY, -1)
    gate_part = mm(gate_grad, gate_weight, NT)
    fixed = jnp.concatenate([tail[: HALO - 8], tail[HALO - 8 :] + from_next], axis=0).astype(bf16)
    mixer_grad = jnp.concatenate(
        [jnp.concatenate([mixed_in_grad[: rows - HALO], fixed], axis=0), raw_grad], axis=1
    )
    mixer_weight_grad = scattered_by_parts(mm(normed, mixer_grad, TN).astype(bf16))
    normed_in_grad = gate_part + mm(mixer_grad, mixer_weight, NT)
    norm_gain_grad = jnp.sum(normed_in_grad * inputs * in_scale, axis=0)
    scaled_in = normed_in_grad * norm_gain
    input_grad = (
        out_cotangent.astype(f32)
        + in_scale * scaled_in
        - inputs * in_scale**3 * jnp.mean(scaled_in * inputs, axis=-1, keepdims=True)
    )

    vector_local = jnp.concatenate(
        [
            norm_gain_grad,
            jnp.sum(middle_sums[:8], axis=0),
            tap_grads[: CONV_WIDTH + 1].reshape(-1),
            late_sums[1, :HEADS],
            late_sums[0, :HEADS] * rate_row[0, :HEADS],
            jnp.sum(middle_sums[8:].reshape(8, HEADS, HEAD_SIZE), axis=(0, 2)),
        ]
    )
    size = vector_local.shape[0]
    piece = -(-size // count)
    parts = exchange(jnp.pad(vector_local, (0, piece * count - size)).reshape(count, piece))
    total = jnp.broadcast_to(jnp.sum(parts, axis=0, keepdims=True), (count, piece))
    vector_grad = exchange(total).reshape(-1)[:size]

    in_grad = jnp.concatenate([gate_weight_grad, mixer_weight_grad[:, : CONV_CHANNELS + HEADS]], axis=1)
    in_first_new, in_second_new, in_weight_new = adamw(
        in_weight, in_first, in_second, in_grad, RATE_MATRIX, WEIGHT_DECAY
    )
    out_first_new, out_second_new, out_weight_new = adamw(
        out_weight, out_first, out_second, out_grad, RATE_MATRIX, WEIGHT_DECAY
    )
    vector_first_new, vector_second_new, vector_new = adamw(
        vector_params, vector_first, vector_second, vector_grad, RATE_VECTOR, 0.0
    )
    return (
        block_output,
        input_grad.astype(bf16),
        in_first_new,
        in_second_new,
        in_weight_new,
        out_first_new,
        out_second_new,
        out_weight_new,
        vector_first_new,
        vector_second_new,
        vector_new,
    )


def solution(mesh):
    split = P(EVERY, None)
    in_specs = (split, split, P(), split, split, P(), split, split, split, split, P(), P())
    out_specs = (split,) * 8 + (P(),) * 3
    return jax.shard_map(
        per_device, mesh=mesh, in_specs=in_specs, out_specs=out_specs, check_vma=False
    )
```

```python
import functools

import jax
import jax.numpy as jnp
from jax import lax
from jax.experimental import pallas as pl
from jax.experimental.pallas import tpu as pltpu
from jax.sharding import PartitionSpec as P

WIDTH = 768
INNER = 1536
HEADS = 24
HEAD_SIZE = 64
STATE = 128
CONV_WIDTH = 4
STRETCH = 256
STEP = 10
CONV_CHANNELS = 1792
LANES = 128
PAIRS = HEADS // 2
MIXED = CONV_CHANNELS + LANES
HALO = 16
CHUNK = 32
PART = 64
LOG2E = 1.4426950408889634
HALF = STRETCH // 2
TILE = 384

EPS = 1e-05
BETA_ONE = 0.9
BETA_TWO = 0.95
ADAM_EPS = 1e-08
WEIGHT_DECAY = 0.1
RATE_MATRIX = 0.05
RATE_VECTOR = 0.3
HIGHEST = lax.Precision.HIGHEST
f32 = jnp.float32
bf16 = jnp.bfloat16
EVERY = ("seq", "head")
ROOM = 56 * 1024 * 1024


def passed_along(value, axis, steps):
    count = lax.axis_size(axis)
    leading, last = (max(0, -steps), min(count, count - steps))
    return lax.ppermute(value, axis, [(source, source + steps) for source in range(leading, last)])


def fetched(value, axis, bit):
    return lax.ppermute(value, axis, [(k, k ^ bit) for k in range(lax.axis_size(axis))])


def laid(pieces):
    rows, width = pieces[0][1].shape
    whole_array = jnp.zeros((rows * len(pieces), width), pieces[0][1].dtype)
    for place, piece in pieces:
        whole_array = lax.dynamic_update_slice(whole_array, piece, (place * rows, 0))
    return whole_array


def split_vector(vector):
    cursor = 0
    pieces = []
    for length in (WIDTH, INNER, CONV_WIDTH * CONV_CHANNELS, CONV_CHANNELS, HEADS, HEADS, HEADS):
        pieces.append(vector[cursor : cursor + length])
        cursor = cursor + length
    norm_gain, gated_gain, conv_flat, conv_bias, step_bias, log_rate, skip_gain = pieces
    return (
        norm_gain,
        gated_gain,
        conv_flat.reshape(CONV_WIDTH, CONV_CHANNELS),
        conv_bias,
        step_bias,
        log_rate,
        skip_gain,
    )


def adamw(weight, first, second, grad, rate, decay):
    first_new = BETA_ONE * first + (1.0 - BETA_ONE) * grad
    second_new = BETA_TWO * second + (1.0 - BETA_TWO) * grad * grad
    corrected_first = first_new / (1.0 - BETA_ONE**STEP)
    corrected_second = second_new / (1.0 - BETA_TWO**STEP)
    weight_new = weight - rate * (
        corrected_first / (jnp.sqrt(corrected_second) + ADAM_EPS) + decay * weight
    )
    return (first_new, second_new, weight_new)


def mm(left, right, dims=((1,), (0,)), precision=None):
    return lax.dot_general(left, right, (dims, ((), ())), preferred_element_type=f32, precision=precision)


NT = ((1,), (1,))
TN = ((0,), (0,))


def spec(block, index):
    return pl.BlockSpec(block, index)


def whole(*shape):
    return pl.BlockSpec(shape, lambda *ids: (0,) * len(shape))


def call(body, grid, ins, outs, out_shapes, scratch, micros):
    return pl.pallas_call(
        body,
        grid=grid,
        in_specs=ins,
        out_specs=outs,
        out_shape=[jax.ShapeDtypeStruct(shape, kind) for shape, kind in out_shapes],
        scratch_shapes=scratch,
        compiler_params=pltpu.CompilerParams(vmem_limit_bytes=ROOM),
        cost_estimate=pl.CostEstimate(flops=0, bytes_accessed=int(micros * 3.4e6), transcendentals=0),
    )


def in_two(value):
    top = value.astype(bf16)
    return top, (value - top.astype(f32)).astype(bf16)


def spread_heads(per_head, spreader):
    return mm(jnp.concatenate(in_two(per_head), axis=1), spreader)


def eights(value):
    return jnp.sum(value.reshape(value.shape[0] // 8, 8, value.shape[1]), axis=0)


def tiles(width):
    return [slice(j * LANES, (j + 1) * LANES) for j in range(width // LANES)]


def chunks(count, size, body):
    def step(i, _):
        body(pl.ds(pl.multiple_of(i * size, size), size))
        return 0

    lax.fori_loop(0, count // size, step, 0, unroll=2)


def sigmoid(v):
    return 0.5 * jnp.tanh(0.5 * v) + 0.5


def softplus(v):
    small = jnp.exp(-jnp.abs(v))
    series = small * (1.0 - small * (0.5 - small * (1.0 / 3.0 - small * 0.25)))
    return jnp.maximum(v, 0.0) + jnp.where(small < 0.01, series, jnp.log(1.0 + small))


def spread_masks(masks, same):
    @pl.when(pl.program_id(0) == 0)
    def _():
        for k in range(1, CONV_WIDTH):
            same[k - 1] = jnp.broadcast_to(masks[:, k - 1 : k], same.shape[1:])


def hold(mixed, held):
    count = mixed.shape[0] - HALO
    for j, cols in enumerate(tiles(TILE)):
        held[j, :HALO, :] = mixed[count:, cols].astype(f32)
        held[j, HALO:, :] = mixed[:count, cols].astype(f32)


def conv_part(held, same, taps, rows, cols):
    taken = [held[cols.start // LANES, pl.ds(HALO + rows - k, PART), :] for k in range(CONV_WIDTH)]
    total = taps[CONV_WIDTH : CONV_WIDTH + 1, cols] + taps[3:4, cols] * taken[0]
    for k in range(1, CONV_WIDTH):
        total = total + taps[3 - k : 4 - k, cols] * (taken[k] * same[k - 1, rows : rows + PART, :])
    return total, taken


def each_tile(convolve, other):
    for cols in tiles(TILE)[:-1]:
        convolve(cols)
    ending = pl.program_id(0) == pl.num_programs(0) - 1
    cols = tiles(TILE)[-1]
    pl.when(jnp.logical_not(ending))(lambda: convolve(cols))
    pl.when(ending)(lambda: other(cols))


def conv_forward(bits, where, normed, masks, taps, *others):
    pieces, (out, mixed, weight_out, held, same, weight) = others[: len(bits)], others[len(bits) :]
    count = out.shape[0]
    spread_masks(masks, same)
    size = pieces[0].shape[0]
    for bit, piece in zip(bits, pieces):
        start = pl.multiple_of((where[0] ^ bit) * size, 8)
        weight[pl.ds(start, size), :] = piece[...].astype(f32)
    weight_out[...] = weight[...].astype(bf16)
    low = mm(normed[...], weight_out[...]).astype(bf16)
    mixed[...] = low
    hold(low, held)

    def convolve(cols):
        for rows in range(0, count, PART):
            total, _ = conv_part(held, same, taps, rows, cols)
            out[rows : rows + PART, cols] = (total * sigmoid(total)).astype(bf16)

    def other(cols):
        out[:, cols] = mixed[:count, cols]

    each_tile(convolve, other)


def local_states(
    values, both, raw, masks, bias, rate, spreader,
    scaled, cumul_out, delta_out, cumul_rows, start, factors, device_state, device_decay,
    state, reach, weighted, steps, ends,
):
    c = pl.program_id(0)

    @pl.when(c == 0)
    def _():
        state[...] = jnp.zeros_like(state)
        reach[...] = jnp.ones_like(reach)

    delta = softplus(raw[...].astype(f32) + bias[...])
    row = lax.broadcasted_iota(jnp.int32, (STRETCH, STRETCH), 0)
    col = lax.broadcasted_iota(jnp.int32, (STRETCH, STRETCH), 1)
    cumul = mm((row >= col).astype(f32), delta * rate[...], precision=HIGHEST)
    last = cumul[STRETCH - 1 : STRETCH, :]
    carry = jnp.exp(last) * masks[STRETCH - 1 : STRETCH, 4:5]
    cumul_out[...] = cumul
    delta_out[...] = delta
    cumul_rows[0] = cumul.T[: cumul_rows.shape[1], :] * LOG2E
    steps[...] = spread_heads(delta, spreader[...])
    ends[...] = spread_heads(jnp.exp(last - cumul) * masks[:, 3:4] * delta, spreader[...])
    for cols in tiles(INNER):
        v = values[:, cols].astype(f32)
        scaled[:, cols] = (v * steps[:, cols]).astype(bf16)
        weighted[:, cols] = (v * ends[:, cols]).astype(bf16)
    start[0] = state[...].astype(bf16)
    line = lax.broadcasted_iota(jnp.int32, (8, LANES), 0)
    wide = spread_heads(jnp.where(line == 0, carry, reach[...]), spreader[...])
    factors[0] = wide
    state[...] = state[...] * wide[0:1, :] + mm(both[:, :STATE], weighted[...], TN)
    reach[...] = reach[...] * carry

    @pl.when(c == pl.num_programs(0) - 1)
    def _():
        for j, cols in enumerate(tiles(INNER)):
            device_state[j] = state[:, cols].astype(bf16)
        device_decay[...] = reach[...]


def spread_columns(cumul, columns):
    for h in range(HEADS):
        columns[h] = jnp.broadcast_to(cumul[:, h : h + 1] * LOG2E, (STRETCH, LANES))


def diagonal(scaled, both, cumul, cumul_rows, masks, segments, out, columns, scores):
    spread_columns(cumul, columns)
    row = lax.broadcasted_iota(jnp.int32, (STRETCH, STRETCH), 0)
    col = lax.broadcasted_iota(jnp.int32, (STRETCH, STRETCH), 1)
    inside = (row >= col) & (masks[:, 5:6] == segments[0])
    scores[...] = jnp.where(inside, mm(both[:, STATE:], both[:, :STATE], NT), 0.0)
    low = lax.broadcasted_iota(jnp.int32, (HALF, LANES), 1) < HEAD_SIZE

    def pair(j, _):
        cols = pl.ds(pl.multiple_of(j * LANES, LANES), LANES)
        v = scaled[:, cols]
        tops, bottoms = [], []
        for q in range(2):
            h = 2 * j + q
            line = cumul_rows[0, pl.ds(h, 1), :]
            upper = columns[h, :HALF, :]
            lower = columns[h, HALF:, :]
            top = jnp.exp2(jnp.minimum(upper - line[:, :HALF], 0.0)) * scores[:HALF, :HALF]
            left = jnp.exp2(jnp.minimum(lower - line[:, :HALF], 0.0)) * scores[HALF:, :HALF]
            right = jnp.exp2(jnp.minimum(lower - line[:, HALF:], 0.0)) * scores[HALF:, HALF:]
            tops.append(mm(top.astype(bf16), v[:HALF]))
            bottoms.append(mm(jnp.concatenate([left.astype(bf16), right.astype(bf16)], axis=1), v))
        out[:HALF, cols] = jnp.where(low, *tops)
        out[HALF:, cols] = jnp.where(low, *bottoms)
        return 0

    lax.fori_loop(0, PAIRS, pair, 0, unroll=2)


def diagonal_back(
    scaled, both, cumul, cumul_rows, masks, segments, out_grad, sums, both_grad, columns, scores, total
):
    spread_columns(cumul, columns)
    row = lax.broadcasted_iota(jnp.int32, (STRETCH, STRETCH), 0)
    col = lax.broadcasted_iota(jnp.int32, (STRETCH, STRETCH), 1)
    inside = (row <= col) & (masks[:, 5:6] == segments[0])
    scores[...] = jnp.where(inside, mm(both[:, :STATE], both[:, STATE:], NT), 0.0)
    total[...] = jnp.zeros_like(total)
    low = lax.broadcasted_iota(jnp.int32, (HALF, LANES), 1) < HEAD_SIZE
    first = lax.broadcasted_iota(jnp.int32, (STRETCH, LANES), 1) < HEAD_SIZE

    def pair(j, _):
        cols = pl.ds(pl.multiple_of(j * LANES, LANES), LANES)
        v = scaled[:, cols]
        g = out_grad[:, cols]
        tops, bottoms = [], []
        for q in range(2):
            h = 2 * j + q
            line = cumul_rows[0, pl.ds(h, 1), :]
            upper = columns[h, :HALF, :]
            lower = columns[h, HALF:, :]
            own = jnp.where(first == (q == 0), g.astype(f32), 0.0).astype(bf16)
            left = jnp.exp2(jnp.minimum(line[:, :HALF] - upper, 0.0))
            right = jnp.exp2(jnp.minimum(line[:, HALF:] - upper, 0.0))
            corner = jnp.exp2(jnp.minimum(line[:, HALF:] - lower, 0.0))
            tops.append(
                mm(
                    jnp.concatenate(
                        [(left * scores[:HALF, :HALF]).astype(bf16), (right * scores[:HALF, HALF:]).astype(bf16)],
                        axis=1,
                    ),
                    g,
                )
            )
            bottoms.append(mm((corner * scores[HALF:, HALF:]).astype(bf16), g[HALF:]))
            top_grad = mm(v[:HALF], own, NT)
            total[:HALF, :HALF] += left * top_grad[:, :HALF]
            total[:HALF, HALF:] += right * top_grad[:, HALF:]
            total[HALF:, HALF:] += corner * mm(v[HALF:], own[HALF:], NT)
        sums[:HALF, cols] = jnp.where(low, *tops)
        sums[HALF:, cols] = jnp.where(low, *bottoms)
        return 0

    lax.fori_loop(0, PAIRS, pair, 0, unroll=2)
    scores_grad = jnp.where(inside, total[...], 0.0).astype(bf16)
    both_grad[:, :STATE] = mm(scores_grad, both[:, STATE:])
    both_grad[:, STATE:] = mm(scores_grad, both[:, :STATE], TN)


def prefix(parts, decays, second, out, reverse):
    count = parts.shape[0]
    rows = out.shape[1]

    def step(i, state):
        k = count - 1 - i if reverse else i
        out[pl.ds(k, 1)] = state.astype(bf16)[None]
        two = decays[pl.ds(k, 1)][0]
        decay = jnp.where(second[...] > 0.0, two[1:2, :], two[0:1, :])
        return decay * state + parts[pl.ds(k, 1), :rows, :][0].astype(f32)

    lax.fori_loop(0, count, step, jnp.zeros((rows, LANES), f32))


def head_sums(products, heads):
    return sum(mm(product[...], heads[...]) for product in products)


def entered(start, factors, prior, j, cols):
    return start[0, :, cols].astype(f32) + factors[0, 1:2, cols] * prior[j].astype(f32)


def middle(
    diag, values, both, cumul, masks, start, factors, prior, gate, normed_grad, gain, skip, heads,
    spreader,
    gated_low, gate_grad, mixed_grad, row_sums, reads_grad, after_local, sums, start_grad,
    after_decay, full, entry, enter, gated_all, sig_all, mixed_all, entry_low, high, low, state_grad, tail_decay,
):
    i = pl.program_id(0)

    @pl.when(i == 0)
    def _():
        state_grad[...] = jnp.zeros_like(state_grad)
        tail_decay[...] = jnp.ones_like(tail_decay)
        sums[...] = jnp.zeros_like(sums)

    reads = both[:, STATE:]
    for j, cols in enumerate(tiles(INNER)):
        full[:, cols] = entered(start, factors, prior, j, cols).astype(bf16)
    entry[...] = mm(reads, full[...])
    enter[...] = spread_heads(jnp.exp(cumul[...]) * masks[:, 4:5], spreader[...])

    def rows_step(rows):
        square = jnp.zeros((CHUNK, LANES), f32)
        cross = jnp.zeros((CHUNK, LANES), f32)
        for cols in tiles(INNER):
            mixed_sum = diag[rows, cols] + entry[rows, cols] * enter[rows, cols]
            mixed = (mixed_sum + skip[:, cols] * values[rows, cols].astype(f32)).astype(bf16)
            z = gate[rows, cols]
            sig = sigmoid(z)
            gated = mixed.astype(f32) * (z * sig)
            square = square + gated * gated
            cross = cross + (normed_grad[rows, cols] * gain[:, cols]) * gated
            entry[rows, cols] = mixed_sum
            gated_all[rows, cols] = gated
            sig_all[rows, cols] = sig
            mixed_all[rows, cols] = mixed
        scale = lax.rsqrt(jnp.sum(square, axis=1, keepdims=True) * (1.0 / INNER) + EPS)
        pull = jnp.sum(cross, axis=1, keepdims=True) * (1.0 / INNER) * (scale * scale * scale)
        scale = jnp.broadcast_to(scale, (CHUNK, LANES))
        pull = jnp.broadcast_to(pull, (CHUNK, LANES))
        for cols in tiles(INNER):
            gated = gated_all[rows, cols]
            sig = sig_all[rows, cols]
            back = normed_grad[rows, cols]
            unit = gated * scale
            gated_low[rows, cols] = (unit * gain[:, cols]).astype(bf16)
            gated_grad = scale * (back * gain[:, cols]) - gated * pull
            act = gate[rows, cols] * sig
            slope = sig + act * (1.0 - sig)
            gate_grad[rows, cols] = (gated_grad * mixed_all[rows, cols].astype(f32) * slope).astype(bf16)
            low_grad = (gated_grad * act).astype(bf16)
            mixed_grad[rows, cols] = low_grad
            grad = low_grad.astype(f32)
            entry_low[rows, cols] = (grad * enter[rows, cols]).astype(bf16)
            high[rows, cols], low[rows, cols] = in_two(grad * entry[rows, cols])
            sums[0:8, cols] += eights(back * unit)
            sums[8:16, cols] += eights(grad * values[rows, cols].astype(f32))

    chunks(STRETCH, CHUNK, rows_step)
    row_sums[...] = head_sums((high, low), heads)
    reads_grad[...] = mm(entry_low[...], full[...], NT)
    after_local[0] = state_grad[...].astype(bf16)
    after_decay[0] = tail_decay[...]
    state_grad[...] = state_grad[...] * factors[0, 0:1, :] + mm(reads, entry_low[...], TN)
    tail_decay[...] = tail_decay[...] * factors[0, 0:1, :]

    @pl.when(i == pl.num_programs(0) - 1)
    def _():
        for j, cols in enumerate(tiles(INNER)):
            start_grad[j] = state_grad[:, cols].astype(bf16)


def late(
    values, both, cumul, delta, raw, masks, bias, rate, factors, start, prior, after_local, after_decay, after,
    diag_sums, scaled, out_grad, row_sums, reads_grad, both_grad, skip, heads, spreader,
    conv_grad, sums,
    after_low, spread_grad, factor, wide, weighted, joint, outer_low, high, low,
):
    @pl.when(pl.program_id(0) == 0)
    def _():
        sums[...] = jnp.zeros_like(sums)

    carry_rows = []
    for j, cols in enumerate(tiles(INNER)):
        here = after_local[0, :, cols].astype(f32) + after_decay[0, 0:1, cols] * after[j].astype(f32)
        after_low[:, cols] = here.astype(bf16)
        carry_rows.append(eights(here * entered(start, factors, prior, j, cols)) * factors[0, 0:1, cols])
    carry_grad = sum(mm(part, heads[...]) for part in in_two(jnp.concatenate(carry_rows, axis=1)))
    spread_grad[...] = mm(both[:, :STATE], after_low[...])
    step = delta[...]
    total = cumul[...]
    end_factor = jnp.exp(total[STRETCH - 1 : STRETCH, :] - total) * masks[:, 3:4]
    factor[...] = spread_heads(end_factor, spreader[...])
    wide[...] = spread_heads(step, spreader[...])

    def rows_step(rows):
        for cols in tiles(INNER):
            v = values[rows, cols].astype(f32)
            ends = factor[rows, cols]
            step_wide = wide[rows, cols]
            inner = diag_sums[rows, cols]
            outer = spread_grad[rows, cols] * ends
            both_sums = inner + outer
            conv_grad[rows, cols] = (
                step_wide * both_sums + skip[:, cols] * out_grad[rows, cols].astype(f32)
            ).astype(bf16)
            weighted[rows, cols] = (v * (ends * step_wide)).astype(bf16)
            joint[rows, cols] = (v * both_sums).astype(bf16)
            outer_low[rows, cols] = (v * outer).astype(bf16)
            high[rows, cols], low[rows, cols] = in_two(scaled[rows, cols].astype(f32) * inner)

    chunks(STRETCH, CHUNK, rows_step)
    conv_grad[:, INNER : INNER + STATE] = (
        both_grad[:, :STATE] + mm(weighted[...], after_low[...], NT)
    ).astype(bf16)
    conv_grad[:, INNER + STATE : CONV_CHANNELS] = (both_grad[:, STATE:] + reads_grad[...]).astype(bf16)
    end_spread = head_sums((outer_low,), heads) * step
    last_grad = jnp.sum(end_spread, axis=0, keepdims=True) + jnp.sum(carry_grad, axis=0, keepdims=True)
    cumul_grad = row_sums[...] - head_sums((high, low), heads) - end_spread
    row = lax.broadcasted_iota(jnp.int32, (STRETCH, STRETCH), 0)
    col = lax.broadcasted_iota(jnp.int32, (STRETCH, STRETCH), 1)
    decay_grad = mm((row <= col).astype(f32), cumul_grad, precision=HIGHEST) + last_grad
    step_grad = head_sums((joint,), heads) + decay_grad * rate[...]
    pre_grad = step_grad * sigmoid(raw[...].astype(f32) + bias[...])
    conv_grad[:, CONV_CHANNELS:] = pre_grad.astype(bf16)
    sums[0:1, :] += jnp.sum(decay_grad * step, axis=0, keepdims=True)
    sums[1:2, :] += jnp.sum(pre_grad, axis=0, keepdims=True)


def conv_back(mixed, grad, masks, taps, out, rim, tail, tap_grads, held, same, kept):
    rows_all = grad.shape[0]
    spread_masks(masks, same)
    hold(mixed, held)
    kept[:, :, pl.ds(rows_all, 8), :] = jnp.zeros(kept.shape[:2] + (8, LANES), f32)

    def convolve(cols):
        tile = cols.start // LANES
        found = [jnp.zeros((8, LANES), f32) for _ in range(CONV_WIDTH + 1)]
        for rows in range(0, rows_all, PART):
            total, taken = conv_part(held, same, taps, rows, cols)
            sig = sigmoid(total)
            here = grad[rows : rows + PART, cols].astype(f32) * (sig * (1.0 + total * (1.0 - sig)))
            found[CONV_WIDTH] = found[CONV_WIDTH] + eights(here)
            for k in range(CONV_WIDTH):
                masked = here if k == 0 else here * same[k - 1, rows : rows + PART, :]
                kept[k, tile, pl.ds(rows, PART), :] = masked
                found[3 - k] = found[3 - k] + eights(masked * taken[k])
        lines = [jnp.sum(line, axis=0, keepdims=True) for line in found]
        tap_grads[:, cols] = jnp.concatenate(lines + [jnp.zeros((3, LANES), f32)], axis=0)
        for rows in range(0, rows_all, PART):
            value = taps[3:4, cols] * kept[0, tile, pl.ds(rows, PART), :]
            for k in range(1, CONV_WIDTH):
                value = value + taps[3 - k : 4 - k, cols] * kept[k, tile, pl.ds(rows + k, PART), :]
            out[rows : rows + PART, cols] = value.astype(bf16)
            if rows + PART == rows_all:
                tail[:, cols] = value[PART - HALO :, :]
        lines = [jnp.zeros((5, LANES), f32)]
        for m in (3, 2, 1):
            line = jnp.zeros((1, LANES), f32)
            for k in range(m, CONV_WIDTH):
                line = line + taps[3 - k : 4 - k, cols] * kept[k, tile, k - m : k - m + 1, :]
            lines.append(line)
        rim[:, cols] = jnp.concatenate(lines, axis=0)

    def other(cols):
        out[:, cols] = grad[:, cols]
        tail[:, cols] = grad[rows_all - HALO :, cols].astype(f32)
        rim[:, cols] = jnp.zeros((8, LANES), f32)
        tap_grads[:, cols] = jnp.zeros((8, LANES), f32)

    each_tile(convolve, other)


def per_device(
    block_input,
    out_cotangent,
    segment_ids,
    in_weight,
    out_weight,
    vector_params,
    in_first,
    in_second,
    out_first,
    out_second,
    vector_first,
    vector_second,
):
    count = lax.axis_size("seq") * lax.axis_size("head")
    device_index = lax.axis_index(EVERY)
    rows = block_input.shape[0]
    stretches = rows // STRETCH
    own_rows = in_weight.shape[0]
    halo = passed_along(block_input[rows - HALO :], EVERY, 1)

    head_index, seq_index = lax.axis_index("head"), lax.axis_index("seq")
    chips = lax.axis_size("seq") // 2
    mixer_own = jnp.pad(in_weight[:, INNER:].astype(bf16), ((0, 0), (0, LANES - HEADS)))
    mixer_group = laid(
        [(head_index, mixer_own)]
        + [(head_index ^ k, fetched(mixer_own, "head", k)) for k in range(1, lax.axis_size("head"))]
    )
    mixer_group, halo, block_now, segment_now, vector_now = lax.optimization_barrier(
        (mixer_group, halo, block_input, segment_ids, vector_params)
    )
    norm_gain, gated_gain, conv_taps, conv_bias, step_bias, log_rate, skip_gain = split_vector(vector_now)

    def unit_rows(block):
        wide = block.astype(f32)
        scale = lax.rsqrt(jnp.mean(wide * wide, axis=-1, keepdims=True) + EPS)
        return wide, scale

    inputs, in_scale = unit_rows(block_now)
    normed = (inputs * in_scale * norm_gain).astype(bf16)
    halo_wide, halo_scale = unit_rows(halo)
    extended = jnp.concatenate([normed, (halo_wide * halo_scale * norm_gain).astype(bf16)], axis=0)

    padded = jnp.concatenate(
        [jnp.full((3,), -1, jnp.int32), segment_now, jnp.full((3,), -1, jnp.int32)]
    )
    window = lax.dynamic_slice_in_dim(padded, device_index * rows, rows + 6)
    own = window[3 : 3 + rows]
    blocks = own.reshape(stretches, STRETCH)
    before = window[2 : 2 + rows].reshape(stretches, STRETCH)[:, :1]
    columns = [(window[3 - k : 3 - k + rows] == own) for k in (1, 2, 3)]
    columns.append((blocks == blocks[:, -1:]).reshape(rows))
    columns.append((blocks == before).reshape(rows))
    columns.append(own)
    columns += [jnp.zeros((rows,), f32)] * 2
    masks = jnp.stack([column.astype(f32) for column in columns], axis=1)
    marks = masks.shape[1]
    segments = blocks.astype(f32).reshape(stretches, 1, STRETCH)

    taps = jnp.concatenate([conv_taps, conv_bias[None], jnp.zeros((3, CONV_CHANNELS), f32)], axis=0)
    taps = jnp.pad(taps, ((0, 0), (0, LANES)))

    def head_row(vector):
        return jnp.pad(vector, (0, LANES - HEADS)).reshape(1, LANES)

    bias_row = head_row(step_bias)
    rate_row = head_row(-jnp.exp(log_rate))
    skip_row = jnp.repeat(skip_gain, HEAD_SIZE).reshape(1, INNER)
    gain_row = gated_gain.reshape(1, INNER)
    head_of = (
        lax.broadcasted_iota(jnp.int32, (INNER, LANES), 0) // HEAD_SIZE
        == lax.broadcasted_iota(jnp.int32, (INNER, LANES), 1)
    ).astype(bf16)
    spreader = jnp.concatenate([head_of.T, head_of.T], axis=0)

    near = [(0, mixer_group)] + [(2 * k, fetched(mixer_group, "seq", 2 * k)) for k in range(1, chips)]
    near, extended, normed, masks, taps, spreader, head_of = lax.optimization_barrier(
        ([piece for _, piece in near], extended, normed, masks, taps, spreader, head_of)
    )
    bits = [2 * k for k in range(chips)] + [2 * k + 1 for k in range(chips)]
    pieces = near + [fetched(piece, "seq", 1) for piece in near]
    rest_own = jnp.concatenate([in_weight[:, :WIDTH], in_weight[:, WIDTH:INNER], out_weight], axis=0).astype(bf16)
    rest_own, pieces = lax.optimization_barrier((rest_own, pieces))
    rest = lax.all_gather(rest_own, EVERY, axis=0, tiled=True).reshape(count, -1, WIDTH)
    gate_weight = jnp.concatenate(
        [rest[:, :own_rows].reshape(WIDTH, WIDTH), rest[:, own_rows : 2 * own_rows].reshape(WIDTH, WIDTH)], axis=1
    )
    out_full = rest[:, 2 * own_rows :].reshape(INNER, WIDTH)

    convolved, mixed_low, mixer_weight = call(
        functools.partial(conv_forward, bits),
        (MIXED // TILE,),
        [
            pl.BlockSpec(memory_space=pltpu.SMEM),
            whole(rows + HALO, WIDTH),
            whole(rows, marks),
            spec((8, TILE), lambda i: (0, i)),
        ]
        + [spec((pieces[0].shape[0], TILE), lambda i: (0, i))] * len(pieces),
        [
            spec((rows, TILE), lambda i: (0, i)),
            spec((rows + HALO, TILE), lambda i: (0, i)),
            spec((WIDTH, TILE), lambda i: (0, i)),
        ],
        [((rows, MIXED), bf16), ((rows + HALO, MIXED), bf16), ((WIDTH, MIXED), bf16)],
        [
            pltpu.VMEM((TILE // LANES, rows + HALO, LANES), f32),
            pltpu.VMEM((3, rows, LANES), f32),
            pltpu.VMEM((WIDTH, TILE), f32),
        ],
        14,
    )(seq_index.reshape(1), extended, masks, taps, *pieces)

    by_block = lambda *tail: spec((STRETCH,) + tail, lambda c: (c,) + (0,) * len(tail))
    both_spec = spec((STRETCH, 2 * STATE), lambda c: (c, INNER // (2 * STATE)))
    values_spec = spec((STRETCH, INNER), lambda c: (c, 0))
    raw_spec = spec((STRETCH, LANES), lambda c: (c, CONV_CHANNELS // LANES))
    per_block = lambda *tail: spec((1,) + tail, lambda c: (c,) + (0,) * len(tail))

    scaled, cumul, delta, cumul_rows, start, factors, device_state, device_decay = call(
        local_states,
        (stretches,),
        [values_spec, both_spec, raw_spec, by_block(marks), whole(1, LANES), whole(1, LANES), whole(2 * LANES, INNER)],
        [
            by_block(INNER),
            by_block(LANES),
            by_block(LANES),
            per_block(32, STRETCH),
            per_block(STATE, INNER),
            per_block(8, INNER),
            whole(PAIRS, STATE, LANES),
            whole(8, LANES),
        ],
        [
            ((rows, INNER), bf16),
            ((rows, LANES), f32),
            ((rows, LANES), f32),
            ((stretches, 32, STRETCH), f32),
            ((stretches, STATE, INNER), bf16),
            ((stretches, 8, INNER), f32),
            ((PAIRS, STATE, LANES), bf16),
            ((8, LANES), f32),
        ],
        [
            pltpu.VMEM((STATE, INNER), f32),
            pltpu.VMEM((8, LANES), f32),
            pltpu.VMEM((STRETCH, INNER), bf16),
            pltpu.VMEM((STRETCH, INNER), f32),
            pltpu.VMEM((STRETCH, INNER), f32),
        ],
        9,
    )(convolved, convolved, convolved, masks, bias_row, rate_row, spreader)

    share = PAIRS * STATE // count
    decay_high = device_decay[0].astype(bf16)
    decay_low = (device_decay[0] - decay_high.astype(f32)).astype(bf16)
    decay_rows = jnp.broadcast_to(jnp.stack([decay_high, decay_low])[None], (count, 2, LANES))
    sent = jnp.concatenate([device_state.reshape(count, share, LANES), decay_rows], axis=1)

    def exchange(value):
        return lax.all_to_all(value, EVERY, split_axis=0, concat_axis=0, tiled=True)

    def scan_parts(parts, reverse):
        return pl.pallas_call(
            functools.partial(prefix, reverse=reverse),
            out_shape=jax.ShapeDtypeStruct((count, share, LANES), bf16),
            compiler_params=pltpu.CompilerParams(vmem_limit_bytes=ROOM),
        )(parts, pair_decays, second)

    arrived = exchange(sent)
    all_decays = arrived[:, share, :HEADS].astype(f32) + arrived[:, share + 1, :HEADS].astype(f32)
    wide_decays = jnp.repeat(all_decays, HEAD_SIZE, axis=1).reshape(count, PAIRS, LANES)
    wide_decays = jnp.pad(wide_decays, ((0, 0), (0, 1), (0, 0)))
    first_pair = device_index * share // STATE
    pair_decays = lax.dynamic_slice_in_dim(wide_decays, first_pair, 2, axis=1)
    places = device_index * share + lax.broadcasted_iota(jnp.int32, (share, LANES), 0)
    second = (places >= (first_pair + 1) * STATE).astype(f32)
    prior = exchange(scan_parts(arrived, False)).reshape(PAIRS, STATE, LANES)

    diag = call(
        diagonal,
        (stretches,),
        [
            by_block(INNER),
            both_spec,
            by_block(LANES),
            per_block(32, STRETCH),
            by_block(marks),
            per_block(1, STRETCH),
        ],
        [by_block(INNER)],
        [((rows, INNER), f32)],
        [pltpu.VMEM((HEADS, STRETCH, LANES), f32), pltpu.VMEM((STRETCH, STRETCH), f32)],
        16,
    )(scaled, convolved, cumul, cumul_rows, masks, segments)[0]
    gate = jnp.dot(normed, gate_weight, preferred_element_type=f32)
    normed_grad = mm(out_cotangent, out_full, NT)

    back = stretches - 1
    by_block_r = lambda *tail: spec((STRETCH,) + tail, lambda c: (back - c,) + (0,) * len(tail))
    per_block_r = lambda *tail: spec((1,) + tail, lambda c: (back - c,) + (0,) * len(tail))
    wide_scratch = lambda kind: pltpu.VMEM((STRETCH, INNER), kind)
    (
        gated_low,
        gate_grad,
        mixed_grad,
        row_sums,
        reads_grad,
        after_local,
        middle_sums,
        start_grad,
        after_decay,
    ) = call(
        middle,
        (stretches,),
        [
            by_block_r(INNER),
            spec((STRETCH, INNER), lambda c: (back - c, 0)),
            spec((STRETCH, 2 * STATE), lambda c: (back - c, INNER // (2 * STATE))),
            by_block_r(LANES),
            by_block_r(marks),
            per_block_r(STATE, INNER),
            per_block_r(8, INNER),
            whole(PAIRS, STATE, LANES),
            by_block_r(INNER),
            by_block_r(INNER),
            whole(1, INNER),
            whole(1, INNER),
            whole(INNER, LANES),
            whole(2 * LANES, INNER),
        ],
        [
            by_block_r(INNER),
            by_block_r(INNER),
            by_block_r(INNER),
            by_block_r(LANES),
            by_block_r(STATE),
            per_block_r(STATE, INNER),
            whole(16, INNER),
            whole(PAIRS, STATE, LANES),
            per_block_r(8, INNER),
        ],
        [
            ((rows, INNER), bf16),
            ((rows, INNER), bf16),
            ((rows, INNER), bf16),
            ((rows, LANES), f32),
            ((rows, STATE), f32),
            ((stretches, STATE, INNER), bf16),
            ((16, INNER), f32),
            ((PAIRS, STATE, LANES), bf16),
            ((stretches, 8, INNER), f32),
        ],
        [
            pltpu.VMEM((STATE, INNER), bf16),
            wide_scratch(f32),
            wide_scratch(f32),
            wide_scratch(f32),
            wide_scratch(f32),
            wide_scratch(bf16),
            wide_scratch(bf16),
            wide_scratch(bf16),
            wide_scratch(bf16),
            pltpu.VMEM((STATE, INNER), f32),
            pltpu.VMEM((8, INNER), f32),
        ],
        24,
    )(
        diag, convolved, convolved, cumul, masks, start, factors, prior, gate, normed_grad,
        gain_row, skip_row, head_of, spreader,
    )

    sent_back = exchange(start_grad.reshape(count, share, LANES))
    diag_sums, both_grad = call(
        diagonal_back,
        (stretches,),
        [
            by_block(INNER),
            both_spec,
            by_block(LANES),
            per_block(32, STRETCH),
            by_block(marks),
            per_block(1, STRETCH),
            by_block(INNER),
        ],
        [by_block(INNER), by_block(2 * STATE)],
        [((rows, INNER), f32), ((rows, 2 * STATE), f32)],
        [
            pltpu.VMEM((HEADS, STRETCH, LANES), f32),
            pltpu.VMEM((STRETCH, STRETCH), f32),
            pltpu.VMEM((STRETCH, STRETCH), f32),
        ],
        20,
    )(scaled, convolved, cumul, cumul_rows, masks, segments, mixed_grad)
    sent_back, diag_sums, both_grad = lax.optimization_barrier((sent_back, diag_sums, both_grad))
    scanned = scan_parts(sent_back, True)
    gated_low, gate_grad, scanned = lax.optimization_barrier((gated_low, gate_grad, scanned))
    after = exchange(scanned)
    block_output = (inputs + mm(gated_low, out_full)).astype(bf16)

    gate_term = mm(normed, gate_grad, TN).astype(bf16)
    out_term = mm(gated_low, out_cotangent, TN).astype(bf16)
    rest_term = jnp.concatenate(
        [
            gate_term[:, :WIDTH].reshape(count, -1, WIDTH),
            gate_term[:, WIDTH:].reshape(count, -1, WIDTH),
            out_term.reshape(count, -1, WIDTH),
        ],
        axis=1,
    ).reshape(-1, WIDTH)
    rest_term, block_output, after = lax.optimization_barrier((rest_term, block_output, after))
    after = after.reshape(PAIRS, STATE, LANES)
    rest_line = lax.psum_scatter(rest_term, "seq", scatter_dimension=0, tiled=True)

    conv_out_grad, late_sums = call(
        late,
        (stretches,),
        [
            values_spec,
            both_spec,
            by_block(LANES),
            by_block(LANES),
            raw_spec,
            by_block(marks),
            whole(1, LANES),
            whole(1, LANES),
            per_block(8, INNER),
            per_block(STATE, INNER),
            whole(PAIRS, STATE, LANES),
            per_block(STATE, INNER),
            per_block(8, INNER),
            whole(PAIRS, STATE, LANES),
            by_block(INNER),
            by_block(INNER),
            by_block(INNER),
            by_block(LANES),
            by_block(STATE),
            by_block(2 * STATE),
            whole(1, INNER),
            whole(INNER, LANES),
            whole(2 * LANES, INNER),
        ],
        [by_block(MIXED), whole(8, LANES)],
        [((rows, MIXED), bf16), ((8, LANES), f32)],
        [
            pltpu.VMEM((STATE, INNER), bf16),
            wide_scratch(f32),
            wide_scratch(f32),
            wide_scratch(f32),
        ]
        + [wide_scratch(bf16)] * 5,
        18,
    )(
        convolved, convolved, cumul, delta, convolved, masks, bias_row, rate_row, factors, start, prior, after_local, after_decay,
        after, diag_sums, scaled, mixed_grad, row_sums, reads_grad, both_grad, skip_row, head_of, spreader,
    )

    mixed_in_grad, rim, tail, tap_grads = call(
        conv_back,
        (MIXED // TILE,),
        [
            spec((rows + HALO, TILE), lambda i: (0, i)),
            spec((rows, TILE), lambda i: (0, i)),
            whole(rows, marks),
            spec((8, TILE), lambda i: (0, i)),
        ],
        [
            spec((rows, TILE), lambda i: (0, i)),
            spec((8, TILE), lambda i: (0, i)),
            spec((HALO, TILE), lambda i: (0, i)),
            spec((8, TILE), lambda i: (0, i)),
        ],
        [
            ((rows, MIXED), bf16),
            ((8, MIXED), f32),
            ((HALO, MIXED), f32),
            ((8, MIXED), f32),
        ],
        [
            pltpu.VMEM((TILE // LANES, rows + HALO, LANES), f32),
            pltpu.VMEM((3, rows, LANES), f32),
            pltpu.VMEM((CONV_WIDTH, TILE // LANES, rows + 8, LANES), f32),
        ],
        20,
    )(mixed_low, conv_out_grad, masks, taps)

    from_next = passed_along(rim, EVERY, -1)
    gate_grad, rim = lax.optimization_barrier((gate_grad, rim))
    gate_part = mm(gate_grad, gate_weight, NT)
    from_next, gate_part = lax.optimization_barrier((from_next, gate_part))
    fixed = jnp.concatenate([tail[: HALO - 8], tail[HALO - 8 :] + from_next], axis=0).astype(bf16)
    mixer_grad = lax.dynamic_update_slice(mixed_in_grad, fixed, (rows - HALO, 0))
    mixer_grad, rest_line = lax.optimization_barrier((mixer_grad, rest_line))
    rest_grad = lax.psum_scatter(rest_line, "head", scatter_dimension=0, tiled=True)
    rest_grad = lax.optimization_barrier(rest_grad).astype(f32)
    gate_weight_grad = jnp.concatenate([rest_grad[:own_rows], rest_grad[own_rows : 2 * own_rows]], axis=1)
    out_grad = rest_grad[2 * own_rows :]

    term = mm(normed, mixer_grad, TN).astype(bf16)
    line_rows = own_rows * lax.axis_size("head")

    def block_of(value, place, size):
        return lax.dynamic_slice_in_dim(value, place * size, size, axis=0)

    summed = []
    for k in range(chips):
        given = block_of(term, seq_index ^ (2 * k) ^ 1, line_rows)
        kept = block_of(term, seq_index ^ (2 * k), line_rows)
        summed.append(kept.astype(f32) + fetched(given, "seq", 1).astype(f32))
    sending = [part.astype(bf16) for part in summed[1:]]
    sending, mixer_grad = lax.optimization_barrier((sending, mixer_grad))
    line = summed[0]
    for k, part in enumerate(sending, 1):
        line = line + fetched(part, "seq", 2 * k).astype(f32)
    normed_in_grad = gate_part + mm(mixer_grad, mixer_weight, NT)
    norm_gain_grad = jnp.sum(normed_in_grad * inputs * in_scale, axis=0)
    scaled_in = normed_in_grad * norm_gain
    input_grad = (
        out_cotangent.astype(f32)
        + in_scale * scaled_in
        - inputs * in_scale**3 * jnp.mean(scaled_in * inputs, axis=-1, keepdims=True)
    )

    vector_local = jnp.concatenate(
        [
            norm_gain_grad,
            jnp.sum(middle_sums[:8], axis=0),
            tap_grads[: CONV_WIDTH + 1, :CONV_CHANNELS].reshape(-1),
            late_sums[1, :HEADS],
            late_sums[0, :HEADS] * rate_row[0, :HEADS],
            jnp.sum(middle_sums[8:].reshape(8, HEADS, HEAD_SIZE), axis=(0, 2)),
            jnp.zeros((-vector_params.shape[0] % count,), f32),
        ]
    )
    line, vector_local = lax.optimization_barrier((line, vector_local))
    parts = exchange(vector_local.reshape(count, -1))
    total = jnp.broadcast_to(jnp.sum(parts, axis=0, keepdims=True), parts.shape)
    vector_grad = exchange(total).reshape(-1)[: vector_params.shape[0]]
    mixer_weight_grad = block_of(line, head_index, own_rows)
    for k in range(1, lax.axis_size("head")):
        given = block_of(line, head_index ^ k, own_rows).astype(bf16)
        mixer_weight_grad = mixer_weight_grad + fetched(given, "head", k).astype(f32)

    in_grad = jnp.concatenate([gate_weight_grad, mixer_weight_grad[:, : CONV_CHANNELS + HEADS]], axis=1)
    in_first_new, in_second_new, in_weight_new = adamw(
        in_weight, in_first, in_second, in_grad, RATE_MATRIX, WEIGHT_DECAY
    )
    out_first_new, out_second_new, out_weight_new = adamw(
        out_weight, out_first, out_second, out_grad, RATE_MATRIX, WEIGHT_DECAY
    )
    vector_first_new, vector_second_new, vector_new = adamw(
        vector_params, vector_first, vector_second, vector_grad, RATE_VECTOR, 0.0
    )
    return (
        block_output,
        input_grad.astype(bf16),
        in_first_new,
        in_second_new,
        in_weight_new,
        out_first_new,
        out_second_new,
        out_weight_new,
        vector_first_new,
        vector_second_new,
        vector_new,
    )


def solution(mesh):
    split = P(EVERY, None)
    in_specs = (split, split, P(), split, split, P(), split, split, split, split, P(), P())
    out_specs = (split,) * 8 + (P(),) * 3
    return jax.shard_map(
        per_device, mesh=mesh, in_specs=in_specs, out_specs=out_specs, check_vma=False
    )
```

```python
import functools

import jax
import jax.numpy as jnp
from jax import lax
from jax.experimental import pallas as pl
from jax.experimental.pallas import tpu as pltpu
from jax.sharding import PartitionSpec as P

WIDTH = 768
INNER = 1536
HEADS = 24
HEAD_SIZE = 64
STATE = 128
CONV_WIDTH = 4
STRETCH = 256
STEP = 10
CONV_CHANNELS = 1792
LANES = 128
PAIRS = HEADS // 2
MIXED = CONV_CHANNELS + LANES
HALO = 16
CHUNK = 32
PART = 64
LOG2E = 1.4426950408889634
HALF = STRETCH // 2
TILE = 384

EPS = 1e-05
BETA_ONE = 0.9
BETA_TWO = 0.95
ADAM_EPS = 1e-08
WEIGHT_DECAY = 0.1
RATE_MATRIX = 0.05
RATE_VECTOR = 0.3
HIGHEST = lax.Precision.HIGHEST
f32 = jnp.float32
bf16 = jnp.bfloat16
EVERY = ("seq", "head")
ROOM = 56 * 1024 * 1024


def passed_along(value, axis, steps):
    count = lax.axis_size(axis)
    leading, last = (max(0, -steps), min(count, count - steps))
    return lax.ppermute(value, axis, [(source, source + steps) for source in range(leading, last)])


def fetched(value, axis, bit):
    return lax.ppermute(value, axis, [(k, k ^ bit) for k in range(lax.axis_size(axis))])


def laid(pieces):
    rows, width = pieces[0][1].shape
    whole_array = jnp.zeros((rows * len(pieces), width), pieces[0][1].dtype)
    for place, piece in pieces:
        whole_array = lax.dynamic_update_slice(whole_array, piece, (place * rows, 0))
    return whole_array


def split_vector(vector):
    cursor = 0
    pieces = []
    for length in (WIDTH, INNER, CONV_WIDTH * CONV_CHANNELS, CONV_CHANNELS, HEADS, HEADS, HEADS):
        pieces.append(vector[cursor : cursor + length])
        cursor = cursor + length
    norm_gain, gated_gain, conv_flat, conv_bias, step_bias, log_rate, skip_gain = pieces
    return (
        norm_gain,
        gated_gain,
        conv_flat.reshape(CONV_WIDTH, CONV_CHANNELS),
        conv_bias,
        step_bias,
        log_rate,
        skip_gain,
    )


def adamw(weight, first, second, grad, rate, decay):
    first_new = BETA_ONE * first + (1.0 - BETA_ONE) * grad
    second_new = BETA_TWO * second + (1.0 - BETA_TWO) * grad * grad
    corrected_first = first_new / (1.0 - BETA_ONE**STEP)
    corrected_second = second_new / (1.0 - BETA_TWO**STEP)
    weight_new = weight - rate * (
        corrected_first / (jnp.sqrt(corrected_second) + ADAM_EPS) + decay * weight
    )
    return (first_new, second_new, weight_new)


def mm(left, right, dims=((1,), (0,)), precision=None):
    return lax.dot_general(left, right, (dims, ((), ())), preferred_element_type=f32, precision=precision)


NT = ((1,), (1,))
TN = ((0,), (0,))


def spec(block, index):
    return pl.BlockSpec(block, index)


def whole(*shape):
    return pl.BlockSpec(shape, lambda *ids: (0,) * len(shape))


def call(body, grid, ins, outs, out_shapes, scratch, micros):
    return pl.pallas_call(
        body,
        grid=grid,
        in_specs=ins,
        out_specs=outs,
        out_shape=[jax.ShapeDtypeStruct(shape, kind) for shape, kind in out_shapes],
        scratch_shapes=scratch,
        compiler_params=pltpu.CompilerParams(vmem_limit_bytes=ROOM),
        cost_estimate=pl.CostEstimate(flops=0, bytes_accessed=int(micros * 3.4e6), transcendentals=0),
    )


def in_two(value):
    top = value.astype(bf16)
    return top, (value - top.astype(f32)).astype(bf16)


def spread_heads(per_head, spreader):
    return mm(jnp.concatenate(in_two(per_head), axis=1), spreader)


def eights(value):
    return jnp.sum(value.reshape(value.shape[0] // 8, 8, value.shape[1]), axis=0)


def tiles(width):
    return [slice(j * LANES, (j + 1) * LANES) for j in range(width // LANES)]


def chunks(count, size, body):
    def step(i, _):
        body(pl.ds(pl.multiple_of(i * size, size), size))
        return 0

    lax.fori_loop(0, count // size, step, 0, unroll=2)


def sigmoid(v):
    return 0.5 * jnp.tanh(0.5 * v) + 0.5


def softplus(v):
    small = jnp.exp(-jnp.abs(v))
    series = small * (1.0 - small * (0.5 - small * (1.0 / 3.0 - small * 0.25)))
    return jnp.maximum(v, 0.0) + jnp.where(small < 0.01, series, jnp.log(1.0 + small))


def spread_masks(masks, same):
    @pl.when(pl.program_id(0) == 0)
    def _():
        for k in range(1, CONV_WIDTH):
            same[k - 1] = jnp.broadcast_to(masks[:, k - 1 : k], same.shape[1:])


def hold(mixed, held):
    count = mixed.shape[0] - HALO
    for j, cols in enumerate(tiles(TILE)):
        held[j, :HALO, :] = mixed[count:, cols].astype(f32)
        held[j, HALO:, :] = mixed[:count, cols].astype(f32)


def conv_part(held, same, taps, rows, cols):
    taken = [held[cols.start // LANES, pl.ds(HALO + rows - k, PART), :] for k in range(CONV_WIDTH)]
    total = taps[CONV_WIDTH : CONV_WIDTH + 1, cols] + taps[3:4, cols] * taken[0]
    for k in range(1, CONV_WIDTH):
        total = total + taps[3 - k : 4 - k, cols] * (taken[k] * same[k - 1, rows : rows + PART, :])
    return total, taken


def each_tile(convolve, other):
    for cols in tiles(TILE)[:-1]:
        convolve(cols)
    ending = pl.program_id(0) == pl.num_programs(0) - 1
    cols = tiles(TILE)[-1]
    pl.when(jnp.logical_not(ending))(lambda: convolve(cols))
    pl.when(ending)(lambda: other(cols))


def conv_forward(bits, where, normed, masks, taps, *others):
    pieces, (out, mixed, weight_out, held, same, weight) = others[: len(bits)], others[len(bits) :]
    count = out.shape[0]
    spread_masks(masks, same)
    size = pieces[0].shape[0]
    for bit, piece in zip(bits, pieces):
        start = pl.multiple_of((where[0] ^ bit) * size, 8)
        weight[pl.ds(start, size), :] = piece[...].astype(f32)
    weight_out[...] = weight[...].astype(bf16)
    low = mm(normed[...], weight_out[...]).astype(bf16)
    mixed[...] = low
    hold(low, held)

    def convolve(cols):
        for rows in range(0, count, PART):
            total, _ = conv_part(held, same, taps, rows, cols)
            out[rows : rows + PART, cols] = (total * sigmoid(total)).astype(bf16)

    def other(cols):
        out[:, cols] = mixed[:count, cols]

    each_tile(convolve, other)


def local_states(
    values, both, raw, masks, bias, rate, spreader,
    scaled, cumul_out, delta_out, cumul_rows, start, factors, device_state, device_decay,
    state, reach, weighted, spreads,
):
    c = pl.program_id(0)

    @pl.when(c == 0)
    def _():
        state[...] = jnp.zeros_like(state)
        reach[...] = jnp.ones_like(reach)

    delta = softplus(raw[...].astype(f32) + bias[...])
    cumul = sums_until(delta * rate[...], False)
    last = cumul[STRETCH - 1 : STRETCH, :]
    carry = jnp.exp(last) * masks[STRETCH - 1 : STRETCH, 4:5]
    cumul_out[...] = cumul
    delta_out[...] = delta
    cumul_rows[0] = cumul.T[: cumul_rows.shape[1], :] * LOG2E
    end_weight = jnp.exp(last - cumul) * masks[:, 3:4] * delta
    line = lax.broadcasted_iota(jnp.int32, (8, LANES), 0)
    factor_rows = jnp.where(line == 0, carry, reach[...])
    spreads[...] = spread_heads(
        jnp.concatenate([delta, end_weight, factor_rows, factor_rows], axis=0), spreader[...]
    )
    for cols in tiles(INNER):
        v = values[:, cols].astype(f32)
        scaled[:, cols] = (v * spreads[:STRETCH, cols]).astype(bf16)
        weighted[:, cols] = (v * spreads[STRETCH : 2 * STRETCH, cols]).astype(bf16)
    start[0] = state[...].astype(bf16)
    wide = spreads[2 * STRETCH : 2 * STRETCH + 8, :]
    factors[0] = wide
    state[...] = state[...] * wide[0:1, :] + mm(both[:, :STATE], weighted[...], TN)
    reach[...] = reach[...] * carry

    @pl.when(c == pl.num_programs(0) - 1)
    def _():
        for j, cols in enumerate(tiles(INNER)):
            device_state[j] = state[:, cols].astype(bf16)
        top, low = in_two(reach[...])
        device_decay[...] = jnp.concatenate([top[:1], low[:1], jnp.zeros((14, LANES), bf16)], axis=0)


def spread_columns(cumul, columns):
    for h in range(HEADS):
        columns[h] = jnp.broadcast_to(cumul[:, h : h + 1] * LOG2E, (STRETCH, LANES))


def diagonal(scaled, both, cumul, cumul_rows, masks, segments, out, columns, scores):
    spread_columns(cumul, columns)
    row = lax.broadcasted_iota(jnp.int32, (STRETCH, STRETCH), 0)
    col = lax.broadcasted_iota(jnp.int32, (STRETCH, STRETCH), 1)
    inside = (row >= col) & (masks[:, 5:6] == segments[0])
    scores[...] = jnp.where(inside, mm(both[:, STATE:], both[:, :STATE], NT), 0.0)
    low = lax.broadcasted_iota(jnp.int32, (HALF, LANES), 1) < HEAD_SIZE

    def pair(j, _):
        cols = pl.ds(pl.multiple_of(j * LANES, LANES), LANES)
        v = scaled[:, cols]
        tops, bottoms = [], []
        for q in range(2):
            h = 2 * j + q
            line = cumul_rows[0, pl.ds(h, 1), :]
            upper = columns[h, :HALF, :]
            lower = columns[h, HALF:, :]
            top = jnp.exp2(jnp.minimum(upper - line[:, :HALF], 0.0)) * scores[:HALF, :HALF]
            left = jnp.exp2(jnp.minimum(lower - line[:, :HALF], 0.0)) * scores[HALF:, :HALF]
            right = jnp.exp2(jnp.minimum(lower - line[:, HALF:], 0.0)) * scores[HALF:, HALF:]
            tops.append(mm(top.astype(bf16), v[:HALF]))
            bottoms.append(mm(jnp.concatenate([left.astype(bf16), right.astype(bf16)], axis=1), v))
        out[:HALF, cols] = jnp.where(low, *tops)
        out[HALF:, cols] = jnp.where(low, *bottoms)
        return 0

    lax.fori_loop(0, PAIRS, pair, 0, unroll=2)


def diagonal_back(
    scaled, both, cumul, cumul_rows, masks, segments, out_grad, sums, both_grad, columns, scores, total
):
    spread_columns(cumul, columns)
    row = lax.broadcasted_iota(jnp.int32, (STRETCH, STRETCH), 0)
    col = lax.broadcasted_iota(jnp.int32, (STRETCH, STRETCH), 1)
    inside = (row <= col) & (masks[:, 5:6] == segments[0])
    scores[...] = jnp.where(inside, mm(both[:, :STATE], both[:, STATE:], NT), 0.0)
    total[...] = jnp.zeros_like(total)
    low = lax.broadcasted_iota(jnp.int32, (HALF, LANES), 1) < HEAD_SIZE
    first = lax.broadcasted_iota(jnp.int32, (STRETCH, LANES), 1) < HEAD_SIZE

    def pair(j, _):
        cols = pl.ds(pl.multiple_of(j * LANES, LANES), LANES)
        v = scaled[:, cols]
        g = out_grad[:, cols]
        tops, bottoms = [], []
        for q in range(2):
            h = 2 * j + q
            line = cumul_rows[0, pl.ds(h, 1), :]
            upper = columns[h, :HALF, :]
            lower = columns[h, HALF:, :]
            own = jnp.where(first == (q == 0), g.astype(f32), 0.0).astype(bf16)
            left = jnp.exp2(jnp.minimum(line[:, :HALF] - upper, 0.0))
            right = jnp.exp2(jnp.minimum(line[:, HALF:] - upper, 0.0))
            corner = jnp.exp2(jnp.minimum(line[:, HALF:] - lower, 0.0))
            tops.append(
                mm(
                    jnp.concatenate(
                        [(left * scores[:HALF, :HALF]).astype(bf16), (right * scores[:HALF, HALF:]).astype(bf16)],
                        axis=1,
                    ),
                    g,
                )
            )
            bottoms.append(mm((corner * scores[HALF:, HALF:]).astype(bf16), g[HALF:]))
            top_grad = mm(v[:HALF], own, NT)
            total[:HALF, :HALF] += left * top_grad[:, :HALF]
            total[:HALF, HALF:] += right * top_grad[:, HALF:]
            total[HALF:, HALF:] += corner * mm(v[HALF:], own[HALF:], NT)
        sums[:HALF, cols] = jnp.where(low, *tops)
        sums[HALF:, cols] = jnp.where(low, *bottoms)
        return 0

    lax.fori_loop(0, PAIRS, pair, 0, unroll=2)
    scores_grad = jnp.where(inside, total[...], 0.0).astype(bf16)
    both_grad[:, :STATE] = mm(scores_grad, both[:, STATE:])
    both_grad[:, STATE:] = mm(scores_grad, both[:, :STATE], TN)


def prefix(where, parts, decays, out, wide, reverse):
    count = parts.shape[0]
    rows = out.shape[1]
    first = where[0] * rows // STATE
    head = 2 * first + lax.broadcasted_iota(jnp.int32, (LANES, 2 * LANES), 1) // HEAD_SIZE
    chosen = (lax.broadcasted_iota(jnp.int32, (LANES, 2 * LANES), 0) == head).astype(f32)
    wide[...] = mm(decays[...], chosen, precision=HIGHEST)
    places = where[0] * rows + lax.broadcasted_iota(jnp.int32, (rows, LANES), 0)
    second = places >= (first + 1) * STATE

    def step(i, state):
        k = count - 1 - i if reverse else i
        out[pl.ds(k, 1)] = state.astype(bf16)[None]
        two = wide[pl.ds(k, 1), :]
        decay = jnp.where(second, two[:, LANES:], two[:, :LANES])
        return decay * state + parts[pl.ds(k, 1), :rows, :][0].astype(f32)

    lax.fori_loop(0, count, step, jnp.zeros((rows, LANES), f32))


def sums_until(value, upper):
    row = lax.broadcasted_iota(jnp.int32, (STRETCH, STRETCH), 0)
    col = lax.broadcasted_iota(jnp.int32, (STRETCH, STRETCH), 1)
    triangle = ((row <= col) if upper else (row >= col)).astype(bf16)
    top = value.astype(bf16)
    rest = value - top.astype(f32)
    middle_part, low = in_two(rest)
    out = mm(triangle, jnp.concatenate([top, middle_part, low], axis=1))
    return out[:, :LANES] + out[:, LANES : 2 * LANES] + out[:, 2 * LANES :]


def entered(start, factors, prior, j, cols):
    return start[0, :, cols].astype(f32) + factors[0, 1:2, cols] * prior[j].astype(f32)


def middle(
    diag, values, both, cumul, masks, start, factors, prior, gate, normed_grad, gain, skip, heads,
    spreader,
    gated_low, gate_grad, mixed_grad, row_sums, reads_grad, after_local, sums, start_grad,
    after_decay, full, entry, enter, gated_all, sig_all, mixed_all, entry_low, products, state_grad, tail_decay,
):
    i = pl.program_id(0)

    @pl.when(i == 0)
    def _():
        state_grad[...] = jnp.zeros_like(state_grad)
        tail_decay[...] = jnp.ones_like(tail_decay)
        sums[...] = jnp.zeros_like(sums)

    reads = both[:, STATE:]
    for j, cols in enumerate(tiles(INNER)):
        full[:, cols] = entered(start, factors, prior, j, cols).astype(bf16)
    entry[...] = mm(reads, full[...])
    enter[...] = spread_heads(jnp.exp(cumul[...]) * masks[:, 4:5], spreader[...])

    def rows_step(rows):
        square = jnp.zeros((CHUNK, LANES), f32)
        cross = jnp.zeros((CHUNK, LANES), f32)
        for cols in tiles(INNER):
            mixed_sum = diag[rows, cols] + entry[rows, cols] * enter[rows, cols]
            mixed = (mixed_sum + skip[:, cols] * values[rows, cols].astype(f32)).astype(bf16)
            z = gate[rows, cols]
            sig = sigmoid(z)
            gated = mixed.astype(f32) * (z * sig)
            square = square + gated * gated
            cross = cross + (normed_grad[rows, cols] * gain[:, cols]) * gated
            entry[rows, cols] = mixed_sum
            gated_all[rows, cols] = gated
            sig_all[rows, cols] = sig
            mixed_all[rows, cols] = mixed
        scale = lax.rsqrt(jnp.sum(square, axis=1, keepdims=True) * (1.0 / INNER) + EPS)
        pull = jnp.sum(cross, axis=1, keepdims=True) * (1.0 / INNER) * (scale * scale * scale)
        scale = jnp.broadcast_to(scale, (CHUNK, LANES))
        pull = jnp.broadcast_to(pull, (CHUNK, LANES))
        for cols in tiles(INNER):
            gated = gated_all[rows, cols]
            sig = sig_all[rows, cols]
            back = normed_grad[rows, cols]
            unit = gated * scale
            gated_low[rows, cols] = (unit * gain[:, cols]).astype(bf16)
            gated_grad = scale * (back * gain[:, cols]) - gated * pull
            act = gate[rows, cols] * sig
            slope = sig + act * (1.0 - sig)
            gate_grad[rows, cols] = (gated_grad * mixed_all[rows, cols].astype(f32) * slope).astype(bf16)
            low_grad = (gated_grad * act).astype(bf16)
            mixed_grad[rows, cols] = low_grad
            grad = low_grad.astype(f32)
            entry_low[rows, cols] = (grad * enter[rows, cols]).astype(bf16)
            products[0, rows, cols], products[1, rows, cols] = in_two(grad * entry[rows, cols])
            sums[0:8, cols] += eights(back * unit)
            sums[8:16, cols] += eights(grad * values[rows, cols].astype(f32))

    chunks(STRETCH, CHUNK, rows_step)
    summed = mm(products[...].reshape(2 * STRETCH, INNER), heads[...])
    row_sums[...] = summed[:STRETCH] + summed[STRETCH:]
    reads_grad[...] = mm(entry_low[...], full[...], NT)
    after_local[0] = state_grad[...].astype(bf16)
    after_decay[0] = tail_decay[...]
    state_grad[...] = state_grad[...] * factors[0, 0:1, :] + mm(reads, entry_low[...], TN)
    tail_decay[...] = tail_decay[...] * factors[0, 0:1, :]

    @pl.when(i == pl.num_programs(0) - 1)
    def _():
        for j, cols in enumerate(tiles(INNER)):
            start_grad[j] = state_grad[:, cols].astype(bf16)


def late(
    values, both, cumul, delta, raw, masks, bias, rate, factors, start, prior, after_local, after_decay, after,
    diag_sums, scaled, out_grad, row_sums, reads_grad, both_grad, skip, heads, spreader,
    conv_grad, sums,
    after_low, spread_grad, spreads, weighted, products,
):
    @pl.when(pl.program_id(0) == 0)
    def _():
        sums[...] = jnp.zeros_like(sums)

    carry_rows = []
    for j, cols in enumerate(tiles(INNER)):
        here = after_local[0, :, cols].astype(f32) + after_decay[0, 0:1, cols] * after[j].astype(f32)
        after_low[:, cols] = here.astype(bf16)
        carry_rows.append(eights(here * entered(start, factors, prior, j, cols)) * factors[0, 0:1, cols])
    top, low = in_two(jnp.concatenate(carry_rows, axis=1))
    products[4 * STRETCH :, :] = jnp.concatenate([top, low], axis=0)
    spread_grad[...] = mm(both[:, :STATE], after_low[...])
    step = delta[...]
    total = cumul[...]
    end_factor = jnp.exp(total[STRETCH - 1 : STRETCH, :] - total) * masks[:, 3:4]
    spreads[...] = spread_heads(jnp.concatenate([end_factor, step], axis=0), spreader[...])
    later = lambda rows, k: pl.ds(pl.multiple_of(rows.start + k * STRETCH, CHUNK), CHUNK)

    def rows_step(rows):
        for cols in tiles(INNER):
            v = values[rows, cols].astype(f32)
            ends = spreads[rows, cols]
            step_wide = spreads[later(rows, 1), cols]
            inner = diag_sums[rows, cols]
            outer = spread_grad[rows, cols] * ends
            both_sums = inner + outer
            conv_grad[rows, cols] = (
                step_wide * both_sums + skip[:, cols] * out_grad[rows, cols].astype(f32)
            ).astype(bf16)
            weighted[rows, cols] = (v * (ends * step_wide)).astype(bf16)
            products[rows, cols] = (v * both_sums).astype(bf16)
            products[later(rows, 1), cols] = (v * outer).astype(bf16)
            top, low = in_two(scaled[rows, cols].astype(f32) * inner)
            products[later(rows, 2), cols] = top
            products[later(rows, 3), cols] = low

    chunks(STRETCH, CHUNK, rows_step)
    conv_grad[:, INNER : INNER + STATE] = (
        both_grad[:, :STATE] + mm(weighted[...], after_low[...], NT)
    ).astype(bf16)
    conv_grad[:, INNER + STATE : CONV_CHANNELS] = (both_grad[:, STATE:] + reads_grad[...]).astype(bf16)
    summed = mm(products[...], heads[...])
    joint, outer_sum, top, low = [summed[k * STRETCH : (k + 1) * STRETCH] for k in range(4)]
    end_spread = outer_sum * step
    last_grad = jnp.sum(end_spread, axis=0, keepdims=True) + jnp.sum(summed[4 * STRETCH :], axis=0, keepdims=True)
    cumul_grad = row_sums[...] - (top + low) - end_spread
    decay_grad = sums_until(cumul_grad, True) + last_grad
    step_grad = joint + decay_grad * rate[...]
    pre_grad = step_grad * sigmoid(raw[...].astype(f32) + bias[...])
    conv_grad[:, CONV_CHANNELS:] = pre_grad.astype(bf16)
    sums[0:1, :] += jnp.sum(decay_grad * step, axis=0, keepdims=True)
    sums[1:2, :] += jnp.sum(pre_grad, axis=0, keepdims=True)


def conv_back(mixed, grad, masks, taps, out, rim, tail, tap_grads, held, same, kept):
    rows_all = grad.shape[0]
    spread_masks(masks, same)
    hold(mixed, held)
    kept[:, :, pl.ds(rows_all, 8), :] = jnp.zeros(kept.shape[:2] + (8, LANES), f32)

    def convolve(cols):
        tile = cols.start // LANES
        found = [jnp.zeros((8, LANES), f32) for _ in range(CONV_WIDTH + 1)]
        for rows in range(0, rows_all, PART):
            total, taken = conv_part(held, same, taps, rows, cols)
            sig = sigmoid(total)
            here = grad[rows : rows + PART, cols].astype(f32) * (sig * (1.0 + total * (1.0 - sig)))
            found[CONV_WIDTH] = found[CONV_WIDTH] + eights(here)
            for k in range(CONV_WIDTH):
                masked = here if k == 0 else here * same[k - 1, rows : rows + PART, :]
                kept[k, tile, pl.ds(rows, PART), :] = masked
                found[3 - k] = found[3 - k] + eights(masked * taken[k])
        lines = [jnp.sum(line, axis=0, keepdims=True) for line in found]
        tap_grads[:, cols] = jnp.concatenate(lines + [jnp.zeros((3, LANES), f32)], axis=0)
        for rows in range(0, rows_all, PART):
            value = taps[3:4, cols] * kept[0, tile, pl.ds(rows, PART), :]
            for k in range(1, CONV_WIDTH):
                value = value + taps[3 - k : 4 - k, cols] * kept[k, tile, pl.ds(rows + k, PART), :]
            out[rows : rows + PART, cols] = value.astype(bf16)
            if rows + PART == rows_all:
                tail[:, cols] = value[PART - HALO :, :]
        lines = [jnp.zeros((5, LANES), f32)]
        for m in (3, 2, 1):
            line = jnp.zeros((1, LANES), f32)
            for k in range(m, CONV_WIDTH):
                line = line + taps[3 - k : 4 - k, cols] * kept[k, tile, k - m : k - m + 1, :]
            lines.append(line)
        rim[:, cols] = jnp.concatenate(lines, axis=0)

    def other(cols):
        out[:, cols] = grad[:, cols]
        tail[:, cols] = grad[rows_all - HALO :, cols].astype(f32)
        rim[:, cols] = jnp.zeros((8, LANES), f32)
        tap_grads[:, cols] = jnp.zeros((8, LANES), f32)

    each_tile(convolve, other)


def per_device(
    block_input,
    out_cotangent,
    segment_ids,
    in_weight,
    out_weight,
    vector_params,
    in_first,
    in_second,
    out_first,
    out_second,
    vector_first,
    vector_second,
):
    count = lax.axis_size("seq") * lax.axis_size("head")
    device_index = lax.axis_index(EVERY)
    rows = block_input.shape[0]
    stretches = rows // STRETCH
    own_rows = in_weight.shape[0]
    halo = passed_along(block_input[rows - HALO :], EVERY, 1)

    head_index, seq_index = lax.axis_index("head"), lax.axis_index("seq")
    chips = lax.axis_size("seq") // 2
    mixer_own = jnp.pad(in_weight[:, INNER:].astype(bf16), ((0, 0), (0, LANES - HEADS)))
    mixer_group = laid(
        [(head_index, mixer_own)]
        + [(head_index ^ k, fetched(mixer_own, "head", k)) for k in range(1, lax.axis_size("head"))]
    )
    mixer_group, halo, block_now, segment_now, vector_now = lax.optimization_barrier(
        (mixer_group, halo, block_input, segment_ids, vector_params)
    )
    norm_gain, gated_gain, conv_taps, conv_bias, step_bias, log_rate, skip_gain = split_vector(vector_now)

    def unit_rows(block):
        wide = block.astype(f32)
        scale = lax.rsqrt(jnp.mean(wide * wide, axis=-1, keepdims=True) + EPS)
        return wide, scale

    inputs, in_scale = unit_rows(block_now)
    normed = (inputs * in_scale * norm_gain).astype(bf16)
    halo_wide, halo_scale = unit_rows(halo)
    extended = jnp.concatenate([normed, (halo_wide * halo_scale * norm_gain).astype(bf16)], axis=0)

    padded = jnp.concatenate(
        [jnp.full((3,), -1, jnp.int32), segment_now, jnp.full((3,), -1, jnp.int32)]
    )
    window = lax.dynamic_slice_in_dim(padded, device_index * rows, rows + 6)
    own = window[3 : 3 + rows]
    blocks = own.reshape(stretches, STRETCH)
    before = window[2 : 2 + rows].reshape(stretches, STRETCH)[:, :1]
    columns = [(window[3 - k : 3 - k + rows] == own) for k in (1, 2, 3)]
    columns.append((blocks == blocks[:, -1:]).reshape(rows))
    columns.append((blocks == before).reshape(rows))
    columns.append(own)
    columns += [jnp.zeros((rows,), f32)] * 2
    masks = jnp.stack([column.astype(f32) for column in columns], axis=1)
    marks = masks.shape[1]
    segments = blocks.astype(f32).reshape(stretches, 1, STRETCH)

    taps = jnp.concatenate([conv_taps, conv_bias[None], jnp.zeros((3, CONV_CHANNELS), f32)], axis=0)
    taps = jnp.pad(taps, ((0, 0), (0, LANES)))

    def head_row(vector):
        return jnp.pad(vector, (0, LANES - HEADS)).reshape(1, LANES)

    bias_row = head_row(step_bias)
    rate_row = head_row(-jnp.exp(log_rate))
    skip_row = jnp.repeat(skip_gain, HEAD_SIZE).reshape(1, INNER)
    gain_row = gated_gain.reshape(1, INNER)
    head_of = (
        lax.broadcasted_iota(jnp.int32, (INNER, LANES), 0) // HEAD_SIZE
        == lax.broadcasted_iota(jnp.int32, (INNER, LANES), 1)
    ).astype(bf16)
    spreader = jnp.concatenate([head_of.T, head_of.T], axis=0)

    near = [(0, mixer_group)] + [(2 * k, fetched(mixer_group, "seq", 2 * k)) for k in range(1, chips)]
    near, extended, normed, masks, taps, spreader, head_of = lax.optimization_barrier(
        ([piece for _, piece in near], extended, normed, masks, taps, spreader, head_of)
    )
    rest_own = jnp.concatenate([in_weight[:, :WIDTH], in_weight[:, WIDTH:INNER], out_weight], axis=0).astype(bf16)
    rest_own, _ = lax.optimization_barrier((rest_own, mixer_group))
    bits = [2 * k for k in range(chips)] + [2 * k + 1 for k in range(chips)]
    pieces = near + [fetched(piece, "seq", 1) for piece in near]
    rest = lax.all_gather(rest_own, EVERY, axis=0, tiled=True).reshape(count, -1, WIDTH)
    gate_weight = jnp.concatenate(
        [rest[:, :own_rows].reshape(WIDTH, WIDTH), rest[:, own_rows : 2 * own_rows].reshape(WIDTH, WIDTH)], axis=1
    )
    out_full = rest[:, 2 * own_rows :].reshape(INNER, WIDTH)

    convolved, mixed_low, mixer_weight = call(
        functools.partial(conv_forward, bits),
        (MIXED // TILE,),
        [
            pl.BlockSpec(memory_space=pltpu.SMEM),
            whole(rows + HALO, WIDTH),
            whole(rows, marks),
            spec((8, TILE), lambda i: (0, i)),
        ]
        + [spec((pieces[0].shape[0], TILE), lambda i: (0, i))] * len(pieces),
        [
            spec((rows, TILE), lambda i: (0, i)),
            spec((rows + HALO, TILE), lambda i: (0, i)),
            spec((WIDTH, TILE), lambda i: (0, i)),
        ],
        [((rows, MIXED), bf16), ((rows + HALO, MIXED), bf16), ((WIDTH, MIXED), bf16)],
        [
            pltpu.VMEM((TILE // LANES, rows + HALO, LANES), f32),
            pltpu.VMEM((3, rows, LANES), f32),
            pltpu.VMEM((WIDTH, TILE), f32),
        ],
        14,
    )(seq_index.reshape(1), extended, masks, taps, *pieces)

    by_block = lambda *tail: spec((STRETCH,) + tail, lambda c: (c,) + (0,) * len(tail))
    both_spec = spec((STRETCH, 2 * STATE), lambda c: (c, INNER // (2 * STATE)))
    values_spec = spec((STRETCH, INNER), lambda c: (c, 0))
    raw_spec = spec((STRETCH, LANES), lambda c: (c, CONV_CHANNELS // LANES))
    per_block = lambda *tail: spec((1,) + tail, lambda c: (c,) + (0,) * len(tail))

    scaled, cumul, delta, cumul_rows, start, factors, device_state, device_decay = call(
        local_states,
        (stretches,),
        [values_spec, both_spec, raw_spec, by_block(marks), whole(1, LANES), whole(1, LANES), whole(2 * LANES, INNER)],
        [
            by_block(INNER),
            by_block(LANES),
            by_block(LANES),
            per_block(32, STRETCH),
            per_block(STATE, INNER),
            per_block(8, INNER),
            whole(PAIRS, STATE, LANES),
            whole(16, LANES),
        ],
        [
            ((rows, INNER), bf16),
            ((rows, LANES), f32),
            ((rows, LANES), f32),
            ((stretches, 32, STRETCH), f32),
            ((stretches, STATE, INNER), bf16),
            ((stretches, 8, INNER), f32),
            ((PAIRS, STATE, LANES), bf16),
            ((16, LANES), bf16),
        ],
        [
            pltpu.VMEM((STATE, INNER), f32),
            pltpu.VMEM((8, LANES), f32),
            pltpu.VMEM((STRETCH, INNER), bf16),
            pltpu.VMEM((2 * STRETCH + 16, INNER), f32),
        ],
        9,
    )(convolved, convolved, convolved, masks, bias_row, rate_row, spreader)

    share = PAIRS * STATE // count
    decay_rows = jnp.broadcast_to(device_decay[None, :2], (count, 2, LANES))
    sent = jnp.concatenate([device_state.reshape(count, share, LANES), decay_rows], axis=1)

    def exchange(value):
        return lax.all_to_all(value, EVERY, split_axis=0, concat_axis=0, tiled=True)

    def scan_parts(parts, reverse):
        return pl.pallas_call(
            functools.partial(prefix, reverse=reverse),
            in_specs=[pl.BlockSpec(memory_space=pltpu.SMEM)] + [pl.BlockSpec(memory_space=pltpu.VMEM)] * 2,
            out_shape=jax.ShapeDtypeStruct((count, share, LANES), bf16),
            scratch_shapes=[pltpu.VMEM((count, 2 * LANES), f32)],
            compiler_params=pltpu.CompilerParams(vmem_limit_bytes=ROOM),
        )(device_index.reshape(1), parts, all_decays)

    arrived = exchange(sent)
    all_decays = arrived[:, share].astype(f32) + arrived[:, share + 1].astype(f32)
    prior = exchange(scan_parts(arrived, False)).reshape(PAIRS, STATE, LANES)

    diag = call(
        diagonal,
        (stretches,),
        [
            by_block(INNER),
            both_spec,
            by_block(LANES),
            per_block(32, STRETCH),
            by_block(marks),
            per_block(1, STRETCH),
        ],
        [by_block(INNER)],
        [((rows, INNER), f32)],
        [pltpu.VMEM((HEADS, STRETCH, LANES), f32), pltpu.VMEM((STRETCH, STRETCH), f32)],
        16,
    )(scaled, convolved, cumul, cumul_rows, masks, segments)[0]
    gate = jnp.dot(normed, gate_weight, preferred_element_type=f32)
    normed_grad = mm(out_cotangent, out_full, NT)

    back = stretches - 1
    by_block_r = lambda *tail: spec((STRETCH,) + tail, lambda c: (back - c,) + (0,) * len(tail))
    per_block_r = lambda *tail: spec((1,) + tail, lambda c: (back - c,) + (0,) * len(tail))
    wide_scratch = lambda kind: pltpu.VMEM((STRETCH, INNER), kind)
    (
        gated_low,
        gate_grad,
        mixed_grad,
        row_sums,
        reads_grad,
        after_local,
        middle_sums,
        start_grad,
        after_decay,
    ) = call(
        middle,
        (stretches,),
        [
            by_block_r(INNER),
            spec((STRETCH, INNER), lambda c: (back - c, 0)),
            spec((STRETCH, 2 * STATE), lambda c: (back - c, INNER // (2 * STATE))),
            by_block_r(LANES),
            by_block_r(marks),
            per_block_r(STATE, INNER),
            per_block_r(8, INNER),
            whole(PAIRS, STATE, LANES),
            by_block_r(INNER),
            by_block_r(INNER),
            whole(1, INNER),
            whole(1, INNER),
            whole(INNER, LANES),
            whole(2 * LANES, INNER),
        ],
        [
            by_block_r(INNER),
            by_block_r(INNER),
            by_block_r(INNER),
            by_block_r(LANES),
            by_block_r(STATE),
            per_block_r(STATE, INNER),
            whole(16, INNER),
            whole(PAIRS, STATE, LANES),
            per_block_r(8, INNER),
        ],
        [
            ((rows, INNER), bf16),
            ((rows, INNER), bf16),
            ((rows, INNER), bf16),
            ((rows, LANES), f32),
            ((rows, STATE), f32),
            ((stretches, STATE, INNER), bf16),
            ((16, INNER), f32),
            ((PAIRS, STATE, LANES), bf16),
            ((stretches, 8, INNER), f32),
        ],
        [
            pltpu.VMEM((STATE, INNER), bf16),
            wide_scratch(f32),
            wide_scratch(f32),
            wide_scratch(f32),
            wide_scratch(f32),
            wide_scratch(bf16),
            wide_scratch(bf16),
            pltpu.VMEM((2, STRETCH, INNER), bf16),
            pltpu.VMEM((STATE, INNER), f32),
            pltpu.VMEM((8, INNER), f32),
        ],
        24,
    )(
        diag, convolved, convolved, cumul, masks, start, factors, prior, gate, normed_grad,
        gain_row, skip_row, head_of, spreader,
    )

    sent_back = exchange(start_grad.reshape(count, share, LANES))
    diag_sums, both_grad = call(
        diagonal_back,
        (stretches,),
        [
            by_block(INNER),
            both_spec,
            by_block(LANES),
            per_block(32, STRETCH),
            by_block(marks),
            per_block(1, STRETCH),
            by_block(INNER),
        ],
        [by_block(INNER), by_block(2 * STATE)],
        [((rows, INNER), f32), ((rows, 2 * STATE), f32)],
        [
            pltpu.VMEM((HEADS, STRETCH, LANES), f32),
            pltpu.VMEM((STRETCH, STRETCH), f32),
            pltpu.VMEM((STRETCH, STRETCH), f32),
        ],
        20,
    )(scaled, convolved, cumul, cumul_rows, masks, segments, mixed_grad)
    sent_back, diag_sums, both_grad = lax.optimization_barrier((sent_back, diag_sums, both_grad))
    scanned = scan_parts(sent_back, True)
    gated_low, gate_grad, scanned = lax.optimization_barrier((gated_low, gate_grad, scanned))
    after = exchange(scanned)
    block_output = (inputs + mm(gated_low, out_full)).astype(bf16)

    gate_term = mm(normed, gate_grad, TN).astype(bf16)
    out_term = mm(gated_low, out_cotangent, TN).astype(bf16)
    rest_term = jnp.concatenate(
        [
            gate_term[:, :WIDTH].reshape(count, -1, WIDTH),
            gate_term[:, WIDTH:].reshape(count, -1, WIDTH),
            out_term.reshape(count, -1, WIDTH),
        ],
        axis=1,
    ).reshape(-1, WIDTH)
    rest_term, block_output, after = lax.optimization_barrier((rest_term, block_output, after))
    after = after.reshape(PAIRS, STATE, LANES)
    rest_line = lax.psum_scatter(rest_term, "seq", scatter_dimension=0, tiled=True)

    conv_out_grad, late_sums = call(
        late,
        (stretches,),
        [
            values_spec,
            both_spec,
            by_block(LANES),
            by_block(LANES),
            raw_spec,
            by_block(marks),
            whole(1, LANES),
            whole(1, LANES),
            per_block(8, INNER),
            per_block(STATE, INNER),
            whole(PAIRS, STATE, LANES),
            per_block(STATE, INNER),
            per_block(8, INNER),
            whole(PAIRS, STATE, LANES),
            by_block(INNER),
            by_block(INNER),
            by_block(INNER),
            by_block(LANES),
            by_block(STATE),
            by_block(2 * STATE),
            whole(1, INNER),
            whole(INNER, LANES),
            whole(2 * LANES, INNER),
        ],
        [by_block(MIXED), whole(8, LANES)],
        [((rows, MIXED), bf16), ((8, LANES), f32)],
        [
            pltpu.VMEM((STATE, INNER), bf16),
            wide_scratch(f32),
            pltpu.VMEM((2 * STRETCH, INNER), f32),
            wide_scratch(bf16),
            pltpu.VMEM((4 * STRETCH + 16, INNER), bf16),
        ],
        18,
    )(
        convolved, convolved, cumul, delta, convolved, masks, bias_row, rate_row, factors, start, prior, after_local, after_decay,
        after, diag_sums, scaled, mixed_grad, row_sums, reads_grad, both_grad, skip_row, head_of, spreader,
    )

    mixed_in_grad, rim, tail, tap_grads = call(
        conv_back,
        (MIXED // TILE,),
        [
            spec((rows + HALO, TILE), lambda i: (0, i)),
            spec((rows, TILE), lambda i: (0, i)),
            whole(rows, marks),
            spec((8, TILE), lambda i: (0, i)),
        ],
        [
            spec((rows, TILE), lambda i: (0, i)),
            spec((8, TILE), lambda i: (0, i)),
            spec((HALO, TILE), lambda i: (0, i)),
            spec((8, TILE), lambda i: (0, i)),
        ],
        [
            ((rows, MIXED), bf16),
            ((8, MIXED), f32),
            ((HALO, MIXED), f32),
            ((8, MIXED), f32),
        ],
        [
            pltpu.VMEM((TILE // LANES, rows + HALO, LANES), f32),
            pltpu.VMEM((3, rows, LANES), f32),
            pltpu.VMEM((CONV_WIDTH, TILE // LANES, rows + 8, LANES), f32),
        ],
        20,
    )(mixed_low, conv_out_grad, masks, taps)

    from_next = passed_along(rim, EVERY, -1)
    gate_grad, rim = lax.optimization_barrier((gate_grad, rim))
    gate_part = mm(gate_grad, gate_weight, NT)
    from_next, gate_part = lax.optimization_barrier((from_next, gate_part))
    fixed = jnp.concatenate([tail[: HALO - 8], tail[HALO - 8 :] + from_next], axis=0).astype(bf16)
    mixer_grad = lax.dynamic_update_slice(mixed_in_grad, fixed, (rows - HALO, 0))
    term = mm(normed, mixer_grad, TN).astype(bf16)
    line_rows = own_rows * lax.axis_size("head")

    def block_of(value, place, size):
        return lax.dynamic_slice_in_dim(value, place * size, size, axis=0)

    summed = []
    for k in range(chips):
        given = block_of(term, seq_index ^ (2 * k) ^ 1, line_rows)
        kept = block_of(term, seq_index ^ (2 * k), line_rows)
        summed.append(kept.astype(f32) + fetched(given, "seq", 1).astype(f32))
    sending = [part.astype(bf16) for part in summed[1:]]
    early = jnp.concatenate(
        [
            jnp.sum(middle_sums[:8], axis=0),
            tap_grads[: CONV_WIDTH + 1, :CONV_CHANNELS].reshape(-1),
            late_sums[1, :HEADS],
            late_sums[0, :HEADS] * rate_row[0, :HEADS],
            jnp.sum(middle_sums[8:].reshape(8, HEADS, HEAD_SIZE), axis=(0, 2)),
        ]
    )
    size = early.shape[0]
    early = jnp.pad(early, (0, -size % count)).reshape(count, -1)
    sending, mixer_grad, rest_line, early = lax.optimization_barrier((sending, mixer_grad, rest_line, early))
    rest_grad = lax.psum_scatter(rest_line, "head", scatter_dimension=0, tiled=True)
    rest_grad = lax.optimization_barrier(rest_grad).astype(f32)
    gate_weight_grad = jnp.concatenate([rest_grad[:own_rows], rest_grad[own_rows : 2 * own_rows]], axis=1)
    out_grad = rest_grad[2 * own_rows :]
    line = summed[0]
    for k, part in enumerate(sending, 1):
        line = line + fetched(part, "seq", 2 * k).astype(f32)
    normed_in_grad = gate_part + mm(mixer_grad, mixer_weight, NT)
    norm_gain_grad = jnp.sum(normed_in_grad * inputs * in_scale, axis=0)
    scaled_in = normed_in_grad * norm_gain
    input_grad = (
        out_cotangent.astype(f32)
        + in_scale * scaled_in
        - inputs * in_scale**3 * jnp.mean(scaled_in * inputs, axis=-1, keepdims=True)
    )

    early_parts = exchange(early)
    line, norm_gain_grad, early_parts = lax.optimization_barrier((line, norm_gain_grad, early_parts))
    own_early = jnp.sum(early_parts, axis=0)
    both_vectors = jnp.concatenate([own_early, norm_gain_grad])
    both_vectors = exchange(jnp.broadcast_to(both_vectors[None], (count,) + both_vectors.shape))
    vector_grad = jnp.concatenate(
        [
            jnp.sum(both_vectors[:, own_early.shape[0] :], axis=0),
            both_vectors[:, : own_early.shape[0]].reshape(-1)[:size],
        ]
    )
    mixer_weight_grad = block_of(line, head_index, own_rows)
    for k in range(1, lax.axis_size("head")):
        given = block_of(line, head_index ^ k, own_rows).astype(bf16)
        mixer_weight_grad = mixer_weight_grad + fetched(given, "head", k).astype(f32)

    in_grad = jnp.concatenate([gate_weight_grad, mixer_weight_grad[:, : CONV_CHANNELS + HEADS]], axis=1)
    in_first_new, in_second_new, in_weight_new = adamw(
        in_weight, in_first, in_second, in_grad, RATE_MATRIX, WEIGHT_DECAY
    )
    out_first_new, out_second_new, out_weight_new = adamw(
        out_weight, out_first, out_second, out_grad, RATE_MATRIX, WEIGHT_DECAY
    )
    vector_first_new, vector_second_new, vector_new = adamw(
        vector_params, vector_first, vector_second, vector_grad, RATE_VECTOR, 0.0
    )
    return (
        block_output,
        input_grad.astype(bf16),
        in_first_new,
        in_second_new,
        in_weight_new,
        out_first_new,
        out_second_new,
        out_weight_new,
        vector_first_new,
        vector_second_new,
        vector_new,
    )


def solution(mesh):
    split = P(EVERY, None)
    in_specs = (split, split, P(), split, split, P(), split, split, split, split, P(), P())
    out_specs = (split,) * 8 + (P(),) * 3
    return jax.shard_map(
        per_device, mesh=mesh, in_specs=in_specs, out_specs=out_specs, check_vma=False
    )
```

```python
import functools

import jax
import jax.numpy as jnp
from jax import lax
from jax.experimental import pallas as pl
from jax.experimental.pallas import tpu as pltpu
from jax.sharding import PartitionSpec as P

WIDTH = 768
INNER = 1536
HEADS = 24
HEAD_SIZE = 64
STATE = 128
CONV_WIDTH = 4
STRETCH = 256
STEP = 10
CONV_CHANNELS = 1792
LANES = 128
PAIRS = HEADS // 2
MIXED = CONV_CHANNELS + LANES
HALO = 16
CHUNK = 32
PART = 64
LOG2E = 1.4426950408889634
HALF = STRETCH // 2
TILE = 384

EPS = 1e-05
BETA_ONE = 0.9
BETA_TWO = 0.95
ADAM_EPS = 1e-08
WEIGHT_DECAY = 0.1
RATE_MATRIX = 0.05
RATE_VECTOR = 0.3
HIGHEST = lax.Precision.HIGHEST
f32 = jnp.float32
bf16 = jnp.bfloat16
EVERY = ("seq", "head")
ROOM = 56 * 1024 * 1024


def passed_along(value, axis, steps):
    count = lax.axis_size(axis)
    leading, last = (max(0, -steps), min(count, count - steps))
    return lax.ppermute(value, axis, [(source, source + steps) for source in range(leading, last)])


def fetched(value, axis, bit):
    return lax.ppermute(value, axis, [(k, k ^ bit) for k in range(lax.axis_size(axis))])


def laid(pieces):
    rows, width = pieces[0][1].shape
    whole_array = jnp.zeros((rows * len(pieces), width), pieces[0][1].dtype)
    for place, piece in pieces:
        whole_array = lax.dynamic_update_slice(whole_array, piece, (place * rows, 0))
    return whole_array


def split_vector(vector):
    cursor = 0
    pieces = []
    for length in (WIDTH, INNER, CONV_WIDTH * CONV_CHANNELS, CONV_CHANNELS, HEADS, HEADS, HEADS):
        pieces.append(vector[cursor : cursor + length])
        cursor = cursor + length
    norm_gain, gated_gain, conv_flat, conv_bias, step_bias, log_rate, skip_gain = pieces
    return (
        norm_gain,
        gated_gain,
        conv_flat.reshape(CONV_WIDTH, CONV_CHANNELS),
        conv_bias,
        step_bias,
        log_rate,
        skip_gain,
    )


def adamw(weight, first, second, grad, rate, decay):
    first_new = BETA_ONE * first + (1.0 - BETA_ONE) * grad
    second_new = BETA_TWO * second + (1.0 - BETA_TWO) * grad * grad
    corrected_first = first_new / (1.0 - BETA_ONE**STEP)
    corrected_second = second_new / (1.0 - BETA_TWO**STEP)
    weight_new = weight - rate * (
        corrected_first / (jnp.sqrt(corrected_second) + ADAM_EPS) + decay * weight
    )
    return (first_new, second_new, weight_new)


def mm(left, right, dims=((1,), (0,)), precision=None):
    return lax.dot_general(left, right, (dims, ((), ())), preferred_element_type=f32, precision=precision)


NT = ((1,), (1,))
TN = ((0,), (0,))


def spec(block, index):
    return pl.BlockSpec(block, index)


def whole(*shape):
    return pl.BlockSpec(shape, lambda *ids: (0,) * len(shape))


def call(body, grid, ins, outs, out_shapes, scratch, micros):
    return pl.pallas_call(
        body,
        grid=grid,
        in_specs=ins,
        out_specs=outs,
        out_shape=[jax.ShapeDtypeStruct(shape, kind) for shape, kind in out_shapes],
        scratch_shapes=scratch,
        compiler_params=pltpu.CompilerParams(vmem_limit_bytes=ROOM),
        cost_estimate=pl.CostEstimate(flops=0, bytes_accessed=int(micros * 3.4e6), transcendentals=0),
    )


def in_two(value):
    top = value.astype(bf16)
    return top, (value - top.astype(f32)).astype(bf16)


def spread_heads(per_head, spreader):
    return mm(jnp.concatenate(in_two(per_head), axis=1), spreader)


def eights(value):
    return jnp.sum(value.reshape(value.shape[0] // 8, 8, value.shape[1]), axis=0)


def tiles(width):
    return [slice(j * LANES, (j + 1) * LANES) for j in range(width // LANES)]


def chunks(count, size, body):
    def step(i, _):
        body(pl.ds(pl.multiple_of(i * size, size), size))
        return 0

    lax.fori_loop(0, count // size, step, 0, unroll=2)


def sigmoid(v):
    return 0.5 * jnp.tanh(0.5 * v) + 0.5


def softplus(v):
    small = jnp.exp(-jnp.abs(v))
    series = small * (1.0 - small * (0.5 - small * (1.0 / 3.0 - small * 0.25)))
    return jnp.maximum(v, 0.0) + jnp.where(small < 0.01, series, jnp.log(1.0 + small))


def spread_masks(masks, same):
    @pl.when(pl.program_id(0) == 0)
    def _():
        for k in range(1, CONV_WIDTH):
            same[k - 1] = jnp.broadcast_to(masks[:, k - 1 : k], same.shape[1:])


def hold(mixed, held):
    count = mixed.shape[0] - HALO
    for j, cols in enumerate(tiles(TILE)):
        held[j, :HALO, :] = mixed[count:, cols].astype(f32)
        held[j, HALO:, :] = mixed[:count, cols].astype(f32)


def conv_part(held, same, taps, rows, cols):
    taken = [held[cols.start // LANES, pl.ds(HALO + rows - k, PART), :] for k in range(CONV_WIDTH)]
    total = taps[CONV_WIDTH : CONV_WIDTH + 1, cols] + taps[3:4, cols] * taken[0]
    for k in range(1, CONV_WIDTH):
        total = total + taps[3 - k : 4 - k, cols] * (taken[k] * same[k - 1, rows : rows + PART, :])
    return total, taken


def each_tile(convolve, other):
    for cols in tiles(TILE)[:-1]:
        convolve(cols)
    ending = pl.program_id(0) == pl.num_programs(0) - 1
    cols = tiles(TILE)[-1]
    pl.when(jnp.logical_not(ending))(lambda: convolve(cols))
    pl.when(ending)(lambda: other(cols))


def conv_forward(bits, where, normed, masks, taps, *others):
    pieces, (out, mixed, weight_out, held, same, weight) = others[: len(bits)], others[len(bits) :]
    count = out.shape[0]
    spread_masks(masks, same)
    size = pieces[0].shape[0]
    for bit, piece in zip(bits, pieces):
        start = pl.multiple_of((where[0] ^ bit) * size, 8)
        weight[pl.ds(start, size), :] = piece[...].astype(f32)
    weight_out[...] = weight[...].astype(bf16)
    low = mm(normed[...], weight_out[...]).astype(bf16)
    mixed[...] = low
    hold(low, held)

    def convolve(cols):
        for rows in range(0, count, PART):
            total, _ = conv_part(held, same, taps, rows, cols)
            out[rows : rows + PART, cols] = (total * sigmoid(total)).astype(bf16)

    def other(cols):
        out[:, cols] = mixed[:count, cols]

    each_tile(convolve, other)


def local_states(
    values, both, raw, masks, bias, rate, spreader,
    scaled, cumul_out, delta_out, cumul_rows, start, factors, device_state, device_decay,
    state, reach, weighted, spreads,
):
    c = pl.program_id(0)

    @pl.when(c == 0)
    def _():
        state[...] = jnp.zeros_like(state)
        reach[...] = jnp.ones_like(reach)

    delta = softplus(raw[...].astype(f32) + bias[...])
    cumul = sums_until(delta * rate[...], False)
    last = cumul[STRETCH - 1 : STRETCH, :]
    carry = jnp.exp(last) * masks[STRETCH - 1 : STRETCH, 4:5]
    cumul_out[...] = cumul
    delta_out[...] = delta
    cumul_rows[0] = cumul.T[: cumul_rows.shape[1], :] * LOG2E
    end_weight = jnp.exp(last - cumul) * masks[:, 3:4] * delta
    line = lax.broadcasted_iota(jnp.int32, (8, LANES), 0)
    factor_rows = jnp.where(line == 0, carry, reach[...])
    spreads[...] = spread_heads(
        jnp.concatenate([delta, end_weight, factor_rows, factor_rows], axis=0), spreader[...]
    )
    for cols in tiles(INNER):
        v = values[:, cols].astype(f32)
        scaled[:, cols] = (v * spreads[:STRETCH, cols]).astype(bf16)
        weighted[:, cols] = (v * spreads[STRETCH : 2 * STRETCH, cols]).astype(bf16)
    start[0] = state[...].astype(bf16)
    wide = spreads[2 * STRETCH : 2 * STRETCH + 8, :]
    factors[0] = wide
    state[...] = state[...] * wide[0:1, :] + mm(both[:, :STATE], weighted[...], TN)
    reach[...] = reach[...] * carry

    @pl.when(c == pl.num_programs(0) - 1)
    def _():
        for j, cols in enumerate(tiles(INNER)):
            device_state[j] = state[:, cols].astype(bf16)
        top, low = in_two(reach[...])
        device_decay[...] = jnp.concatenate([top[:1], low[:1], jnp.zeros((14, LANES), bf16)], axis=0)


def spread_columns(cumul, columns):
    for h in range(HEADS):
        columns[h] = jnp.broadcast_to(cumul[:, h : h + 1] * LOG2E, (STRETCH, LANES))


def diagonal(scaled, both, cumul, cumul_rows, masks, segments, out, columns, scores):
    spread_columns(cumul, columns)
    row = lax.broadcasted_iota(jnp.int32, (STRETCH, STRETCH), 0)
    col = lax.broadcasted_iota(jnp.int32, (STRETCH, STRETCH), 1)
    inside = (row >= col) & (masks[:, 5:6] == segments[0])
    scores[...] = jnp.where(inside, mm(both[:, STATE:], both[:, :STATE], NT), 0.0)
    low = lax.broadcasted_iota(jnp.int32, (HALF, LANES), 1) < HEAD_SIZE

    def pair(j, _):
        cols = pl.ds(pl.multiple_of(j * LANES, LANES), LANES)
        v = scaled[:, cols]
        tops, bottoms = [], []
        for q in range(2):
            h = 2 * j + q
            line = cumul_rows[0, pl.ds(h, 1), :]
            upper = columns[h, :HALF, :]
            lower = columns[h, HALF:, :]
            top = jnp.exp2(jnp.minimum(upper - line[:, :HALF], 0.0)) * scores[:HALF, :HALF]
            left = jnp.exp2(jnp.minimum(lower - line[:, :HALF], 0.0)) * scores[HALF:, :HALF]
            right = jnp.exp2(jnp.minimum(lower - line[:, HALF:], 0.0)) * scores[HALF:, HALF:]
            tops.append(mm(top.astype(bf16), v[:HALF]))
            bottoms.append(mm(jnp.concatenate([left.astype(bf16), right.astype(bf16)], axis=1), v))
        out[:HALF, cols] = jnp.where(low, *tops)
        out[HALF:, cols] = jnp.where(low, *bottoms)
        return 0

    lax.fori_loop(0, PAIRS, pair, 0, unroll=2)


def diagonal_back(
    scaled, both, cumul, cumul_rows, masks, segments, out_grad, sums, both_grad, columns, scores, total
):
    spread_columns(cumul, columns)
    row = lax.broadcasted_iota(jnp.int32, (STRETCH, STRETCH), 0)
    col = lax.broadcasted_iota(jnp.int32, (STRETCH, STRETCH), 1)
    inside = (row <= col) & (masks[:, 5:6] == segments[0])
    scores[...] = jnp.where(inside, mm(both[:, :STATE], both[:, STATE:], NT), 0.0)
    total[...] = jnp.zeros_like(total)
    low = lax.broadcasted_iota(jnp.int32, (HALF, LANES), 1) < HEAD_SIZE
    first = lax.broadcasted_iota(jnp.int32, (STRETCH, LANES), 1) < HEAD_SIZE

    def pair(j, _):
        cols = pl.ds(pl.multiple_of(j * LANES, LANES), LANES)
        v = scaled[:, cols]
        g = out_grad[:, cols]
        tops, bottoms = [], []
        for q in range(2):
            h = 2 * j + q
            line = cumul_rows[0, pl.ds(h, 1), :]
            upper = columns[h, :HALF, :]
            lower = columns[h, HALF:, :]
            own = jnp.where(first == (q == 0), g.astype(f32), 0.0).astype(bf16)
            left = jnp.exp2(jnp.minimum(line[:, :HALF] - upper, 0.0))
            right = jnp.exp2(jnp.minimum(line[:, HALF:] - upper, 0.0))
            corner = jnp.exp2(jnp.minimum(line[:, HALF:] - lower, 0.0))
            tops.append(
                mm(
                    jnp.concatenate(
                        [(left * scores[:HALF, :HALF]).astype(bf16), (right * scores[:HALF, HALF:]).astype(bf16)],
                        axis=1,
                    ),
                    g,
                )
            )
            bottoms.append(mm((corner * scores[HALF:, HALF:]).astype(bf16), g[HALF:]))
            top_grad = mm(v[:HALF], own, NT)
            total[:HALF, :HALF] += left * top_grad[:, :HALF]
            total[:HALF, HALF:] += right * top_grad[:, HALF:]
            total[HALF:, HALF:] += corner * mm(v[HALF:], own[HALF:], NT)
        sums[:HALF, cols] = jnp.where(low, *tops)
        sums[HALF:, cols] = jnp.where(low, *bottoms)
        return 0

    lax.fori_loop(0, PAIRS, pair, 0, unroll=2)
    scores_grad = jnp.where(inside, total[...], 0.0).astype(bf16)
    both_grad[:, :STATE] = mm(scores_grad, both[:, STATE:])
    both_grad[:, STATE:] = mm(scores_grad, both[:, :STATE], TN)


def prefix(where, parts, decays, out, wide, reverse):
    count = parts.shape[0]
    rows = out.shape[1]
    first = where[0] * rows // STATE
    head = 2 * first + lax.broadcasted_iota(jnp.int32, (LANES, 2 * LANES), 1) // HEAD_SIZE
    chosen = (lax.broadcasted_iota(jnp.int32, (LANES, 2 * LANES), 0) == head).astype(f32)
    wide[...] = mm(decays[...], chosen, precision=HIGHEST)
    places = where[0] * rows + lax.broadcasted_iota(jnp.int32, (rows, LANES), 0)
    second = places >= (first + 1) * STATE

    def step(i, state):
        k = count - 1 - i if reverse else i
        out[pl.ds(k, 1)] = state.astype(bf16)[None]
        two = wide[pl.ds(k, 1), :]
        decay = jnp.where(second, two[:, LANES:], two[:, :LANES])
        return decay * state + parts[pl.ds(k, 1), :rows, :][0].astype(f32)

    lax.fori_loop(0, count, step, jnp.zeros((rows, LANES), f32))


def sums_until(value, upper):
    row = lax.broadcasted_iota(jnp.int32, (STRETCH, STRETCH), 0)
    col = lax.broadcasted_iota(jnp.int32, (STRETCH, STRETCH), 1)
    triangle = ((row <= col) if upper else (row >= col)).astype(bf16)
    top = value.astype(bf16)
    rest = value - top.astype(f32)
    middle_part, low = in_two(rest)
    out = mm(triangle, jnp.concatenate([top, middle_part, low], axis=1))
    return out[:, :LANES] + out[:, LANES : 2 * LANES] + out[:, 2 * LANES :]


def entered(start, factors, prior, j, cols):
    return start[0, :, cols].astype(f32) + factors[0, 1:2, cols] * prior[j].astype(f32)


def middle(
    diag, values, both, cumul, masks, start, factors, prior, gate, normed_grad, gain, skip, heads,
    spreader,
    gated_low, gate_grad, mixed_grad, row_sums, reads_grad, after_local, sums, start_grad,
    after_decay, full, entry, enter, gated_all, sig_all, mixed_all, entry_low, products, state_grad, tail_decay,
):
    i = pl.program_id(0)

    @pl.when(i == 0)
    def _():
        state_grad[...] = jnp.zeros_like(state_grad)
        tail_decay[...] = jnp.ones_like(tail_decay)
        sums[...] = jnp.zeros_like(sums)

    reads = both[:, STATE:]
    for j, cols in enumerate(tiles(INNER)):
        full[:, cols] = entered(start, factors, prior, j, cols).astype(bf16)
    entry[...] = mm(reads, full[...])
    enter[...] = spread_heads(jnp.exp(cumul[...]) * masks[:, 4:5], spreader[...])

    def rows_step(rows):
        square = jnp.zeros((CHUNK, LANES), f32)
        cross = jnp.zeros((CHUNK, LANES), f32)
        for cols in tiles(INNER):
            mixed_sum = diag[rows, cols] + entry[rows, cols] * enter[rows, cols]
            mixed = (mixed_sum + skip[:, cols] * values[rows, cols].astype(f32)).astype(bf16)
            z = gate[rows, cols]
            sig = sigmoid(z)
            gated = mixed.astype(f32) * (z * sig)
            square = square + gated * gated
            cross = cross + (normed_grad[rows, cols] * gain[:, cols]) * gated
            entry[rows, cols] = mixed_sum
            gated_all[rows, cols] = gated
            sig_all[rows, cols] = sig
            mixed_all[rows, cols] = mixed
        scale = lax.rsqrt(jnp.sum(square, axis=1, keepdims=True) * (1.0 / INNER) + EPS)
        pull = jnp.sum(cross, axis=1, keepdims=True) * (1.0 / INNER) * (scale * scale * scale)
        scale = jnp.broadcast_to(scale, (CHUNK, LANES))
        pull = jnp.broadcast_to(pull, (CHUNK, LANES))
        for cols in tiles(INNER):
            gated = gated_all[rows, cols]
            sig = sig_all[rows, cols]
            back = normed_grad[rows, cols]
            unit = gated * scale
            gated_low[rows, cols] = (unit * gain[:, cols]).astype(bf16)
            gated_grad = scale * (back * gain[:, cols]) - gated * pull
            act = gate[rows, cols] * sig
            slope = sig + act * (1.0 - sig)
            gate_grad[rows, cols] = (gated_grad * mixed_all[rows, cols].astype(f32) * slope).astype(bf16)
            low_grad = (gated_grad * act).astype(bf16)
            mixed_grad[rows, cols] = low_grad
            grad = low_grad.astype(f32)
            entry_low[rows, cols] = (grad * enter[rows, cols]).astype(bf16)
            products[0, rows, cols], products[1, rows, cols] = in_two(grad * entry[rows, cols])
            sums[0:8, cols] += eights(back * unit)
            sums[8:16, cols] += eights(grad * values[rows, cols].astype(f32))

    chunks(STRETCH, CHUNK, rows_step)
    summed = mm(products[...].reshape(2 * STRETCH, INNER), heads[...])
    row_sums[...] = summed[:STRETCH] + summed[STRETCH:]
    reads_grad[...] = mm(entry_low[...], full[...], NT)
    after_local[0] = state_grad[...].astype(bf16)
    after_decay[0] = tail_decay[...]
    state_grad[...] = state_grad[...] * factors[0, 0:1, :] + mm(reads, entry_low[...], TN)
    tail_decay[...] = tail_decay[...] * factors[0, 0:1, :]

    @pl.when(i == pl.num_programs(0) - 1)
    def _():
        for j, cols in enumerate(tiles(INNER)):
            start_grad[j] = state_grad[:, cols].astype(bf16)


def late(
    values, both, cumul, delta, raw, masks, bias, rate, factors, start, prior, after_local, after_decay, after,
    diag_sums, scaled, out_grad, row_sums, reads_grad, both_grad, skip, heads, spreader,
    conv_grad, sums,
    after_low, spread_grad, spreads, weighted, products,
):
    @pl.when(pl.program_id(0) == 0)
    def _():
        sums[...] = jnp.zeros_like(sums)

    carry_rows = []
    for j, cols in enumerate(tiles(INNER)):
        here = after_local[0, :, cols].astype(f32) + after_decay[0, 0:1, cols] * after[j].astype(f32)
        after_low[:, cols] = here.astype(bf16)
        carry_rows.append(eights(here * entered(start, factors, prior, j, cols)) * factors[0, 0:1, cols])
    top, low = in_two(jnp.concatenate(carry_rows, axis=1))
    products[4 * STRETCH :, :] = jnp.concatenate([top, low], axis=0)
    spread_grad[...] = mm(both[:, :STATE], after_low[...])
    step = delta[...]
    total = cumul[...]
    end_factor = jnp.exp(total[STRETCH - 1 : STRETCH, :] - total) * masks[:, 3:4]
    spreads[...] = spread_heads(jnp.concatenate([end_factor, step], axis=0), spreader[...])
    later = lambda rows, k: pl.ds(pl.multiple_of(rows.start + k * STRETCH, CHUNK), CHUNK)

    def rows_step(rows):
        for cols in tiles(INNER):
            v = values[rows, cols].astype(f32)
            ends = spreads[rows, cols]
            step_wide = spreads[later(rows, 1), cols]
            inner = diag_sums[rows, cols]
            outer = spread_grad[rows, cols] * ends
            both_sums = inner + outer
            conv_grad[rows, cols] = (
                step_wide * both_sums + skip[:, cols] * out_grad[rows, cols].astype(f32)
            ).astype(bf16)
            weighted[rows, cols] = (v * (ends * step_wide)).astype(bf16)
            products[rows, cols] = (v * both_sums).astype(bf16)
            products[later(rows, 1), cols] = (v * outer).astype(bf16)
            top, low = in_two(scaled[rows, cols].astype(f32) * inner)
            products[later(rows, 2), cols] = top
            products[later(rows, 3), cols] = low

    chunks(STRETCH, CHUNK, rows_step)
    conv_grad[:, INNER : INNER + STATE] = (
        both_grad[:, :STATE] + mm(weighted[...], after_low[...], NT)
    ).astype(bf16)
    conv_grad[:, INNER + STATE : CONV_CHANNELS] = (both_grad[:, STATE:] + reads_grad[...]).astype(bf16)
    summed = mm(products[...], heads[...])
    joint, outer_sum, top, low = [summed[k * STRETCH : (k + 1) * STRETCH] for k in range(4)]
    end_spread = outer_sum * step
    last_grad = jnp.sum(end_spread, axis=0, keepdims=True) + jnp.sum(summed[4 * STRETCH :], axis=0, keepdims=True)
    cumul_grad = row_sums[...] - (top + low) - end_spread
    decay_grad = sums_until(cumul_grad, True) + last_grad
    step_grad = joint + decay_grad * rate[...]
    pre_grad = step_grad * sigmoid(raw[...].astype(f32) + bias[...])
    conv_grad[:, CONV_CHANNELS:] = pre_grad.astype(bf16)
    sums[0:1, :] += jnp.sum(decay_grad * step, axis=0, keepdims=True)
    sums[1:2, :] += jnp.sum(pre_grad, axis=0, keepdims=True)


def conv_back(mixed, grad, masks, taps, out, rim, tail, tap_grads, held, same, kept):
    rows_all = grad.shape[0]
    spread_masks(masks, same)
    hold(mixed, held)
    kept[:, :, pl.ds(rows_all, 8), :] = jnp.zeros(kept.shape[:2] + (8, LANES), f32)

    def convolve(cols):
        tile = cols.start // LANES
        found = [jnp.zeros((8, LANES), f32) for _ in range(CONV_WIDTH + 1)]
        for rows in range(0, rows_all, PART):
            total, taken = conv_part(held, same, taps, rows, cols)
            sig = sigmoid(total)
            here = grad[rows : rows + PART, cols].astype(f32) * (sig * (1.0 + total * (1.0 - sig)))
            found[CONV_WIDTH] = found[CONV_WIDTH] + eights(here)
            for k in range(CONV_WIDTH):
                masked = here if k == 0 else here * same[k - 1, rows : rows + PART, :]
                kept[k, tile, pl.ds(rows, PART), :] = masked
                found[3 - k] = found[3 - k] + eights(masked * taken[k])
        lines = [jnp.sum(line, axis=0, keepdims=True) for line in found]
        tap_grads[:, cols] = jnp.concatenate(lines + [jnp.zeros((3, LANES), f32)], axis=0)
        for rows in range(0, rows_all, PART):
            value = taps[3:4, cols] * kept[0, tile, pl.ds(rows, PART), :]
            for k in range(1, CONV_WIDTH):
                value = value + taps[3 - k : 4 - k, cols] * kept[k, tile, pl.ds(rows + k, PART), :]
            out[rows : rows + PART, cols] = value.astype(bf16)
            if rows + PART == rows_all:
                tail[:, cols] = value[PART - HALO :, :]
        lines = [jnp.zeros((5, LANES), f32)]
        for m in (3, 2, 1):
            line = jnp.zeros((1, LANES), f32)
            for k in range(m, CONV_WIDTH):
                line = line + taps[3 - k : 4 - k, cols] * kept[k, tile, k - m : k - m + 1, :]
            lines.append(line)
        rim[:, cols] = jnp.concatenate(lines, axis=0)

    def other(cols):
        out[:, cols] = grad[:, cols]
        tail[:, cols] = grad[rows_all - HALO :, cols].astype(f32)
        rim[:, cols] = jnp.zeros((8, LANES), f32)
        tap_grads[:, cols] = jnp.zeros((8, LANES), f32)

    each_tile(convolve, other)


def per_device(
    block_input,
    out_cotangent,
    segment_ids,
    in_weight,
    out_weight,
    vector_params,
    in_first,
    in_second,
    out_first,
    out_second,
    vector_first,
    vector_second,
):
    count = lax.axis_size("seq") * lax.axis_size("head")
    device_index = lax.axis_index(EVERY)
    rows = block_input.shape[0]
    stretches = rows // STRETCH
    own_rows = in_weight.shape[0]
    halo = passed_along(block_input[rows - HALO :], EVERY, 1)

    head_index, seq_index = lax.axis_index("head"), lax.axis_index("seq")
    chips = lax.axis_size("seq") // 2
    mixer_own = jnp.pad(in_weight[:, INNER:].astype(bf16), ((0, 0), (0, LANES - HEADS)))
    mixer_group = laid(
        [(head_index, mixer_own)]
        + [(head_index ^ k, fetched(mixer_own, "head", k)) for k in range(1, lax.axis_size("head"))]
    )
    mixer_group, halo, block_now, segment_now, vector_now, none = lax.optimization_barrier(
        (mixer_group, halo, block_input, segment_ids, vector_params, jnp.zeros((), jnp.int32))
    )
    norm_gain, gated_gain, conv_taps, conv_bias, step_bias, log_rate, skip_gain = split_vector(vector_now)

    def unit_rows(block):
        wide = block.astype(f32)
        scale = lax.rsqrt(jnp.mean(wide * wide, axis=-1, keepdims=True) + EPS)
        return wide, scale

    inputs, in_scale = unit_rows(block_now)
    normed = (inputs * in_scale * norm_gain).astype(bf16)
    halo_wide, halo_scale = unit_rows(halo)
    extended = jnp.concatenate([normed, (halo_wide * halo_scale * norm_gain).astype(bf16)], axis=0)

    padded = jnp.concatenate(
        [jnp.full((3,), -1, jnp.int32), segment_now, jnp.full((3,), -1, jnp.int32)]
    )
    window = lax.dynamic_slice_in_dim(padded, device_index * rows, rows + 6)
    own = window[3 : 3 + rows]
    blocks = own.reshape(stretches, STRETCH)
    before = window[2 : 2 + rows].reshape(stretches, STRETCH)[:, :1]
    columns = [(window[3 - k : 3 - k + rows] == own) for k in (1, 2, 3)]
    columns.append((blocks == blocks[:, -1:]).reshape(rows))
    columns.append((blocks == before).reshape(rows))
    columns.append(own)
    marks = 8
    lane = lax.broadcasted_iota(jnp.int32, (rows, marks), 1)
    masks = jnp.zeros((rows, marks), f32)
    for k, column in enumerate(columns):
        masks = jnp.where(lane == k, column.astype(f32)[:, None], masks)
    segments = blocks.astype(f32).reshape(stretches, 1, STRETCH)

    taps = jnp.concatenate([conv_taps, conv_bias[None], jnp.zeros((3, CONV_CHANNELS), f32)], axis=0)
    taps = jnp.pad(taps, ((0, 0), (0, LANES)))

    def head_row(vector):
        return jnp.pad(vector, (0, LANES - HEADS)).reshape(1, LANES)

    bias_row = head_row(step_bias)
    rate_row = head_row(-jnp.exp(log_rate))
    skip_row = jnp.repeat(skip_gain, HEAD_SIZE).reshape(1, INNER)
    gain_row = gated_gain.reshape(1, INNER)
    head_of = (
        lax.broadcasted_iota(jnp.int32, (INNER, LANES), 0) // HEAD_SIZE
        == lax.broadcasted_iota(jnp.int32, (INNER, LANES), 1) + none
    ).astype(bf16)
    spreader = jnp.concatenate([head_of.T, head_of.T], axis=0)

    rest_own = jnp.concatenate([in_weight[:, :WIDTH], in_weight[:, WIDTH:INNER], out_weight], axis=0).astype(bf16)
    rest_own, _ = lax.optimization_barrier((rest_own, mixer_group))
    near = [(0, mixer_group)] + [(2 * k, fetched(mixer_group, "seq", 2 * k)) for k in range(1, chips)]
    near, extended, normed, masks, taps, spreader, head_of = lax.optimization_barrier(
        ([piece for _, piece in near], extended, normed, masks, taps, spreader, head_of)
    )
    bits = [2 * k for k in range(chips)] + [2 * k + 1 for k in range(chips)]
    pieces = near + [fetched(piece, "seq", 1) for piece in near]
    rest = lax.all_gather(rest_own, EVERY, axis=0, tiled=True).reshape(count, -1, WIDTH)
    gate_weight = jnp.concatenate(
        [rest[:, :own_rows].reshape(WIDTH, WIDTH), rest[:, own_rows : 2 * own_rows].reshape(WIDTH, WIDTH)], axis=1
    )
    out_full = rest[:, 2 * own_rows :].reshape(INNER, WIDTH)

    convolved, mixed_low, mixer_weight = call(
        functools.partial(conv_forward, bits),
        (MIXED // TILE,),
        [
            pl.BlockSpec(memory_space=pltpu.SMEM),
            whole(rows + HALO, WIDTH),
            whole(rows, marks),
            spec((8, TILE), lambda i: (0, i)),
        ]
        + [spec((pieces[0].shape[0], TILE), lambda i: (0, i))] * len(pieces),
        [
            spec((rows, TILE), lambda i: (0, i)),
            spec((rows + HALO, TILE), lambda i: (0, i)),
            spec((WIDTH, TILE), lambda i: (0, i)),
        ],
        [((rows, MIXED), bf16), ((rows + HALO, MIXED), bf16), ((WIDTH, MIXED), bf16)],
        [
            pltpu.VMEM((TILE // LANES, rows + HALO, LANES), f32),
            pltpu.VMEM((3, rows, LANES), f32),
            pltpu.VMEM((WIDTH, TILE), f32),
        ],
        14,
    )(seq_index.reshape(1), extended, masks, taps, *pieces)

    by_block = lambda *tail: spec((STRETCH,) + tail, lambda c: (c,) + (0,) * len(tail))
    both_spec = spec((STRETCH, 2 * STATE), lambda c: (c, INNER // (2 * STATE)))
    values_spec = spec((STRETCH, INNER), lambda c: (c, 0))
    raw_spec = spec((STRETCH, LANES), lambda c: (c, CONV_CHANNELS // LANES))
    per_block = lambda *tail: spec((1,) + tail, lambda c: (c,) + (0,) * len(tail))

    scaled, cumul, delta, cumul_rows, start, factors, device_state, device_decay = call(
        local_states,
        (stretches,),
        [values_spec, both_spec, raw_spec, by_block(marks), whole(1, LANES), whole(1, LANES), whole(2 * LANES, INNER)],
        [
            by_block(INNER),
            by_block(LANES),
            by_block(LANES),
            per_block(32, STRETCH),
            per_block(STATE, INNER),
            per_block(8, INNER),
            whole(PAIRS, STATE, LANES),
            whole(16, LANES),
        ],
        [
            ((rows, INNER), bf16),
            ((rows, LANES), f32),
            ((rows, LANES), f32),
            ((stretches, 32, STRETCH), f32),
            ((stretches, STATE, INNER), bf16),
            ((stretches, 8, INNER), f32),
            ((PAIRS, STATE, LANES), bf16),
            ((16, LANES), bf16),
        ],
        [
            pltpu.VMEM((STATE, INNER), f32),
            pltpu.VMEM((8, LANES), f32),
            pltpu.VMEM((STRETCH, INNER), bf16),
            pltpu.VMEM((2 * STRETCH + 16, INNER), f32),
        ],
        9,
    )(convolved, convolved, convolved, masks, bias_row, rate_row, spreader)

    share = PAIRS * STATE // count
    decay_rows = jnp.broadcast_to(device_decay[None, :2], (count, 2, LANES))
    sent = jnp.concatenate([device_state.reshape(count, share, LANES), decay_rows], axis=1)

    def exchange(value):
        return lax.all_to_all(value, EVERY, split_axis=0, concat_axis=0, tiled=True)

    def scan_parts(parts, reverse):
        return pl.pallas_call(
            functools.partial(prefix, reverse=reverse),
            in_specs=[pl.BlockSpec(memory_space=pltpu.SMEM)] + [pl.BlockSpec(memory_space=pltpu.VMEM)] * 2,
            out_shape=jax.ShapeDtypeStruct((count, share, LANES), bf16),
            scratch_shapes=[pltpu.VMEM((count, 2 * LANES), f32)],
            compiler_params=pltpu.CompilerParams(vmem_limit_bytes=ROOM),
        )(device_index.reshape(1), parts, all_decays)

    arrived = exchange(sent)
    all_decays = arrived[:, share].astype(f32) + arrived[:, share + 1].astype(f32)
    prior = exchange(scan_parts(arrived, False)).reshape(PAIRS, STATE, LANES)

    diag = call(
        diagonal,
        (stretches,),
        [
            by_block(INNER),
            both_spec,
            by_block(LANES),
            per_block(32, STRETCH),
            by_block(marks),
            per_block(1, STRETCH),
        ],
        [by_block(INNER)],
        [((rows, INNER), f32)],
        [pltpu.VMEM((HEADS, STRETCH, LANES), f32), pltpu.VMEM((STRETCH, STRETCH), f32)],
        16,
    )(scaled, convolved, cumul, cumul_rows, masks, segments)[0]
    gate = jnp.dot(normed, gate_weight, preferred_element_type=f32)
    normed_grad = mm(out_cotangent, out_full, NT)

    back = stretches - 1
    by_block_r = lambda *tail: spec((STRETCH,) + tail, lambda c: (back - c,) + (0,) * len(tail))
    per_block_r = lambda *tail: spec((1,) + tail, lambda c: (back - c,) + (0,) * len(tail))
    wide_scratch = lambda kind: pltpu.VMEM((STRETCH, INNER), kind)
    (
        gated_low,
        gate_grad,
        mixed_grad,
        row_sums,
        reads_grad,
        after_local,
        middle_sums,
        start_grad,
        after_decay,
    ) = call(
        middle,
        (stretches,),
        [
            by_block_r(INNER),
            spec((STRETCH, INNER), lambda c: (back - c, 0)),
            spec((STRETCH, 2 * STATE), lambda c: (back - c, INNER // (2 * STATE))),
            by_block_r(LANES),
            by_block_r(marks),
            per_block_r(STATE, INNER),
            per_block_r(8, INNER),
            whole(PAIRS, STATE, LANES),
            by_block_r(INNER),
            by_block_r(INNER),
            whole(1, INNER),
            whole(1, INNER),
            whole(INNER, LANES),
            whole(2 * LANES, INNER),
        ],
        [
            by_block_r(INNER),
            by_block_r(INNER),
            by_block_r(INNER),
            by_block_r(LANES),
            by_block_r(STATE),
            per_block_r(STATE, INNER),
            whole(16, INNER),
            whole(PAIRS, STATE, LANES),
            per_block_r(8, INNER),
        ],
        [
            ((rows, INNER), bf16),
            ((rows, INNER), bf16),
            ((rows, INNER), bf16),
            ((rows, LANES), f32),
            ((rows, STATE), f32),
            ((stretches, STATE, INNER), bf16),
            ((16, INNER), f32),
            ((PAIRS, STATE, LANES), bf16),
            ((stretches, 8, INNER), f32),
        ],
        [
            pltpu.VMEM((STATE, INNER), bf16),
            wide_scratch(f32),
            wide_scratch(f32),
            wide_scratch(f32),
            wide_scratch(f32),
            wide_scratch(bf16),
            wide_scratch(bf16),
            pltpu.VMEM((2, STRETCH, INNER), bf16),
            pltpu.VMEM((STATE, INNER), f32),
            pltpu.VMEM((8, INNER), f32),
        ],
        24,
    )(
        diag, convolved, convolved, cumul, masks, start, factors, prior, gate, normed_grad,
        gain_row, skip_row, head_of, spreader,
    )

    sent_back = exchange(start_grad.reshape(count, share, LANES))
    gate_term = mm(normed, gate_grad, TN).astype(bf16)
    out_term = mm(gated_low, out_cotangent, TN).astype(bf16)
    rest_term = jnp.concatenate(
        [
            gate_term[:, :WIDTH].reshape(count, -1, WIDTH),
            gate_term[:, WIDTH:].reshape(count, -1, WIDTH),
            out_term.reshape(count, -1, WIDTH),
        ],
        axis=1,
    ).reshape(-1, WIDTH)
    sent_back, rest_term = lax.optimization_barrier((sent_back, rest_term))
    rest_line = lax.psum_scatter(rest_term, "seq", scatter_dimension=0, tiled=True)
    scanned = scan_parts(sent_back, True)
    scanned, mixed_grad, gated_low = lax.optimization_barrier((scanned, mixed_grad, gated_low))
    after = exchange(scanned)
    block_output = (inputs + mm(gated_low, out_full)).astype(bf16)
    diag_sums, both_grad = call(
        diagonal_back,
        (stretches,),
        [
            by_block(INNER),
            both_spec,
            by_block(LANES),
            per_block(32, STRETCH),
            by_block(marks),
            per_block(1, STRETCH),
            by_block(INNER),
        ],
        [by_block(INNER), by_block(2 * STATE)],
        [((rows, INNER), f32), ((rows, 2 * STATE), f32)],
        [
            pltpu.VMEM((HEADS, STRETCH, LANES), f32),
            pltpu.VMEM((STRETCH, STRETCH), f32),
            pltpu.VMEM((STRETCH, STRETCH), f32),
        ],
        20,
    )(scaled, convolved, cumul, cumul_rows, masks, segments, mixed_grad)
    after, diag_sums, both_grad, block_output = lax.optimization_barrier((after, diag_sums, both_grad, block_output))
    after = after.reshape(PAIRS, STATE, LANES)

    conv_out_grad, late_sums = call(
        late,
        (stretches,),
        [
            values_spec,
            both_spec,
            by_block(LANES),
            by_block(LANES),
            raw_spec,
            by_block(marks),
            whole(1, LANES),
            whole(1, LANES),
            per_block(8, INNER),
            per_block(STATE, INNER),
            whole(PAIRS, STATE, LANES),
            per_block(STATE, INNER),
            per_block(8, INNER),
            whole(PAIRS, STATE, LANES),
            by_block(INNER),
            by_block(INNER),
            by_block(INNER),
            by_block(LANES),
            by_block(STATE),
            by_block(2 * STATE),
            whole(1, INNER),
            whole(INNER, LANES),
            whole(2 * LANES, INNER),
        ],
        [by_block(MIXED), whole(8, LANES)],
        [((rows, MIXED), bf16), ((8, LANES), f32)],
        [
            pltpu.VMEM((STATE, INNER), bf16),
            wide_scratch(f32),
            pltpu.VMEM((2 * STRETCH, INNER), f32),
            wide_scratch(bf16),
            pltpu.VMEM((4 * STRETCH + 16, INNER), bf16),
        ],
        18,
    )(
        convolved, convolved, cumul, delta, convolved, masks, bias_row, rate_row, factors, start, prior, after_local, after_decay,
        after, diag_sums, scaled, mixed_grad, row_sums, reads_grad, both_grad, skip_row, head_of, spreader,
    )

    mixed_in_grad, rim, tail, tap_grads = call(
        conv_back,
        (MIXED // TILE,),
        [
            spec((rows + HALO, TILE), lambda i: (0, i)),
            spec((rows, TILE), lambda i: (0, i)),
            whole(rows, marks),
            spec((8, TILE), lambda i: (0, i)),
        ],
        [
            spec((rows, TILE), lambda i: (0, i)),
            spec((8, TILE), lambda i: (0, i)),
            spec((HALO, TILE), lambda i: (0, i)),
            spec((8, TILE), lambda i: (0, i)),
        ],
        [
            ((rows, MIXED), bf16),
            ((8, MIXED), f32),
            ((HALO, MIXED), f32),
            ((8, MIXED), f32),
        ],
        [
            pltpu.VMEM((TILE // LANES, rows + HALO, LANES), f32),
            pltpu.VMEM((3, rows, LANES), f32),
            pltpu.VMEM((CONV_WIDTH, TILE // LANES, rows + 8, LANES), f32),
        ],
        20,
    )(mixed_low, conv_out_grad, masks, taps)

    rim, rest_line = lax.optimization_barrier((rim, rest_line))
    rest_grad = lax.psum_scatter(rest_line, "head", scatter_dimension=0, tiled=True)
    rest_grad = lax.optimization_barrier(rest_grad).astype(f32)
    gate_weight_grad = jnp.concatenate([rest_grad[:own_rows], rest_grad[own_rows : 2 * own_rows]], axis=1)
    out_grad = rest_grad[2 * own_rows :]
    from_next = passed_along(rim, EVERY, -1)
    gate_grad, rim = lax.optimization_barrier((gate_grad, rim))
    gate_part = mm(gate_grad, gate_weight, NT)
    from_next, gate_part = lax.optimization_barrier((from_next, gate_part))
    fixed = jnp.concatenate([tail[: HALO - 8], tail[HALO - 8 :] + from_next], axis=0).astype(bf16)
    mixer_grad = lax.dynamic_update_slice(mixed_in_grad, fixed, (rows - HALO, 0))
    term = mm(normed, mixer_grad, TN).astype(bf16)
    line_rows = own_rows * lax.axis_size("head")

    def block_of(value, place, size):
        return lax.dynamic_slice_in_dim(value, place * size, size, axis=0)

    summed = []
    for k in range(chips):
        given = block_of(term, seq_index ^ (2 * k) ^ 1, line_rows)
        kept = block_of(term, seq_index ^ (2 * k), line_rows)
        summed.append(kept.astype(f32) + fetched(given, "seq", 1).astype(f32))
    sending = [part.astype(bf16) for part in summed[1:]]
    early = jnp.concatenate(
        [
            jnp.sum(middle_sums[:8], axis=0),
            tap_grads[: CONV_WIDTH + 1, :CONV_CHANNELS].reshape(-1),
            late_sums[1, :HEADS],
            late_sums[0, :HEADS] * rate_row[0, :HEADS],
            jnp.sum(middle_sums[8:].reshape(8, HEADS, HEAD_SIZE), axis=(0, 2)),
        ]
    )
    size = early.shape[0]
    early = jnp.pad(early, (0, -size % count)).reshape(count, -1)
    sending, mixer_grad, early = lax.optimization_barrier((sending, mixer_grad, early))
    line = summed[0]
    for k, part in enumerate(sending, 1):
        line = line + fetched(part, "seq", 2 * k).astype(f32)
    normed_in_grad = gate_part + mm(mixer_grad, mixer_weight, NT)
    norm_gain_grad = jnp.sum(normed_in_grad * inputs * in_scale, axis=0)
    scaled_in = normed_in_grad * norm_gain
    input_grad = (
        out_cotangent.astype(f32)
        + in_scale * scaled_in
        - inputs * in_scale**3 * jnp.mean(scaled_in * inputs, axis=-1, keepdims=True)
    )

    early_parts = exchange(early)
    out_new = adamw(out_weight, out_first, out_second, out_grad, RATE_MATRIX, WEIGHT_DECAY)
    line, norm_gain_grad, early_parts, out_new = lax.optimization_barrier((line, norm_gain_grad, early_parts, out_new))
    own_early = jnp.sum(early_parts, axis=0)
    both_vectors = jnp.concatenate([own_early, norm_gain_grad])
    both_vectors = exchange(jnp.broadcast_to(both_vectors[None], (count,) + both_vectors.shape))
    mixer_weight_grad = block_of(line, head_index, own_rows)
    for k in range(1, lax.axis_size("head")):
        given = block_of(line, head_index ^ k, own_rows).astype(bf16)
        mixer_weight_grad = mixer_weight_grad + fetched(given, "head", k).astype(f32)
    in_grad = jnp.concatenate([gate_weight_grad, mixer_weight_grad[:, : CONV_CHANNELS + HEADS]], axis=1)
    in_new = adamw(in_weight, in_first, in_second, in_grad, RATE_MATRIX, WEIGHT_DECAY)
    both_vectors, in_new = lax.optimization_barrier((both_vectors, in_new))
    vector_grad = jnp.concatenate(
        [
            jnp.sum(both_vectors[:, own_early.shape[0] :], axis=0),
            both_vectors[:, : own_early.shape[0]].reshape(-1)[:size],
        ]
    )
    vector_first_new, vector_second_new, vector_new = adamw(
        vector_params, vector_first, vector_second, vector_grad, RATE_VECTOR, 0.0
    )
    return (
        block_output,
        input_grad.astype(bf16),
        *in_new,
        *out_new,
        vector_first_new,
        vector_second_new,
        vector_new,
    )


def solution(mesh):
    split = P(EVERY, None)
    in_specs = (split, split, P(), split, split, P(), split, split, split, split, P(), P())
    out_specs = (split,) * 8 + (P(),) * 3
    return jax.shard_map(
        per_device, mesh=mesh, in_specs=in_specs, out_specs=out_specs, check_vma=False
    )
```

```python
import functools

import jax
import jax.numpy as jnp
from jax import lax
from jax.experimental import pallas as pl
from jax.experimental.pallas import tpu as pltpu
from jax.sharding import PartitionSpec as P

WIDTH = 768
INNER = 1536
HEADS = 24
HEAD_SIZE = 64
STATE = 128
CONV_WIDTH = 4
STRETCH = 256
STEP = 10
CONV_CHANNELS = 1792
LANES = 128
PAIRS = HEADS // 2
MIXED = CONV_CHANNELS + LANES
HALO = 16
CHUNK = 32
PART = 64
LOG2E = 1.4426950408889634
HALF = STRETCH // 2
TILE = 384

EPS = 1e-05
BETA_ONE = 0.9
BETA_TWO = 0.95
ADAM_EPS = 1e-08
WEIGHT_DECAY = 0.1
RATE_MATRIX = 0.05
RATE_VECTOR = 0.3
HIGHEST = lax.Precision.HIGHEST
f32 = jnp.float32
bf16 = jnp.bfloat16
EVERY = ("seq", "head")
ROOM = 56 * 1024 * 1024


def passed_along(value, axis, steps):
    count = lax.axis_size(axis)
    leading, last = (max(0, -steps), min(count, count - steps))
    return lax.ppermute(value, axis, [(source, source + steps) for source in range(leading, last)])


def fetched(value, axis, bit):
    return lax.ppermute(value, axis, [(k, k ^ bit) for k in range(lax.axis_size(axis))])


def laid(pieces):
    rows, width = pieces[0][1].shape
    whole_array = jnp.zeros((rows * len(pieces), width), pieces[0][1].dtype)
    for place, piece in pieces:
        whole_array = lax.dynamic_update_slice(whole_array, piece, (place * rows, 0))
    return whole_array


def split_vector(vector):
    cursor = 0
    pieces = []
    for length in (WIDTH, INNER, CONV_WIDTH * CONV_CHANNELS, CONV_CHANNELS, HEADS, HEADS, HEADS):
        pieces.append(vector[cursor : cursor + length])
        cursor = cursor + length
    norm_gain, gated_gain, conv_flat, conv_bias, step_bias, log_rate, skip_gain = pieces
    return (
        norm_gain,
        gated_gain,
        conv_flat.reshape(CONV_WIDTH, CONV_CHANNELS),
        conv_bias,
        step_bias,
        log_rate,
        skip_gain,
    )


def adamw(weight, first, second, grad, rate, decay):
    first_new = BETA_ONE * first + (1.0 - BETA_ONE) * grad
    second_new = BETA_TWO * second + (1.0 - BETA_TWO) * grad * grad
    corrected_first = first_new / (1.0 - BETA_ONE**STEP)
    corrected_second = second_new / (1.0 - BETA_TWO**STEP)
    weight_new = weight - rate * (
        corrected_first / (jnp.sqrt(corrected_second) + ADAM_EPS) + decay * weight
    )
    return (first_new, second_new, weight_new)


def mm(left, right, dims=((1,), (0,)), precision=None):
    return lax.dot_general(left, right, (dims, ((), ())), preferred_element_type=f32, precision=precision)


NT = ((1,), (1,))
TN = ((0,), (0,))


def spec(block, index):
    return pl.BlockSpec(block, index)


def whole(*shape):
    return pl.BlockSpec(shape, lambda *ids: (0,) * len(shape))


def call(body, grid, ins, outs, out_shapes, scratch, micros):
    return pl.pallas_call(
        body,
        grid=grid,
        in_specs=ins,
        out_specs=outs,
        out_shape=[jax.ShapeDtypeStruct(shape, kind) for shape, kind in out_shapes],
        scratch_shapes=scratch,
        compiler_params=pltpu.CompilerParams(vmem_limit_bytes=ROOM),
        cost_estimate=pl.CostEstimate(flops=0, bytes_accessed=int(micros * 3.4e6), transcendentals=0),
    )


def in_two(value):
    top = value.astype(bf16)
    return top, (value - top.astype(f32)).astype(bf16)


def spread_heads(per_head, spreader):
    return mm(jnp.concatenate(in_two(per_head), axis=1), spreader)


def eights(value):
    return jnp.sum(value.reshape(value.shape[0] // 8, 8, value.shape[1]), axis=0)


def tiles(width):
    return [slice(j * LANES, (j + 1) * LANES) for j in range(width // LANES)]


def chunks(count, size, body):
    def step(i, _):
        body(pl.ds(pl.multiple_of(i * size, size), size))
        return 0

    lax.fori_loop(0, count // size, step, 0, unroll=2)


def sigmoid(v):
    return 0.5 * jnp.tanh(0.5 * v) + 0.5


def softplus(v):
    small = jnp.exp(-jnp.abs(v))
    series = small * (1.0 - small * (0.5 - small * (1.0 / 3.0 - small * 0.25)))
    return jnp.maximum(v, 0.0) + jnp.where(small < 0.01, series, jnp.log(1.0 + small))


def spread_masks(masks, same):
    @pl.when(pl.program_id(0) == 0)
    def _():
        for k in range(1, CONV_WIDTH):
            same[k - 1] = jnp.broadcast_to(masks[:, k - 1 : k], same.shape[1:])


def hold(mixed, held):
    count = mixed.shape[0] - HALO
    for j, cols in enumerate(tiles(TILE)):
        held[j, :HALO, :] = mixed[count:, cols].astype(f32)
        held[j, HALO:, :] = mixed[:count, cols].astype(f32)


def conv_part(held, same, taps, rows, cols):
    taken = [held[cols.start // LANES, pl.ds(HALO + rows - k, PART), :] for k in range(CONV_WIDTH)]
    total = taps[CONV_WIDTH : CONV_WIDTH + 1, cols] + taps[3:4, cols] * taken[0]
    for k in range(1, CONV_WIDTH):
        total = total + taps[3 - k : 4 - k, cols] * (taken[k] * same[k - 1, rows : rows + PART, :])
    return total, taken


def each_tile(convolve, other):
    for cols in tiles(TILE)[:-1]:
        convolve(cols)
    ending = pl.program_id(0) == pl.num_programs(0) - 1
    cols = tiles(TILE)[-1]
    pl.when(jnp.logical_not(ending))(lambda: convolve(cols))
    pl.when(ending)(lambda: other(cols))


def conv_forward(bits, where, normed, masks, taps, *others):
    pieces, (out, mixed, weight_out, held, same, weight) = others[: len(bits)], others[len(bits) :]
    count = out.shape[0]
    spread_masks(masks, same)
    size = pieces[0].shape[0]
    for bit, piece in zip(bits, pieces):
        start = pl.multiple_of((where[0] ^ bit) * size, 8)
        weight[pl.ds(start, size), :] = piece[...].astype(f32)
    weight_out[...] = weight[...].astype(bf16)
    low = mm(normed[...], weight_out[...]).astype(bf16)
    mixed[...] = low
    hold(low, held)

    def convolve(cols):
        for rows in range(0, count, PART):
            total, _ = conv_part(held, same, taps, rows, cols)
            out[rows : rows + PART, cols] = (total * sigmoid(total)).astype(bf16)

    def other(cols):
        out[:, cols] = mixed[:count, cols]

    each_tile(convolve, other)


def local_states(
    values, both, raw, masks, bias, rate, spreader,
    scaled, cumul_out, delta_out, cumul_rows, start, factors, device_state, device_decay,
    state, reach, weighted, spreads,
):
    c = pl.program_id(0)

    @pl.when(c == 0)
    def _():
        state[...] = jnp.zeros_like(state)
        reach[...] = jnp.ones_like(reach)

    delta = softplus(raw[...].astype(f32) + bias[...])
    cumul = sums_until(delta * rate[...], False)
    last = cumul[STRETCH - 1 : STRETCH, :]
    carry = jnp.exp(last) * masks[STRETCH - 1 : STRETCH, 4:5]
    cumul_out[...] = cumul
    delta_out[...] = delta
    cumul_rows[0] = cumul.T[: cumul_rows.shape[1], :] * LOG2E
    end_weight = jnp.exp(last - cumul) * masks[:, 3:4] * delta
    line = lax.broadcasted_iota(jnp.int32, (8, LANES), 0)
    factor_rows = jnp.where(line == 0, carry, reach[...])
    spreads[...] = spread_heads(
        jnp.concatenate([delta, end_weight, factor_rows, factor_rows], axis=0), spreader[...]
    )
    for cols in tiles(INNER):
        v = values[:, cols].astype(f32)
        scaled[:, cols] = (v * spreads[:STRETCH, cols]).astype(bf16)
        weighted[:, cols] = (v * spreads[STRETCH : 2 * STRETCH, cols]).astype(bf16)
    start[0] = state[...].astype(bf16)
    wide = spreads[2 * STRETCH : 2 * STRETCH + 8, :]
    factors[0] = wide
    state[...] = state[...] * wide[0:1, :] + mm(both[:, :STATE], weighted[...], TN)
    reach[...] = reach[...] * carry

    @pl.when(c == pl.num_programs(0) - 1)
    def _():
        for j, cols in enumerate(tiles(INNER)):
            device_state[j] = state[:, cols].astype(bf16)
        top, low = in_two(reach[...])
        device_decay[...] = jnp.concatenate([top[:1], low[:1], jnp.zeros((14, LANES), bf16)], axis=0)


def spread_columns(cumul, columns):
    for h in range(HEADS):
        columns[h] = jnp.broadcast_to(cumul[:, h : h + 1] * LOG2E, (STRETCH, LANES))


def diagonal(scaled, both, cumul, cumul_rows, masks, segments, out, columns, scores):
    spread_columns(cumul, columns)
    row = lax.broadcasted_iota(jnp.int32, (STRETCH, STRETCH), 0)
    col = lax.broadcasted_iota(jnp.int32, (STRETCH, STRETCH), 1)
    inside = (row >= col) & (masks[:, 5:6] == segments[0])
    scores[...] = jnp.where(inside, mm(both[:, STATE:], both[:, :STATE], NT), 0.0)
    low = lax.broadcasted_iota(jnp.int32, (HALF, LANES), 1) < HEAD_SIZE

    def pair(j, _):
        cols = pl.ds(pl.multiple_of(j * LANES, LANES), LANES)
        v = scaled[:, cols]
        tops, bottoms = [], []
        for q in range(2):
            h = 2 * j + q
            line = cumul_rows[0, pl.ds(h, 1), :]
            upper = columns[h, :HALF, :]
            lower = columns[h, HALF:, :]
            top = jnp.exp2(jnp.minimum(upper - line[:, :HALF], 0.0)) * scores[:HALF, :HALF]
            left = jnp.exp2(jnp.minimum(lower - line[:, :HALF], 0.0)) * scores[HALF:, :HALF]
            right = jnp.exp2(jnp.minimum(lower - line[:, HALF:], 0.0)) * scores[HALF:, HALF:]
            tops.append(mm(top.astype(bf16), v[:HALF]))
            bottoms.append(mm(jnp.concatenate([left.astype(bf16), right.astype(bf16)], axis=1), v))
        out[:HALF, cols] = jnp.where(low, *tops)
        out[HALF:, cols] = jnp.where(low, *bottoms)
        return 0

    lax.fori_loop(0, PAIRS, pair, 0, unroll=4)


def diagonal_back(
    scaled, both, cumul, cumul_rows, masks, segments, out_grad, sums, both_grad, columns, scores, total
):
    spread_columns(cumul, columns)
    row = lax.broadcasted_iota(jnp.int32, (STRETCH, STRETCH), 0)
    col = lax.broadcasted_iota(jnp.int32, (STRETCH, STRETCH), 1)
    inside = (row <= col) & (masks[:, 5:6] == segments[0])
    scores[...] = jnp.where(inside, mm(both[:, :STATE], both[:, STATE:], NT), 0.0)
    total[...] = jnp.zeros_like(total)
    low = lax.broadcasted_iota(jnp.int32, (HALF, LANES), 1) < HEAD_SIZE
    first = lax.broadcasted_iota(jnp.int32, (STRETCH, LANES), 1) < HEAD_SIZE

    def pair(j, _):
        cols = pl.ds(pl.multiple_of(j * LANES, LANES), LANES)
        v = scaled[:, cols]
        g = out_grad[:, cols]
        tops, bottoms = [], []
        for q in range(2):
            h = 2 * j + q
            line = cumul_rows[0, pl.ds(h, 1), :]
            upper = columns[h, :HALF, :]
            lower = columns[h, HALF:, :]
            own = jnp.where(first == (q == 0), g.astype(f32), 0.0).astype(bf16)
            left = jnp.exp2(jnp.minimum(line[:, :HALF] - upper, 0.0))
            right = jnp.exp2(jnp.minimum(line[:, HALF:] - upper, 0.0))
            corner = jnp.exp2(jnp.minimum(line[:, HALF:] - lower, 0.0))
            tops.append(
                mm(
                    jnp.concatenate(
                        [(left * scores[:HALF, :HALF]).astype(bf16), (right * scores[:HALF, HALF:]).astype(bf16)],
                        axis=1,
                    ),
                    g,
                )
            )
            bottoms.append(mm((corner * scores[HALF:, HALF:]).astype(bf16), g[HALF:]))
            top_grad = mm(v[:HALF], own, NT)
            total[:HALF, :HALF] += left * top_grad[:, :HALF]
            total[:HALF, HALF:] += right * top_grad[:, HALF:]
            total[HALF:, HALF:] += corner * mm(v[HALF:], own[HALF:], NT)
        sums[:HALF, cols] = jnp.where(low, *tops)
        sums[HALF:, cols] = jnp.where(low, *bottoms)
        return 0

    lax.fori_loop(0, PAIRS, pair, 0, unroll=4)
    scores_grad = jnp.where(inside, total[...], 0.0).astype(bf16)
    both_grad[:, :STATE] = mm(scores_grad, both[:, STATE:])
    both_grad[:, STATE:] = mm(scores_grad, both[:, :STATE], TN)


def prefix(where, parts, decays, out, wide, reverse):
    count = parts.shape[0]
    rows = out.shape[1]
    first = where[0] * rows // STATE
    head = 2 * first + lax.broadcasted_iota(jnp.int32, (LANES, 2 * LANES), 1) // HEAD_SIZE
    chosen = (lax.broadcasted_iota(jnp.int32, (LANES, 2 * LANES), 0) == head).astype(f32)
    wide[...] = mm(decays[...], chosen, precision=HIGHEST)
    places = where[0] * rows + lax.broadcasted_iota(jnp.int32, (rows, LANES), 0)
    second = places >= (first + 1) * STATE

    def step(i, state):
        k = count - 1 - i if reverse else i
        out[pl.ds(k, 1)] = state.astype(bf16)[None]
        two = wide[pl.ds(k, 1), :]
        decay = jnp.where(second, two[:, LANES:], two[:, :LANES])
        return decay * state + parts[pl.ds(k, 1), :rows, :][0].astype(f32)

    lax.fori_loop(0, count, step, jnp.zeros((rows, LANES), f32))


def sums_until(value, upper):
    row = lax.broadcasted_iota(jnp.int32, (STRETCH, STRETCH), 0)
    col = lax.broadcasted_iota(jnp.int32, (STRETCH, STRETCH), 1)
    triangle = ((row <= col) if upper else (row >= col)).astype(bf16)
    top = value.astype(bf16)
    rest = value - top.astype(f32)
    middle_part, low = in_two(rest)
    out = mm(triangle, jnp.concatenate([top, middle_part, low], axis=1))
    return out[:, :LANES] + out[:, LANES : 2 * LANES] + out[:, 2 * LANES :]


def entered(start, factors, prior, j, cols):
    return start[0, :, cols].astype(f32) + factors[0, 1:2, cols] * prior[j].astype(f32)


def middle(
    diag, values, both, cumul, masks, start, factors, prior, gate, normed_grad, gain, skip, heads,
    spreader,
    gated_low, gate_grad, mixed_grad, row_sums, reads_grad, after_local, sums, start_grad,
    after_decay, full, entry, enter, gated_all, sig_all, mixed_all, entry_low, products, state_grad, tail_decay,
):
    i = pl.program_id(0)

    @pl.when(i == 0)
    def _():
        state_grad[...] = jnp.zeros_like(state_grad)
        tail_decay[...] = jnp.ones_like(tail_decay)
        sums[...] = jnp.zeros_like(sums)

    reads = both[:, STATE:]
    for j, cols in enumerate(tiles(INNER)):
        full[:, cols] = entered(start, factors, prior, j, cols).astype(bf16)
    entry[...] = mm(reads, full[...])
    enter[...] = spread_heads(jnp.exp(cumul[...]) * masks[:, 4:5], spreader[...])

    def rows_step(rows):
        square = jnp.zeros((CHUNK, LANES), f32)
        cross = jnp.zeros((CHUNK, LANES), f32)
        for cols in tiles(INNER):
            mixed_sum = diag[rows, cols] + entry[rows, cols] * enter[rows, cols]
            mixed = (mixed_sum + skip[:, cols] * values[rows, cols].astype(f32)).astype(bf16)
            z = gate[rows, cols]
            sig = sigmoid(z)
            gated = mixed.astype(f32) * (z * sig)
            square = square + gated * gated
            cross = cross + (normed_grad[rows, cols] * gain[:, cols]) * gated
            entry[rows, cols] = mixed_sum
            gated_all[rows, cols] = gated
            sig_all[rows, cols] = sig
            mixed_all[rows, cols] = mixed
        scale = lax.rsqrt(jnp.sum(square, axis=1, keepdims=True) * (1.0 / INNER) + EPS)
        pull = jnp.sum(cross, axis=1, keepdims=True) * (1.0 / INNER) * (scale * scale * scale)
        scale = jnp.broadcast_to(scale, (CHUNK, LANES))
        pull = jnp.broadcast_to(pull, (CHUNK, LANES))
        for cols in tiles(INNER):
            gated = gated_all[rows, cols]
            sig = sig_all[rows, cols]
            back = normed_grad[rows, cols]
            unit = gated * scale
            gated_low[rows, cols] = (unit * gain[:, cols]).astype(bf16)
            gated_grad = scale * (back * gain[:, cols]) - gated * pull
            act = gate[rows, cols] * sig
            slope = sig + act * (1.0 - sig)
            gate_grad[rows, cols] = (gated_grad * mixed_all[rows, cols].astype(f32) * slope).astype(bf16)
            low_grad = (gated_grad * act).astype(bf16)
            mixed_grad[rows, cols] = low_grad
            grad = low_grad.astype(f32)
            entry_low[rows, cols] = (grad * enter[rows, cols]).astype(bf16)
            products[0, rows, cols], products[1, rows, cols] = in_two(grad * entry[rows, cols])
            sums[0:8, cols] += eights(back * unit)
            sums[8:16, cols] += eights(grad * values[rows, cols].astype(f32))

    chunks(STRETCH, CHUNK, rows_step)
    summed = mm(products[...].reshape(2 * STRETCH, INNER), heads[...])
    row_sums[...] = summed[:STRETCH] + summed[STRETCH:]
    reads_grad[...] = mm(entry_low[...], full[...], NT)
    after_local[0] = state_grad[...].astype(bf16)
    after_decay[0] = tail_decay[...]
    state_grad[...] = state_grad[...] * factors[0, 0:1, :] + mm(reads, entry_low[...], TN)
    tail_decay[...] = tail_decay[...] * factors[0, 0:1, :]

    @pl.when(i == pl.num_programs(0) - 1)
    def _():
        for j, cols in enumerate(tiles(INNER)):
            start_grad[j] = state_grad[:, cols].astype(bf16)


def late(
    values, both, cumul, delta, raw, masks, bias, rate, factors, start, prior, after_local, after_decay, after,
    diag_sums, scaled, out_grad, row_sums, reads_grad, both_grad, skip, heads, spreader,
    conv_grad, sums,
    after_low, spread_grad, spreads, weighted, products,
):
    @pl.when(pl.program_id(0) == 0)
    def _():
        sums[...] = jnp.zeros_like(sums)

    carry_rows = []
    for j, cols in enumerate(tiles(INNER)):
        here = after_local[0, :, cols].astype(f32) + after_decay[0, 0:1, cols] * after[j].astype(f32)
        after_low[:, cols] = here.astype(bf16)
        carry_rows.append(eights(here * entered(start, factors, prior, j, cols)) * factors[0, 0:1, cols])
    top, low = in_two(jnp.concatenate(carry_rows, axis=1))
    products[4 * STRETCH :, :] = jnp.concatenate([top, low], axis=0)
    spread_grad[...] = mm(both[:, :STATE], after_low[...])
    step = delta[...]
    total = cumul[...]
    end_factor = jnp.exp(total[STRETCH - 1 : STRETCH, :] - total) * masks[:, 3:4]
    spreads[...] = spread_heads(jnp.concatenate([end_factor, step], axis=0), spreader[...])
    later = lambda rows, k: pl.ds(pl.multiple_of(rows.start + k * STRETCH, CHUNK), CHUNK)

    def rows_step(rows):
        for cols in tiles(INNER):
            v = values[rows, cols].astype(f32)
            ends = spreads[rows, cols]
            step_wide = spreads[later(rows, 1), cols]
            inner = diag_sums[rows, cols]
            outer = spread_grad[rows, cols] * ends
            both_sums = inner + outer
            conv_grad[rows, cols] = (
                step_wide * both_sums + skip[:, cols] * out_grad[rows, cols].astype(f32)
            ).astype(bf16)
            weighted[rows, cols] = (v * (ends * step_wide)).astype(bf16)
            products[rows, cols] = (v * both_sums).astype(bf16)
            products[later(rows, 1), cols] = (v * outer).astype(bf16)
            top, low = in_two(scaled[rows, cols].astype(f32) * inner)
            products[later(rows, 2), cols] = top
            products[later(rows, 3), cols] = low

    chunks(STRETCH, CHUNK, rows_step)
    conv_grad[:, INNER : INNER + STATE] = (
        both_grad[:, :STATE] + mm(weighted[...], after_low[...], NT)
    ).astype(bf16)
    conv_grad[:, INNER + STATE : CONV_CHANNELS] = (both_grad[:, STATE:] + reads_grad[...]).astype(bf16)
    summed = mm(products[...], heads[...])
    joint, outer_sum, top, low = [summed[k * STRETCH : (k + 1) * STRETCH] for k in range(4)]
    end_spread = outer_sum * step
    last_grad = jnp.sum(end_spread, axis=0, keepdims=True) + jnp.sum(summed[4 * STRETCH :], axis=0, keepdims=True)
    cumul_grad = row_sums[...] - (top + low) - end_spread
    decay_grad = sums_until(cumul_grad, True) + last_grad
    step_grad = joint + decay_grad * rate[...]
    pre_grad = step_grad * sigmoid(raw[...].astype(f32) + bias[...])
    conv_grad[:, CONV_CHANNELS:] = pre_grad.astype(bf16)
    sums[0:1, :] += jnp.sum(decay_grad * step, axis=0, keepdims=True)
    sums[1:2, :] += jnp.sum(pre_grad, axis=0, keepdims=True)


def conv_back(mixed, grad, masks, taps, out, rim, tail, tap_grads, held, same, kept):
    rows_all = grad.shape[0]
    spread_masks(masks, same)
    hold(mixed, held)
    kept[:, :, pl.ds(rows_all, 8), :] = jnp.zeros(kept.shape[:2] + (8, LANES), f32)

    def convolve(cols):
        tile = cols.start // LANES
        found = [jnp.zeros((8, LANES), f32) for _ in range(CONV_WIDTH + 1)]
        for rows in range(0, rows_all, PART):
            total, taken = conv_part(held, same, taps, rows, cols)
            sig = sigmoid(total)
            here = grad[rows : rows + PART, cols].astype(f32) * (sig * (1.0 + total * (1.0 - sig)))
            found[CONV_WIDTH] = found[CONV_WIDTH] + eights(here)
            for k in range(CONV_WIDTH):
                masked = here if k == 0 else here * same[k - 1, rows : rows + PART, :]
                kept[k, tile, pl.ds(rows, PART), :] = masked
                found[3 - k] = found[3 - k] + eights(masked * taken[k])
        lines = [jnp.sum(line, axis=0, keepdims=True) for line in found]
        tap_grads[:, cols] = jnp.concatenate(lines + [jnp.zeros((3, LANES), f32)], axis=0)
        for rows in range(0, rows_all, PART):
            value = taps[3:4, cols] * kept[0, tile, pl.ds(rows, PART), :]
            for k in range(1, CONV_WIDTH):
                value = value + taps[3 - k : 4 - k, cols] * kept[k, tile, pl.ds(rows + k, PART), :]
            out[rows : rows + PART, cols] = value.astype(bf16)
            if rows + PART == rows_all:
                tail[:, cols] = value[PART - HALO :, :]
        lines = [jnp.zeros((5, LANES), f32)]
        for m in (3, 2, 1):
            line = jnp.zeros((1, LANES), f32)
            for k in range(m, CONV_WIDTH):
                line = line + taps[3 - k : 4 - k, cols] * kept[k, tile, k - m : k - m + 1, :]
            lines.append(line)
        rim[:, cols] = jnp.concatenate(lines, axis=0)

    def other(cols):
        out[:, cols] = grad[:, cols]
        tail[:, cols] = grad[rows_all - HALO :, cols].astype(f32)
        rim[:, cols] = jnp.zeros((8, LANES), f32)
        tap_grads[:, cols] = jnp.zeros((8, LANES), f32)

    each_tile(convolve, other)


def per_device(
    block_input,
    out_cotangent,
    segment_ids,
    in_weight,
    out_weight,
    vector_params,
    in_first,
    in_second,
    out_first,
    out_second,
    vector_first,
    vector_second,
):
    count = lax.axis_size("seq") * lax.axis_size("head")
    device_index = lax.axis_index(EVERY)
    rows = block_input.shape[0]
    stretches = rows // STRETCH
    own_rows = in_weight.shape[0]
    halo = passed_along(block_input[rows - HALO :], EVERY, 1)

    head_index, seq_index = lax.axis_index("head"), lax.axis_index("seq")
    chips = lax.axis_size("seq") // 2
    mixer_own = jnp.pad(in_weight[:, INNER:].astype(bf16), ((0, 0), (0, LANES - HEADS)))
    mixer_group = laid(
        [(head_index, mixer_own)]
        + [(head_index ^ k, fetched(mixer_own, "head", k)) for k in range(1, lax.axis_size("head"))]
    )
    mixer_group, halo, block_now, segment_now, vector_now, none = lax.optimization_barrier(
        (mixer_group, halo, block_input, segment_ids, vector_params, jnp.zeros((), jnp.int32))
    )
    norm_gain, gated_gain, conv_taps, conv_bias, step_bias, log_rate, skip_gain = split_vector(vector_now)

    def unit_rows(block):
        wide = block.astype(f32)
        scale = lax.rsqrt(jnp.mean(wide * wide, axis=-1, keepdims=True) + EPS)
        return wide, scale

    inputs, in_scale = unit_rows(block_now)
    normed = (inputs * in_scale * norm_gain).astype(bf16)
    halo_wide, halo_scale = unit_rows(halo)
    extended = jnp.concatenate([normed, (halo_wide * halo_scale * norm_gain).astype(bf16)], axis=0)

    padded = jnp.concatenate(
        [jnp.full((3,), -1, jnp.int32), segment_now, jnp.full((3,), -1, jnp.int32)]
    )
    window = lax.dynamic_slice_in_dim(padded, device_index * rows, rows + 6)
    own = window[3 : 3 + rows]
    blocks = own.reshape(stretches, STRETCH)
    before = window[2 : 2 + rows].reshape(stretches, STRETCH)[:, :1]
    columns = [(window[3 - k : 3 - k + rows] == own) for k in (1, 2, 3)]
    columns.append((blocks == blocks[:, -1:]).reshape(rows))
    columns.append((blocks == before).reshape(rows))
    columns.append(own)
    marks = 8
    lane = lax.broadcasted_iota(jnp.int32, (rows, marks), 1)
    masks = jnp.zeros((rows, marks), f32)
    for k, column in enumerate(columns):
        masks = jnp.where(lane == k, column.astype(f32)[:, None], masks)
    segments = blocks.astype(f32).reshape(stretches, 1, STRETCH)

    taps = jnp.concatenate([conv_taps, conv_bias[None], jnp.zeros((3, CONV_CHANNELS), f32)], axis=0)
    taps = jnp.pad(taps, ((0, 0), (0, LANES)))

    def head_row(vector):
        return jnp.pad(vector, (0, LANES - HEADS)).reshape(1, LANES)

    bias_row = head_row(step_bias)
    rate_row = head_row(-jnp.exp(log_rate))
    skip_row = jnp.repeat(skip_gain, HEAD_SIZE).reshape(1, INNER)
    gain_row = gated_gain.reshape(1, INNER)
    head_of = (
        lax.broadcasted_iota(jnp.int32, (INNER, LANES), 0) // HEAD_SIZE
        == lax.broadcasted_iota(jnp.int32, (INNER, LANES), 1) + none
    ).astype(bf16)
    spreader = jnp.concatenate([head_of.T, head_of.T], axis=0)

    rest_own = jnp.concatenate([in_weight[:, :WIDTH], in_weight[:, WIDTH:INNER], out_weight], axis=0).astype(bf16)
    rest_own, _ = lax.optimization_barrier((rest_own, mixer_group))
    near = [(0, mixer_group)] + [(2 * k, fetched(mixer_group, "seq", 2 * k)) for k in range(1, chips)]
    near, extended, normed, masks, taps, spreader, head_of = lax.optimization_barrier(
        ([piece for _, piece in near], extended, normed, masks, taps, spreader, head_of)
    )
    bits = [2 * k for k in range(chips)] + [2 * k + 1 for k in range(chips)]
    pieces = near + [fetched(piece, "seq", 1) for piece in near]
    rest = lax.all_gather(rest_own, EVERY, axis=0, tiled=True).reshape(count, -1, WIDTH)
    gate_weight = jnp.concatenate(
        [rest[:, :own_rows].reshape(WIDTH, WIDTH), rest[:, own_rows : 2 * own_rows].reshape(WIDTH, WIDTH)], axis=1
    )
    out_full = rest[:, 2 * own_rows :].reshape(INNER, WIDTH)

    convolved, mixed_low, mixer_weight = call(
        functools.partial(conv_forward, bits),
        (MIXED // TILE,),
        [
            pl.BlockSpec(memory_space=pltpu.SMEM),
            whole(rows + HALO, WIDTH),
            whole(rows, marks),
            spec((8, TILE), lambda i: (0, i)),
        ]
        + [spec((pieces[0].shape[0], TILE), lambda i: (0, i))] * len(pieces),
        [
            spec((rows, TILE), lambda i: (0, i)),
            spec((rows + HALO, TILE), lambda i: (0, i)),
            spec((WIDTH, TILE), lambda i: (0, i)),
        ],
        [((rows, MIXED), bf16), ((rows + HALO, MIXED), bf16), ((WIDTH, MIXED), bf16)],
        [
            pltpu.VMEM((TILE // LANES, rows + HALO, LANES), f32),
            pltpu.VMEM((3, rows, LANES), f32),
            pltpu.VMEM((WIDTH, TILE), f32),
        ],
        14,
    )(seq_index.reshape(1), extended, masks, taps, *pieces)

    by_block = lambda *tail: spec((STRETCH,) + tail, lambda c: (c,) + (0,) * len(tail))
    both_spec = spec((STRETCH, 2 * STATE), lambda c: (c, INNER // (2 * STATE)))
    values_spec = spec((STRETCH, INNER), lambda c: (c, 0))
    raw_spec = spec((STRETCH, LANES), lambda c: (c, CONV_CHANNELS // LANES))
    per_block = lambda *tail: spec((1,) + tail, lambda c: (c,) + (0,) * len(tail))

    scaled, cumul, delta, cumul_rows, start, factors, device_state, device_decay = call(
        local_states,
        (stretches,),
        [values_spec, both_spec, raw_spec, by_block(marks), whole(1, LANES), whole(1, LANES), whole(2 * LANES, INNER)],
        [
            by_block(INNER),
            by_block(LANES),
            by_block(LANES),
            per_block(32, STRETCH),
            per_block(STATE, INNER),
            per_block(8, INNER),
            whole(PAIRS, STATE, LANES),
            whole(16, LANES),
        ],
        [
            ((rows, INNER), bf16),
            ((rows, LANES), f32),
            ((rows, LANES), f32),
            ((stretches, 32, STRETCH), f32),
            ((stretches, STATE, INNER), bf16),
            ((stretches, 8, INNER), f32),
            ((PAIRS, STATE, LANES), bf16),
            ((16, LANES), bf16),
        ],
        [
            pltpu.VMEM((STATE, INNER), f32),
            pltpu.VMEM((8, LANES), f32),
            pltpu.VMEM((STRETCH, INNER), bf16),
            pltpu.VMEM((2 * STRETCH + 16, INNER), f32),
        ],
        9,
    )(convolved, convolved, convolved, masks, bias_row, rate_row, spreader)

    share = PAIRS * STATE // count
    decay_rows = jnp.broadcast_to(device_decay[None, :2], (count, 2, LANES))
    sent = jnp.concatenate([device_state.reshape(count, share, LANES), decay_rows], axis=1)

    def exchange(value):
        return lax.all_to_all(value, EVERY, split_axis=0, concat_axis=0, tiled=True)

    def scan_parts(parts, reverse):
        return pl.pallas_call(
            functools.partial(prefix, reverse=reverse),
            in_specs=[pl.BlockSpec(memory_space=pltpu.SMEM)] + [pl.BlockSpec(memory_space=pltpu.VMEM)] * 2,
            out_shape=jax.ShapeDtypeStruct((count, share, LANES), bf16),
            scratch_shapes=[pltpu.VMEM((count, 2 * LANES), f32)],
            compiler_params=pltpu.CompilerParams(vmem_limit_bytes=ROOM),
        )(device_index.reshape(1), parts, all_decays)

    arrived = exchange(sent)
    all_decays = arrived[:, share].astype(f32) + arrived[:, share + 1].astype(f32)
    prior = exchange(scan_parts(arrived, False)).reshape(PAIRS, STATE, LANES)

    diag = call(
        diagonal,
        (stretches,),
        [
            by_block(INNER),
            both_spec,
            by_block(LANES),
            per_block(32, STRETCH),
            by_block(marks),
            per_block(1, STRETCH),
        ],
        [by_block(INNER)],
        [((rows, INNER), f32)],
        [pltpu.VMEM((HEADS, STRETCH, LANES), f32), pltpu.VMEM((STRETCH, STRETCH), f32)],
        16,
    )(scaled, convolved, cumul, cumul_rows, masks, segments)[0]
    gate = jnp.dot(normed, gate_weight, preferred_element_type=f32)
    normed_grad = mm(out_cotangent, out_full, NT)

    back = stretches - 1
    by_block_r = lambda *tail: spec((STRETCH,) + tail, lambda c: (back - c,) + (0,) * len(tail))
    per_block_r = lambda *tail: spec((1,) + tail, lambda c: (back - c,) + (0,) * len(tail))
    wide_scratch = lambda kind: pltpu.VMEM((STRETCH, INNER), kind)
    (
        gated_low,
        gate_grad,
        mixed_grad,
        row_sums,
        reads_grad,
        after_local,
        middle_sums,
        start_grad,
        after_decay,
    ) = call(
        middle,
        (stretches,),
        [
            by_block_r(INNER),
            spec((STRETCH, INNER), lambda c: (back - c, 0)),
            spec((STRETCH, 2 * STATE), lambda c: (back - c, INNER // (2 * STATE))),
            by_block_r(LANES),
            by_block_r(marks),
            per_block_r(STATE, INNER),
            per_block_r(8, INNER),
            whole(PAIRS, STATE, LANES),
            by_block_r(INNER),
            by_block_r(INNER),
            whole(1, INNER),
            whole(1, INNER),
            whole(INNER, LANES),
            whole(2 * LANES, INNER),
        ],
        [
            by_block_r(INNER),
            by_block_r(INNER),
            by_block_r(INNER),
            by_block_r(LANES),
            by_block_r(STATE),
            per_block_r(STATE, INNER),
            whole(16, INNER),
            whole(PAIRS, STATE, LANES),
            per_block_r(8, INNER),
        ],
        [
            ((rows, INNER), bf16),
            ((rows, INNER), bf16),
            ((rows, INNER), bf16),
            ((rows, LANES), f32),
            ((rows, STATE), f32),
            ((stretches, STATE, INNER), bf16),
            ((16, INNER), f32),
            ((PAIRS, STATE, LANES), bf16),
            ((stretches, 8, INNER), f32),
        ],
        [
            pltpu.VMEM((STATE, INNER), bf16),
            wide_scratch(f32),
            wide_scratch(f32),
            wide_scratch(f32),
            wide_scratch(f32),
            wide_scratch(bf16),
            wide_scratch(bf16),
            pltpu.VMEM((2, STRETCH, INNER), bf16),
            pltpu.VMEM((STATE, INNER), f32),
            pltpu.VMEM((8, INNER), f32),
        ],
        24,
    )(
        diag, convolved, convolved, cumul, masks, start, factors, prior, gate, normed_grad,
        gain_row, skip_row, head_of, spreader,
    )

    sent_back = exchange(start_grad.reshape(count, share, LANES))
    gate_term = mm(normed, gate_grad, TN).astype(bf16)
    out_term = mm(gated_low, out_cotangent, TN).astype(bf16)
    rest_term = jnp.concatenate(
        [
            gate_term[:, :WIDTH].reshape(count, -1, WIDTH),
            gate_term[:, WIDTH:].reshape(count, -1, WIDTH),
            out_term.reshape(count, -1, WIDTH),
        ],
        axis=1,
    ).reshape(-1, WIDTH)
    block_output = (inputs + mm(gated_low, out_full)).astype(bf16)
    sent_back, rest_term, block_output = lax.optimization_barrier((sent_back, rest_term, block_output))
    rest_line = lax.psum_scatter(rest_term, "seq", scatter_dimension=0, tiled=True)
    scanned = scan_parts(sent_back, True)
    scanned, mixed_grad = lax.optimization_barrier((scanned, mixed_grad))
    after = exchange(scanned)
    diag_sums, both_grad = call(
        diagonal_back,
        (stretches,),
        [
            by_block(INNER),
            both_spec,
            by_block(LANES),
            per_block(32, STRETCH),
            by_block(marks),
            per_block(1, STRETCH),
            by_block(INNER),
        ],
        [by_block(INNER), by_block(2 * STATE)],
        [((rows, INNER), f32), ((rows, 2 * STATE), f32)],
        [
            pltpu.VMEM((HEADS, STRETCH, LANES), f32),
            pltpu.VMEM((STRETCH, STRETCH), f32),
            pltpu.VMEM((STRETCH, STRETCH), f32),
        ],
        20,
    )(scaled, convolved, cumul, cumul_rows, masks, segments, mixed_grad)
    after, diag_sums, both_grad = lax.optimization_barrier((after, diag_sums, both_grad))
    after = after.reshape(PAIRS, STATE, LANES)

    conv_out_grad, late_sums = call(
        late,
        (stretches,),
        [
            values_spec,
            both_spec,
            by_block(LANES),
            by_block(LANES),
            raw_spec,
            by_block(marks),
            whole(1, LANES),
            whole(1, LANES),
            per_block(8, INNER),
            per_block(STATE, INNER),
            whole(PAIRS, STATE, LANES),
            per_block(STATE, INNER),
            per_block(8, INNER),
            whole(PAIRS, STATE, LANES),
            by_block(INNER),
            by_block(INNER),
            by_block(INNER),
            by_block(LANES),
            by_block(STATE),
            by_block(2 * STATE),
            whole(1, INNER),
            whole(INNER, LANES),
            whole(2 * LANES, INNER),
        ],
        [by_block(MIXED), whole(8, LANES)],
        [((rows, MIXED), bf16), ((8, LANES), f32)],
        [
            pltpu.VMEM((STATE, INNER), bf16),
            wide_scratch(f32),
            pltpu.VMEM((2 * STRETCH, INNER), f32),
            wide_scratch(bf16),
            pltpu.VMEM((4 * STRETCH + 16, INNER), bf16),
        ],
        18,
    )(
        convolved, convolved, cumul, delta, convolved, masks, bias_row, rate_row, factors, start, prior, after_local, after_decay,
        after, diag_sums, scaled, mixed_grad, row_sums, reads_grad, both_grad, skip_row, head_of, spreader,
    )

    mixed_in_grad, rim, tail, tap_grads = call(
        conv_back,
        (MIXED // TILE,),
        [
            spec((rows + HALO, TILE), lambda i: (0, i)),
            spec((rows, TILE), lambda i: (0, i)),
            whole(rows, marks),
            spec((8, TILE), lambda i: (0, i)),
        ],
        [
            spec((rows, TILE), lambda i: (0, i)),
            spec((8, TILE), lambda i: (0, i)),
            spec((HALO, TILE), lambda i: (0, i)),
            spec((8, TILE), lambda i: (0, i)),
        ],
        [
            ((rows, MIXED), bf16),
            ((8, MIXED), f32),
            ((HALO, MIXED), f32),
            ((8, MIXED), f32),
        ],
        [
            pltpu.VMEM((TILE // LANES, rows + HALO, LANES), f32),
            pltpu.VMEM((3, rows, LANES), f32),
            pltpu.VMEM((CONV_WIDTH, TILE // LANES, rows + 8, LANES), f32),
        ],
        20,
    )(mixed_low, conv_out_grad, masks, taps)

    rim, rest_line = lax.optimization_barrier((rim, rest_line))
    rest_grad = lax.psum_scatter(rest_line, "head", scatter_dimension=0, tiled=True)
    rest_grad = lax.optimization_barrier(rest_grad).astype(f32)
    gate_weight_grad = jnp.concatenate([rest_grad[:own_rows], rest_grad[own_rows : 2 * own_rows]], axis=1)
    out_grad = rest_grad[2 * own_rows :]
    from_next = passed_along(rim, EVERY, -1)
    gate_grad, rim = lax.optimization_barrier((gate_grad, rim))
    gate_part = mm(gate_grad, gate_weight, NT)
    from_next, gate_part = lax.optimization_barrier((from_next, gate_part))
    fixed = jnp.concatenate([tail[: HALO - 8], tail[HALO - 8 :] + from_next], axis=0).astype(bf16)
    mixer_grad = lax.dynamic_update_slice(mixed_in_grad, fixed, (rows - HALO, 0))
    term = mm(normed, mixer_grad, TN).astype(bf16)
    line_rows = own_rows * lax.axis_size("head")

    def block_of(value, place, size):
        return lax.dynamic_slice_in_dim(value, place * size, size, axis=0)

    summed = []
    for k in range(chips):
        given = block_of(term, seq_index ^ (2 * k) ^ 1, line_rows)
        kept = block_of(term, seq_index ^ (2 * k), line_rows)
        summed.append(kept.astype(f32) + fetched(given, "seq", 1).astype(f32))
    sending = [part.astype(bf16) for part in summed[1:]]
    early = jnp.concatenate(
        [
            jnp.sum(middle_sums[:8], axis=0),
            tap_grads[: CONV_WIDTH + 1, :CONV_CHANNELS].reshape(-1),
            late_sums[1, :HEADS],
            late_sums[0, :HEADS] * rate_row[0, :HEADS],
            jnp.sum(middle_sums[8:].reshape(8, HEADS, HEAD_SIZE), axis=(0, 2)),
        ]
    )
    size = early.shape[0]
    early = jnp.pad(early, (0, -size % count)).reshape(count, -1)
    sending, mixer_grad, early = lax.optimization_barrier((sending, mixer_grad, early))
    line = summed[0]
    for k, part in enumerate(sending, 1):
        line = line + fetched(part, "seq", 2 * k).astype(f32)
    normed_in_grad = gate_part + mm(mixer_grad, mixer_weight, NT)
    norm_gain_grad = jnp.sum(normed_in_grad * inputs * in_scale, axis=0)
    scaled_in = normed_in_grad * norm_gain
    input_grad = (
        out_cotangent.astype(f32)
        + in_scale * scaled_in
        - inputs * in_scale**3 * jnp.mean(scaled_in * inputs, axis=-1, keepdims=True)
    )

    early_parts = exchange(early)
    out_new = adamw(out_weight, out_first, out_second, out_grad, RATE_MATRIX, WEIGHT_DECAY)
    line, norm_gain_grad, early_parts, out_new = lax.optimization_barrier((line, norm_gain_grad, early_parts, out_new))
    own_early = jnp.sum(early_parts, axis=0)
    both_vectors = jnp.concatenate([own_early, norm_gain_grad])
    both_vectors = exchange(jnp.broadcast_to(both_vectors[None], (count,) + both_vectors.shape))
    mixer_weight_grad = block_of(line, head_index, own_rows)
    for k in range(1, lax.axis_size("head")):
        given = block_of(line, head_index ^ k, own_rows).astype(bf16)
        mixer_weight_grad = mixer_weight_grad + fetched(given, "head", k).astype(f32)
    in_grad = jnp.concatenate([gate_weight_grad, mixer_weight_grad[:, : CONV_CHANNELS + HEADS]], axis=1)
    in_new = adamw(in_weight, in_first, in_second, in_grad, RATE_MATRIX, WEIGHT_DECAY)
    both_vectors, in_new = lax.optimization_barrier((both_vectors, in_new))
    vector_grad = jnp.concatenate(
        [
            jnp.sum(both_vectors[:, own_early.shape[0] :], axis=0),
            both_vectors[:, : own_early.shape[0]].reshape(-1)[:size],
        ]
    )
    vector_first_new, vector_second_new, vector_new = adamw(
        vector_params, vector_first, vector_second, vector_grad, RATE_VECTOR, 0.0
    )
    return (
        block_output,
        input_grad.astype(bf16),
        *in_new,
        *out_new,
        vector_first_new,
        vector_second_new,
        vector_new,
    )


def solution(mesh):
    split = P(EVERY, None)
    in_specs = (split, split, P(), split, split, P(), split, split, split, split, P(), P())
    out_specs = (split,) * 8 + (P(),) * 3
    return jax.shard_map(
        per_device, mesh=mesh, in_specs=in_specs, out_specs=out_specs, check_vma=False
    )
```
